32 devices in a mesh: ctx: 16 (over z, y, x), tp: 2 (over core).
Axes of the slice: x: 2, y: 2, z: 4, core: 2. Of those that a mesh axis runs over, the one named last changes fastest.
Arguments:
- tokens: bfloat16 [2048, 4096], P('ctx', 'tp'), may hold values from -216 to 216
- norm_gain: float32 [4096], P('tp'), may hold values from 0.5 to 1.5
- norm_bias: float32 [4096], P('tp'), may hold values from -3 to 3
- ema_decay: float32 [16, 4096], P(None, 'tp'), may hold values from 0.96 to 1
- ema_phase: float32 [16, 4096], P(None, 'tp'), may hold values from -1 to 1
- ema_in: float32 [16, 4096], P(None, 'tp'), may hold values from -0.6 to 0.6
- ema_out: float32 [2, 16, 4096], P(None, None, 'tp'), may hold values from -1.5 to 1.5
- ema_skip: float32 [4096], P('tp'), may hold values from -4 to 4
- rms_gain: float32 [4096], replicated, may hold values from 0.5 to 1.5
- z_weight: bfloat16 [4096, 256], P('ctx', 'tp'), may hold values from -0.09375 to 0.09375
- v_weight: bfloat16 [4096, 2048], P('ctx', 'tp'), may hold values from -0.09375 to 0.09375
- qk_affine: float32 [4, 256], P(None, 'tp'), may hold values from -1.5 to 4, as said below
Outputs:
- attended: bfloat16 [2048, 2048], P('ctx', 'tp')
The draws below stay inside these ranges and needn't reach their ends.
Inputs may be any that keep to these rules, and one draw needn't show every extreme that they name: `qk_affine`: rows 0 and 2 are positive.
All inputs are finite; a program needn't handle non-finite values.
Results may differ from the reference program's by a relative error of at most 0.015.
The reference program's roundings to bfloat16 on the way (of `normed`, `mixed_rows`, `rms_normed` and `probabilities`) count: a program that leaves them out, or rounds other values in their place, can miss the bound.
Values may be sent and summed in bfloat16 or wider, within the bound.
No kernel may reach another device: no remote copies, remote signals or barrier semaphores. Data moves between devices by JAX's collectives and lax.ppermute only.
A program may use at most 128 MiB of HBM per device.

```python
import math
import jax
import jax.numpy as jnp
from jax import lax

D = 4096
NDIM = 16
ZH = 128
VH = 1024
GROUP = 64
STRETCH = 128
EBLK = 32
TOKENS = 2048
ZDIM = 256
VDIM = 2048


def draw_tokens(key, part):
    keys = jax.random.split(key, 4)
    block_count = TOKENS // EBLK
    base = jax.random.truncated_normal(keys[0], -6.0, 6.0, (TOKENS, D), jnp.float32)
    shifts = jnp.repeat(jax.random.uniform(keys[1], (block_count, D), jnp.float32, -1.0, 1.0), EBLK, axis=0)
    row_scale = jnp.repeat(jnp.exp(jax.random.uniform(keys[2], (block_count, 1), jnp.float32, 0.0, math.log(3.2))), EBLK, axis=0)
    column_scale = jnp.exp(jax.random.uniform(keys[3], (1, D), jnp.float32, 0.0, math.log(3.2)))
    ramp = jnp.exp(math.log(3.0) * jnp.arange(TOKENS, dtype=jnp.float32) / TOKENS)[:, None]
    return ((base + shifts) * row_scale * column_scale * ramp).astype(jnp.bfloat16)


def draw_ema_decay(key, part):
    keys = jax.random.split(key, 3)
    slow_share = 0.5
    slower = jax.random.bernoulli(keys[0], slow_share, (NDIM, D))
    fast_rate = jnp.exp(jax.random.uniform(keys[1], (NDIM, D), jnp.float32, math.log(1.0 / 50.0), math.log(1.0 / 30.0)))
    slow_rate = jax.random.uniform(keys[2], (NDIM, D), jnp.float32, 0.1, 2.0) / TOKENS
    return jnp.exp(-jnp.where(slower, slow_rate, fast_rate)).astype(jnp.float32)


def draw_qk_affine(key, part):
    keys = jax.random.split(key, 4)
    gain_low, gain_high = (math.log(0.5), math.log(2.0))
    query_gain = jnp.exp(jax.random.uniform(keys[0], (ZDIM,), jnp.float32, gain_low, gain_high))
    key_gain = jnp.exp(jax.random.uniform(keys[1], (ZDIM,), jnp.float32, gain_low, gain_high))
    query_bias = 0.3 * jax.random.truncated_normal(keys[2], -5.0, 5.0, (ZDIM,), jnp.float32)
    key_bias = 0.3 * jax.random.truncated_normal(keys[3], -5.0, 5.0, (ZDIM,), jnp.float32)
    return jnp.stack([query_gain, query_bias, key_gain, key_bias]).astype(jnp.float32)


def steps_of(own_key, shape, cuts, low, top_value):
    def one(axis_at, shards_of):
        draws = jax.random.uniform(jax.random.fold_in(jax.random.fold_in(own_key, 6), axis_at), (shards_of,), jnp.float32, low / len(cuts), top_value / len(cuts))
        return jnp.repeat(jnp.exp(draws), shape[axis_at] // shards_of).reshape((-1,) + (1,) * (len(shape) - axis_at - 1))

    factor_of = one(*cuts[0])
    for cut in cuts[1:]:
        factor_of = factor_of * one(*cut)
    return factor_of


def normal_values(own_key, shape, deviation, limit, pieces=(), kind=jnp.bfloat16):
    level = steps_of(own_key, shape, pieces, -0.22, 0.18) if pieces else 1.0
    values = jax.random.normal(own_key, shape, jnp.float32) * deviation * level
    return jnp.minimum(jnp.maximum(values, -limit), limit).astype(kind)


def setup_inputs(seed: int = 0) -> dict:
    key_list = jax.random.split(jax.random.key(seed), 13)
    return {
        "tokens": draw_tokens(jax.random.fold_in(key_list[12], 71), 0),
        "norm_gain": jnp.clip(1.0 + 0.1 * jax.random.normal(key_list[1], (D,), jnp.float32), 0.5, 1.5),
        "norm_bias": normal_values(key_list[2], (D,), 0.5, 3.0, ((0, 2),), jnp.float32),
        "ema_decay": draw_ema_decay(jax.random.fold_in(key_list[12], 71), 0),
        "ema_phase": jnp.clip(jax.random.uniform(key_list[4], (NDIM, D), jnp.float32, -1.0, 1.0) * steps_of(key_list[4], (NDIM, D), ((1, 2),), -0.4, 0.0), -1.0, 1.0),
        "ema_in": normal_values(key_list[5], (NDIM, D), 0.1, 0.6, ((1, 2),), jnp.float32),
        "ema_out": normal_values(key_list[6], (2, NDIM, D), NDIM ** -0.5, 1.5, ((2, 2),), jnp.float32),
        "ema_skip": normal_values(key_list[7], (D,), 1.0, 4.0, ((0, 2),), jnp.float32),
        "rms_gain": jnp.clip(1.0 + 0.1 * jax.random.normal(key_list[8], (D,), jnp.float32), 0.5, 1.5),
        "z_weight": normal_values(key_list[9], (D, ZDIM), D ** -0.5, 0.09375, ((0, 16), (1, 2))),
        "v_weight": normal_values(key_list[10], (D, VDIM), D ** -0.5, 0.09375, ((0, 16), (1, 2))),
        "qk_affine": draw_qk_affine(jax.random.fold_in(key_list[12], 71), 0),
    }


highest = lax.Precision.HIGHEST
epsilon = 1e-05

def ema_tables(decays, phases, ema_in, ema_out, blocklen):
    log_rate = jnp.log(decays)
    powers = jnp.arange(blocklen + 1, dtype=jnp.float32)[:, None, None]
    magnitude = jnp.exp(powers * log_rate)
    power_re = magnitude * jnp.cos(powers * phases)
    power_im = magnitude * jnp.sin(powers * phases)
    coef_re = ema_out[0] * power_re - ema_out[1] * power_im
    coef_im = ema_out[0] * power_im + ema_out[1] * power_re
    kernel = lax.optimization_barrier(jnp.sum(ema_in * coef_re[:blocklen], axis=1))
    offsets = jnp.arange(blocklen)[:, None] - jnp.arange(blocklen)[None, :]
    toeplitz = jnp.where((offsets >= 0)[:, :, None], kernel[jnp.clip(offsets, 0, blocklen - 1)], 0.0)
    feed_re = ema_in * power_re[::-1][1:]
    feed_im = ema_in * power_im[::-1][1:]
    return (toeplitz, coef_re[1:], coef_im[1:], feed_re, feed_im, power_re[blocklen], power_im[blocklen])

def ema_feed(tables, inputs):
    fresh_re = jnp.einsum('sc,sjc->jc', inputs, tables[3], precision=highest)
    fresh_im = jnp.einsum('sc,sjc->jc', inputs, tables[4], precision=highest)
    return (fresh_re, fresh_im)

def rotate(tables, hidden_state, inputs):
    state_re, state_im = hidden_state
    fresh_re, fresh_im = ema_feed(tables, inputs)
    new_re = tables[5] * state_re - tables[6] * state_im + fresh_re
    new_im = tables[5] * state_im + tables[6] * state_re + fresh_im
    return (new_re, new_im)

def ema_block(tables, hidden_state, inputs):
    state_re, state_im = hidden_state
    within = jnp.einsum('tsc,sc->tc', tables[0], inputs, precision=highest)
    carried = jnp.einsum('tjc,jc->tc', tables[1], state_re, precision=highest) - jnp.einsum('tjc,jc->tc', tables[2], state_im, precision=highest)
    return (rotate(tables, hidden_state, inputs), within + carried)

def attention(z_total, v_total, affine):
    queries = (z_total * affine[0] + affine[1]).astype(jnp.bfloat16)
    key_rows = (z_total * affine[2] + affine[3]).astype(jnp.bfloat16)
    values = jax.nn.silu(v_total).astype(jnp.bfloat16)
    row_count = z_total.shape[0]
    stretches = row_count // STRETCH
    queries = queries.reshape(stretches, STRETCH, -1).astype(jnp.float32)
    key_rows = key_rows.reshape(stretches, STRETCH, -1).astype(jnp.float32)
    values = values.reshape(stretches, STRETCH, -1).astype(jnp.float32)
    scores = jnp.einsum('nqd,nkd->nqk', queries, key_rows) * (1.0 / ZH ** 0.5)
    causal = jnp.arange(STRETCH)[:, None] >= jnp.arange(STRETCH)[None, :]
    scores = jnp.where(causal[None], scores, -1e+30)
    row_max = lax.optimization_barrier(jnp.max(scores, axis=-1, keepdims=True))
    weights = jnp.exp(scores - row_max)
    probabilities = (weights / lax.optimization_barrier(jnp.sum(weights, axis=-1, keepdims=True))).astype(jnp.bfloat16)
    result = jnp.einsum('nqk,nkd->nqd', probabilities.astype(jnp.float32), values)
    return result.reshape(row_count, -1).astype(jnp.bfloat16)

def reference(tokens, norm_gain, norm_bias, ema_decay, ema_phase, ema_in, ema_out, ema_skip, rms_gain, z_weight, v_weight, qk_affine):
    length = tokens.shape[0]
    model_width = tokens.shape[1]
    groups = model_width // GROUP
    x_float = tokens.astype(jnp.float32).reshape(length, groups, GROUP)
    prefix_sums = jnp.cumsum(lax.optimization_barrier(jnp.sum(x_float, axis=-1)), axis=0)
    prefix_squares = jnp.cumsum(lax.optimization_barrier(jnp.sum(x_float * x_float, axis=-1)), axis=0)
    counts = (jnp.arange(length, dtype=jnp.float32)[:, None] + 1.0) * GROUP
    average = prefix_sums / counts
    spread = jnp.maximum(prefix_squares / counts - average * average, 0.0)
    scaled = (x_float - average[..., None]) * lax.rsqrt(spread + epsilon)[..., None]
    normed = (scaled.reshape(length, model_width) * norm_gain + norm_bias).astype(jnp.bfloat16)
    inputs = normed.astype(jnp.float32)
    tables = ema_tables(ema_decay, ema_phase, ema_in, ema_out, EBLK)

    def advance(hidden_state, block_rows):
        return ema_block(tables, hidden_state, block_rows)
    initial = (jnp.zeros((NDIM, model_width), jnp.float32), jnp.zeros((NDIM, model_width), jnp.float32))
    _, outputs = lax.scan(advance, initial, inputs.reshape(length // EBLK, EBLK, model_width))
    mixed_rows = jax.nn.silu(outputs.reshape(length, model_width) + ema_skip * inputs).astype(jnp.bfloat16)
    mixed_float = mixed_rows.astype(jnp.float32)
    rms_normed = (mixed_float * lax.rsqrt(lax.optimization_barrier(jnp.mean(mixed_float * mixed_float, axis=-1, keepdims=True)) + 1e-06) * rms_gain).astype(jnp.bfloat16)
    head_count = z_weight.shape[1] // ZH

    def one_head(head_index):
        z_columns = lax.dynamic_slice_in_dim(z_weight, head_index * ZH, ZH, 1)
        v_columns = lax.dynamic_slice_in_dim(v_weight, head_index * VH, VH, 1)
        affine = lax.dynamic_slice_in_dim(qk_affine, head_index * ZH, ZH, 1)
        z_total = jnp.dot(rms_normed, z_columns, preferred_element_type=jnp.float32)
        v_total = jnp.dot(normed, v_columns, preferred_element_type=jnp.float32)
        return attention(z_total, v_total, affine)
    stacked = lax.map(one_head, jnp.arange(head_count))
    return stacked.transpose(1, 0, 2).reshape(length, head_count * VH)
```

```python
import functools

import jax
import jax.numpy as jnp
from jax import lax
from jax.experimental import pallas as pl
from jax.experimental.pallas import tpu as pltpu
from jax.sharding import PartitionSpec as P

NDIM = 16
GROUP = 64
STRETCH = 128
CHUNK = 16
LANES = 128
epsilon = 1e-05
f32 = jnp.float32
bf16 = jnp.bfloat16
VMEM_LIMIT = 48 * 1024 * 1024


def call(kernel, outs, scratch=(), smem_first=False, n_in=1):
    specs = [pl.BlockSpec(memory_space=pltpu.VMEM) for _ in range(n_in)]
    if smem_first:
        specs[0] = pl.BlockSpec(memory_space=pltpu.SMEM)
    return pl.pallas_call(
        kernel,
        out_shape=outs,
        in_specs=specs,
        out_specs=jax.tree.map(lambda _: pl.BlockSpec(memory_space=pltpu.VMEM), outs),
        scratch_shapes=list(scratch),
        compiler_params=pltpu.CompilerParams(vmem_limit_bytes=VMEM_LIMIT),
    )


def pieces(value):
    first = value.astype(bf16)
    rest = value - first.astype(f32)
    second = rest.astype(bf16)
    third = (rest - second.astype(f32)).astype(bf16)
    return first, second, third


def mm(a, b):
    return jnp.dot(a, b, preferred_element_type=f32)


def membership(channels, width, transposed):
    shape = (width, channels) if transposed else (channels, width)
    channel = lax.broadcasted_iota(jnp.int32, shape, 1 if transposed else 0)
    group = lax.broadcasted_iota(jnp.int32, shape, 0 if transposed else 1)
    return jnp.where(channel // GROUP == group, 1.0, 0.0).astype(bf16)


def sums_kernel(x_ref, csum_ref, csq_ref, total_ref):
    length, channels = x_ref.shape
    width = csum_ref.shape[1]
    member = membership(channels, width, False)
    x = x_ref[...]
    square = x.astype(f32) * x.astype(f32)
    high = square.astype(bf16)
    low = (square - high.astype(f32)).astype(bf16)
    row_sums = mm(x, member)
    row_squares = mm(high, member) + mm(low, member)
    rows = lax.broadcasted_iota(jnp.int32, (length, length), 0)
    cols = lax.broadcasted_iota(jnp.int32, (length, length), 1)
    lower = jnp.where(rows >= cols, 1.0, 0.0).astype(bf16)
    for ref, value, at in ((csum_ref, row_sums, 0), (csq_ref, row_squares, 1)):
        one, two, three = pieces(value)
        running = mm(lower, one) + mm(lower, two) + mm(lower, three)
        ref[...] = running
        total_ref[at : at + 1, :] = running[length - 1 : length, :]


def powers_into(ref, q_ref, first_re, first_im, count):
    def one(j, _):
        q_re, q_im = q_ref[j, 0], q_ref[j, 1]
        now_re, now_im = first_re(j), first_im(j)
        for k in range(count):
            ref[k, j, 0] = now_re
            ref[k, j, 1] = now_im
            if k + 1 < count:
                now_re, now_im = now_re * q_re - now_im * q_im, now_re * q_im + now_im * q_re
        return _

    lax.fori_loop(0, NDIM, one, 0)


def feed_kernel(
    me_ref, x_ref, sums_ref, csum_ref, csq_ref, gain_ref, bias_ref, q_ref,
    normed_ref, dense_ref, fresh_ref, end_ref, power_ref,
):
    length, channels = x_ref.shape
    width = csum_ref.shape[1]
    tiles = channels // LANES
    chunks = length // CHUNK
    me = me_ref[0]
    peers = sums_ref.shape[0]
    before = [jnp.zeros((1, width), f32) for _ in range(2)]
    for peer in range(peers):
        earlier = jnp.where(peer < me, 1.0, 0.0)
        for at in range(2):
            before[at] = before[at] + sums_ref[peer, at : at + 1, :] * earlier
    place = lax.broadcasted_iota(jnp.int32, (length, width), 0) + me * length + 1
    counts = place.astype(f32) * GROUP
    average = (before[0] + csum_ref[...]) / counts
    spread = jnp.maximum((before[1] + csq_ref[...]) / counts - average * average, 0.0)
    scale = lax.rsqrt(spread + epsilon)
    member = membership(channels, width, True)
    average_pieces, scale_pieces = pieces(average), pieces(scale)
    for tile in range(tiles):
        lanes = slice(tile * LANES, (tile + 1) * LANES)
        mine = member[:, lanes]
        average_wide = sum(mm(p, mine) for p in average_pieces)
        scale_wide = sum(mm(p, mine) for p in scale_pieces)
        scaled = (x_ref[:, lanes].astype(f32) - average_wide) * scale_wide
        normed = (scaled * gain_ref[:, lanes] + bias_ref[:, lanes]).astype(bf16)
        normed_ref[:, lanes] = normed
        dense_ref[pl.ds(tile, length, stride=tiles), :] = normed.astype(f32)

    sub = q_ref.shape[2]
    powers_into(
        power_ref, q_ref, lambda j: jnp.ones((sub, LANES), f32), lambda j: jnp.zeros((sub, LANES), f32), CHUNK + 1
    )
    step = min(8, tiles)

    def one(j, _):
        for low in range(0, tiles, step):
            rows = slice(low, low + step)
            re = [jnp.zeros((step, LANES), f32) for _ in range(chunks)]
            im = [jnp.zeros((step, LANES), f32) for _ in range(chunks)]
            for b in range(CHUNK):
                p_re = power_ref[CHUNK - 1 - b, j, 0, rows, :]
                p_im = power_ref[CHUNK - 1 - b, j, 1, rows, :]
                for a in range(chunks):
                    at = (a * CHUNK + b) * tiles + low
                    value = dense_ref[at : at + step, :]
                    re[a] = re[a] + p_re * value
                    im[a] = im[a] + p_im * value
            q_re = power_ref[CHUNK, j, 0, rows, :]
            q_im = power_ref[CHUNK, j, 1, rows, :]
            s_re, s_im = re[0], im[0]
            for a in range(chunks):
                fresh_ref[a, j, 0, rows, :] = re[a]
                fresh_ref[a, j, 1, rows, :] = im[a]
                if a:
                    s_re, s_im = (
                        s_re * q_re - s_im * q_im + re[a],
                        s_re * q_im + s_im * q_re + im[a],
                    )
            end_ref[j, 0, rows, :] = s_re
            end_ref[j, 1, rows, :] = s_im
        return _

    lax.fori_loop(0, NDIM, one, 0)


def times(a, b):
    return a[0] * b[0] - a[1] * b[1], a[0] * b[1] + a[1] * b[0]


def scan_kernel(length, ends_ref, q_ref, out_ref):
    peers = ends_ref.shape[0]
    result, base, left = None, (q_ref[:, 0], q_ref[:, 1]), length
    while left:
        if left & 1:
            result = base if result is None else times(result, base)
        left >>= 1
        if left:
            base = times(base, base)
    state = (jnp.zeros_like(base[0]), jnp.zeros_like(base[1]))
    for peer in range(peers):
        out_ref[peer, :, 0] = state[0]
        out_ref[peer, :, 1] = state[1]
        if peer + 1 < peers:
            moved = times(state, result)
            state = (moved[0] + ends_ref[peer, :, 0], moved[1] + ends_ref[peer, :, 1])


def mix_kernel(
    incoming_ref, fresh_ref, dense_ref, q_ref, w_ref, skip_ref,
    mixed_ref, start_ref, coef_ref, tap_ref, out_ref,
):
    length, channels = mixed_ref.shape
    tiles = channels // LANES
    chunks = length // CHUNK
    step = min(8, tiles)

    def first_re(j):
        return w_ref[j, 0] * q_ref[j, 0] - w_ref[j, 1] * q_ref[j, 1]

    def first_im(j):
        return w_ref[j, 0] * q_ref[j, 1] + w_ref[j, 1] * q_ref[j, 0]

    powers_into(coef_ref, q_ref, first_re, first_im, CHUNK)
    tap = skip_ref[...]
    for j in range(NDIM):
        tap = tap + w_ref[j, 0]
    tap_ref[0] = tap

    def one_tap(k, _):
        tap = coef_ref[k, 0, 0]
        for j in range(1, NDIM):
            tap = tap + coef_ref[k, j, 0]
        tap_ref[k + 1] = tap
        return _

    lax.fori_loop(0, CHUNK - 1, one_tap, 0)

    def one(j, _):
        for low in range(0, tiles, step):
            rows = slice(low, low + step)
            q = (q_ref[j, 0, rows, :], q_ref[j, 1, rows, :])
            left = CHUNK
            while left > 1:
                q = times(q, q)
                left //= 2
            state = (incoming_ref[j, 0, rows, :], incoming_ref[j, 1, rows, :])
            for a in range(chunks):
                start_ref[a, j, 0, rows, :] = state[0]
                start_ref[a, j, 1, rows, :] = state[1]
                if a + 1 < chunks:
                    moved = times(state, q)
                    state = (
                        moved[0] + fresh_ref[a, j, 0, rows, :],
                        moved[1] + fresh_ref[a, j, 1, rows, :],
                    )
        return _

    lax.fori_loop(0, NDIM, one, 0)

    for low in range(0, tiles, step):
        rows = slice(low, low + step)
        for b in range(0, CHUNK, 2):
            total = [[jnp.zeros((step, LANES), f32) for _ in range(chunks)] for _ in range(2)]

            def carry(j, total, b=b, rows=rows):
                total = [list(t) for t in total]
                coefs = [(coef_ref[b + i, j, 0, rows, :], coef_ref[b + i, j, 1, rows, :]) for i in range(2)]
                for a in range(chunks):
                    re, im = start_ref[a, j, 0, rows, :], start_ref[a, j, 1, rows, :]
                    for i in range(2):
                        total[i][a] = total[i][a] + coefs[i][0] * re - coefs[i][1] * im
                return total

            total = lax.fori_loop(0, NDIM, carry, total, unroll=4)
            for s in range(b + 2):
                for i in range(2):
                    if s > b + i:
                        continue
                    tap = tap_ref[b + i - s, rows, :]
                    for a in range(chunks):
                        at = (a * CHUNK + s) * tiles + low
                        total[i][a] = total[i][a] + tap * dense_ref[at : at + step, :]
            for i in range(2):
                for a in range(chunks):
                    at = (a * CHUNK + b + i) * tiles + low
                    out_ref[at : at + step, :] = total[i][a]
    for tile in range(tiles):
        lanes = slice(tile * LANES, (tile + 1) * LANES)
        value = out_ref[pl.ds(tile, length, stride=tiles), :]
        mixed_ref[:, lanes] = (value / (1.0 + jnp.exp(-value))).astype(bf16)


def both(block):
    count = lax.axis_size("tp")
    if count == 1:
        return block
    place = lax.axis_index("tp")
    width = block.shape[1]
    others = [
        lax.ppermute(block, "tp", [(i, (i + k) % count) for i in range(count)]) for k in range(1, count)
    ]
    if count == 2:
        other = others[0]
        return jnp.where(
            place == 0, jnp.concatenate([block, other], 1), jnp.concatenate([other, block], 1)
        )
    full = jnp.zeros((block.shape[0], width * count), block.dtype)
    full = lax.dynamic_update_slice_in_dim(full, block, place * width, 1)
    for k, other in enumerate(others, 1):
        full = lax.dynamic_update_slice_in_dim(full, other, ((place - k) % count) * width, 1)
    return full


def attention(z_total, v_total, affine):
    queries = (z_total * affine[0] + affine[1]).astype(bf16)
    key_rows = (z_total * affine[2] + affine[3]).astype(bf16)
    values = jax.nn.silu(v_total).astype(bf16)
    row_count, width = z_total.shape
    stretches = row_count // STRETCH
    queries = queries.reshape(stretches, STRETCH, -1)
    key_rows = key_rows.reshape(stretches, STRETCH, -1)
    values = values.reshape(stretches, STRETCH, -1)
    scores = jnp.einsum("nqd,nkd->nqk", queries, key_rows, preferred_element_type=f32) * (
        1.0 / width**0.5
    )
    causal = jnp.arange(STRETCH)[:, None] >= jnp.arange(STRETCH)[None, :]
    scores = jnp.where(causal[None], scores, -1e30)
    row_max = jnp.max(scores, axis=-1, keepdims=True)
    weights = jnp.exp(scores - row_max)
    probabilities = (weights / jnp.sum(weights, axis=-1, keepdims=True)).astype(bf16)
    result = jnp.einsum("nqk,nkd->nqd", probabilities, values, preferred_element_type=f32)
    return result.reshape(row_count, -1).astype(bf16)


def body(
    tokens, norm_gain, norm_bias, ema_decay, ema_phase, ema_in, ema_out, ema_skip, rms_gain, z_weight, v_weight, qk_affine
):
    length, channels = tokens.shape
    tiles = channels // LANES
    chunks = length // CHUNK
    width = -(-(channels // GROUP) // LANES) * LANES
    place = lax.axis_index("ctx")
    peers = lax.axis_size("ctx")
    head = z_weight.shape[1]
    shape = jax.ShapeDtypeStruct

    weights = lax.all_gather(jnp.concatenate([z_weight, v_weight], 1), "ctx", axis=0, tiled=True)

    csum, csq, totals = call(
        sums_kernel, [shape((length, width), f32), shape((length, width), f32), shape((2, width), f32)]
    )(tokens)
    sums = lax.all_to_all(jnp.broadcast_to(totals[None], (peers, 2, width)), "ctx", 0, 0)

    def dense(a):
        return a.reshape(NDIM, tiles, LANES)

    q = jnp.stack([dense(ema_decay * jnp.cos(ema_phase)), dense(ema_decay * jnp.sin(ema_phase))], 1)
    w = jnp.stack([dense(ema_in * ema_out[0]), dense(ema_in * ema_out[1])], 1)

    normed, rows, fresh, ends = call(
        feed_kernel,
        [
            shape((length, channels), bf16),
            shape((length * tiles, LANES), f32),
            shape((chunks, NDIM, 2, tiles, LANES), f32),
            shape((NDIM, 2, tiles, LANES), f32),
        ],
        [pltpu.VMEM((CHUNK + 1, NDIM, 2, tiles, LANES), f32)],
        True,
        8,
    )(place.astype(jnp.int32).reshape(1), tokens, sums, csum, csq, norm_gain[None], norm_bias[None], q)

    more = max(1, peers // NDIM)

    def split(a):
        a = a.reshape(NDIM, 2, more, tiles // more, LANES).transpose(0, 2, 1, 3, 4)
        return a.reshape(peers, NDIM * more // peers, 2, tiles // more, LANES)

    def join(a):
        a = a.reshape(NDIM, more, 2, tiles // more, LANES).transpose(0, 2, 1, 3, 4)
        return a.reshape(NDIM, 2, tiles, LANES)

    arrived = lax.all_to_all(split(ends), "ctx", 0, 0)
    my_q = lax.dynamic_index_in_dim(split(q), place, 0, False)
    starts = call(functools.partial(scan_kernel, length), shape(arrived.shape, f32), n_in=2)(arrived, my_q)
    incoming = join(lax.all_to_all(starts, "ctx", 0, 0))

    mixed_rows = call(
        mix_kernel,
        shape((length, channels), bf16),
        [
            pltpu.VMEM((chunks, NDIM, 2, tiles, LANES), f32),
            pltpu.VMEM((CHUNK, NDIM, 2, tiles, LANES), f32),
            pltpu.VMEM((CHUNK, tiles, LANES), f32),
            pltpu.VMEM((length * tiles, LANES), f32),
        ],
        n_in=6,
    )(incoming, fresh, rows, q, w, ema_skip.reshape(tiles, LANES))

    full_normed, full_mixed = both(normed), both(mixed_rows)
    mixed_float = full_mixed.astype(f32)
    rms_normed = (
        mixed_float
        * lax.rsqrt(jnp.mean(mixed_float * mixed_float, axis=-1, keepdims=True) + 1e-06)
        * rms_gain
    ).astype(bf16)
    z_total = jnp.dot(rms_normed, weights[:, :head], preferred_element_type=f32)
    v_total = jnp.dot(full_normed, weights[:, head:], preferred_element_type=f32)
    return attention(z_total, v_total, qk_affine)


def solution(mesh):
    in_specs = (
        P("ctx", "tp"),
        P("tp"),
        P("tp"),
        P(None, "tp"),
        P(None, "tp"),
        P(None, "tp"),
        P(None, None, "tp"),
        P("tp"),
        P(),
        P("ctx", "tp"),
        P("ctx", "tp"),
        P(None, "tp"),
    )
    return jax.shard_map(body, mesh=mesh, in_specs=in_specs, out_specs=P("ctx", "tp"), check_vma=False)
```

```python
import functools

import jax
import jax.numpy as jnp
from jax import lax
from jax.experimental import pallas as pl
from jax.experimental.pallas import tpu as pltpu
from jax.sharding import PartitionSpec as P

NDIM = 16
GROUP = 64
STRETCH = 128
CHUNK = 16
LANES = 128
epsilon = 1e-05
f32 = jnp.float32
bf16 = jnp.bfloat16
VMEM_LIMIT = 48 * 1024 * 1024


def call(kernel, outs, scratch=(), smem_first=False, n_in=1):
    specs = [pl.BlockSpec(memory_space=pltpu.VMEM) for _ in range(n_in)]
    if smem_first:
        specs[0] = pl.BlockSpec(memory_space=pltpu.SMEM)
    return pl.pallas_call(
        kernel,
        out_shape=outs,
        in_specs=specs,
        out_specs=jax.tree.map(lambda _: pl.BlockSpec(memory_space=pltpu.VMEM), outs),
        scratch_shapes=list(scratch),
        compiler_params=pltpu.CompilerParams(vmem_limit_bytes=VMEM_LIMIT),
    )


def pieces(value):
    first = value.astype(bf16)
    rest = value - first.astype(f32)
    second = rest.astype(bf16)
    third = (rest - second.astype(f32)).astype(bf16)
    return first, second, third


def mm(a, b):
    return jnp.dot(a, b, preferred_element_type=f32)


def membership(channels, width, transposed):
    shape = (width, channels) if transposed else (channels, width)
    channel = lax.broadcasted_iota(jnp.int32, shape, 1 if transposed else 0)
    group = lax.broadcasted_iota(jnp.int32, shape, 0 if transposed else 1)
    return jnp.where(channel // GROUP == group, 1.0, 0.0).astype(bf16)


def sums_kernel(x_ref, csum_ref, csq_ref, total_ref):
    length, channels = x_ref.shape
    width = csum_ref.shape[1]
    member = membership(channels, width, False)
    x = x_ref[...]
    square = x.astype(f32) * x.astype(f32)
    high = square.astype(bf16)
    low = (square - high.astype(f32)).astype(bf16)
    row_sums = mm(x, member)
    row_squares = mm(high, member) + mm(low, member)
    rows = lax.broadcasted_iota(jnp.int32, (length, length), 0)
    cols = lax.broadcasted_iota(jnp.int32, (length, length), 1)
    lower = jnp.where(rows >= cols, 1.0, 0.0).astype(bf16)
    for ref, value, at in ((csum_ref, row_sums, 0), (csq_ref, row_squares, 1)):
        one, two, three = pieces(value)
        running = mm(lower, one) + mm(lower, two) + mm(lower, three)
        ref[...] = running
        total_ref[at : at + 1, :] = running[length - 1 : length, :]


def powers_into(ref, q_ref, first_re, first_im, count):
    def one(j, _):
        q_re, q_im = q_ref[j, 0], q_ref[j, 1]
        now_re, now_im = first_re(j), first_im(j)
        for k in range(count):
            ref[k, j, 0] = now_re
            ref[k, j, 1] = now_im
            if k + 1 < count:
                now_re, now_im = now_re * q_re - now_im * q_im, now_re * q_im + now_im * q_re
        return _

    lax.fori_loop(0, NDIM, one, 0)


def feed_kernel(
    me_ref, x_ref, sums_ref, csum_ref, csq_ref, gain_ref, bias_ref, q_ref,
    normed_ref, dense_ref, fresh_ref, end_ref, power_ref,
):
    members, _, _, depth = normed_ref.shape
    length, channels = x_ref.shape
    width = csum_ref.shape[1]
    tiles = channels // LANES
    chunks = length // CHUNK
    me = me_ref[0]
    peers = sums_ref.shape[0]
    before = [jnp.zeros((1, width), f32) for _ in range(2)]
    for peer in range(peers):
        earlier = jnp.where(peer < me, 1.0, 0.0)
        for at in range(2):
            before[at] = before[at] + sums_ref[peer, at : at + 1, :] * earlier
    place = lax.broadcasted_iota(jnp.int32, (length, width), 0) + me * length + 1
    counts = place.astype(f32) * GROUP
    average = (before[0] + csum_ref[...]) / counts
    spread = jnp.maximum((before[1] + csq_ref[...]) / counts - average * average, 0.0)
    scale = lax.rsqrt(spread + epsilon)
    member = membership(channels, width, True)
    average_pieces, scale_pieces = pieces(average), pieces(scale)
    for tile in range(tiles):
        lanes = slice(tile * LANES, (tile + 1) * LANES)
        mine = member[:, lanes]
        average_wide = sum(mm(p, mine) for p in average_pieces)
        scale_wide = sum(mm(p, mine) for p in scale_pieces)
        scaled = (x_ref[:, lanes].astype(f32) - average_wide) * scale_wide
        normed = (scaled * gain_ref[:, lanes] + bias_ref[:, lanes]).astype(bf16)
        part = min(depth, LANES)
        for low in range(0, LANES, part):
            at = tile * LANES + low
            block = at // depth
            away = lax.rem(block % members + members - lax.rem(me, members), members)
            normed_ref[away, block // members, :, at % depth : at % depth + part] = normed[:, low : low + part]
        dense_ref[pl.ds(tile, length, stride=tiles), :] = normed.astype(f32)

    sub = q_ref.shape[2]
    powers_into(
        power_ref, q_ref, lambda j: jnp.ones((sub, LANES), f32), lambda j: jnp.zeros((sub, LANES), f32), CHUNK + 1
    )
    step = min(8, tiles)

    def one(j, _):
        for low in range(0, tiles, step):
            rows = slice(low, low + step)
            re = [jnp.zeros((step, LANES), f32) for _ in range(chunks)]
            im = [jnp.zeros((step, LANES), f32) for _ in range(chunks)]
            for b in range(CHUNK):
                p_re = power_ref[CHUNK - 1 - b, j, 0, rows, :]
                p_im = power_ref[CHUNK - 1 - b, j, 1, rows, :]
                for a in range(chunks):
                    at = (a * CHUNK + b) * tiles + low
                    value = dense_ref[at : at + step, :]
                    re[a] = re[a] + p_re * value
                    im[a] = im[a] + p_im * value
            q_re = power_ref[CHUNK, j, 0, rows, :]
            q_im = power_ref[CHUNK, j, 1, rows, :]
            s_re, s_im = re[0], im[0]
            for a in range(chunks):
                fresh_ref[a, j, 0, rows, :] = re[a]
                fresh_ref[a, j, 1, rows, :] = im[a]
                if a:
                    s_re, s_im = (
                        s_re * q_re - s_im * q_im + re[a],
                        s_re * q_im + s_im * q_re + im[a],
                    )
            end_ref[j, 0, rows, :] = s_re
            end_ref[j, 1, rows, :] = s_im
        return _

    lax.fori_loop(0, NDIM, one, 0)


def times(a, b):
    return a[0] * b[0] - a[1] * b[1], a[0] * b[1] + a[1] * b[0]


def scan_kernel(length, ends_ref, q_ref, out_ref):
    peers = ends_ref.shape[0]
    result, base, left = None, (q_ref[:, 0], q_ref[:, 1]), length
    while left:
        if left & 1:
            result = base if result is None else times(result, base)
        left >>= 1
        if left:
            base = times(base, base)
    state = (jnp.zeros_like(base[0]), jnp.zeros_like(base[1]))
    for peer in range(peers):
        out_ref[peer, :, 0] = state[0]
        out_ref[peer, :, 1] = state[1]
        if peer + 1 < peers:
            moved = times(state, result)
            state = (moved[0] + ends_ref[peer, :, 0], moved[1] + ends_ref[peer, :, 1])


def mix_kernel(
    incoming_ref, fresh_ref, dense_ref, q_ref, w_ref, skip_ref,
    mixed_ref, start_ref, coef_ref, tap_ref, out_ref,
):
    length, channels = mixed_ref.shape
    tiles = channels // LANES
    chunks = length // CHUNK
    step = min(8, tiles)

    def first_re(j):
        return w_ref[j, 0] * q_ref[j, 0] - w_ref[j, 1] * q_ref[j, 1]

    def first_im(j):
        return w_ref[j, 0] * q_ref[j, 1] + w_ref[j, 1] * q_ref[j, 0]

    powers_into(coef_ref, q_ref, first_re, first_im, CHUNK)
    tap = skip_ref[...]
    for j in range(NDIM):
        tap = tap + w_ref[j, 0]
    tap_ref[0] = tap

    def one_tap(k, _):
        tap = coef_ref[k, 0, 0]
        for j in range(1, NDIM):
            tap = tap + coef_ref[k, j, 0]
        tap_ref[k + 1] = tap
        return _

    lax.fori_loop(0, CHUNK - 1, one_tap, 0)

    def one(j, _):
        for low in range(0, tiles, step):
            rows = slice(low, low + step)
            q = (q_ref[j, 0, rows, :], q_ref[j, 1, rows, :])
            left = CHUNK
            while left > 1:
                q = times(q, q)
                left //= 2
            state = (incoming_ref[j, 0, rows, :], incoming_ref[j, 1, rows, :])
            for a in range(chunks):
                start_ref[a, j, 0, rows, :] = state[0]
                start_ref[a, j, 1, rows, :] = state[1]
                if a + 1 < chunks:
                    moved = times(state, q)
                    state = (
                        moved[0] + fresh_ref[a, j, 0, rows, :],
                        moved[1] + fresh_ref[a, j, 1, rows, :],
                    )
        return _

    lax.fori_loop(0, NDIM, one, 0)

    for low in range(0, tiles, step):
        rows = slice(low, low + step)
        for b in range(0, CHUNK, 2):
            total = [[jnp.zeros((step, LANES), f32) for _ in range(chunks)] for _ in range(2)]

            def carry(j, total, b=b, rows=rows):
                total = [list(t) for t in total]
                coefs = [(coef_ref[b + i, j, 0, rows, :], coef_ref[b + i, j, 1, rows, :]) for i in range(2)]
                for a in range(chunks):
                    re, im = start_ref[a, j, 0, rows, :], start_ref[a, j, 1, rows, :]
                    for i in range(2):
                        total[i][a] = total[i][a] + coefs[i][0] * re - coefs[i][1] * im
                return total

            total = lax.fori_loop(0, NDIM, carry, total, unroll=4)
            for s in range(b + 2):
                for i in range(2):
                    if s > b + i:
                        continue
                    tap = tap_ref[b + i - s, rows, :]
                    for a in range(chunks):
                        at = (a * CHUNK + s) * tiles + low
                        total[i][a] = total[i][a] + tap * dense_ref[at : at + step, :]
            for i in range(2):
                for a in range(chunks):
                    at = (a * CHUNK + b + i) * tiles + low
                    out_ref[at : at + step, :] = total[i][a]
    for tile in range(tiles):
        lanes = slice(tile * LANES, (tile + 1) * LANES)
        value = out_ref[pl.ds(tile, length, stride=tiles), :]
        mixed_ref[:, lanes] = (value / (1.0 + jnp.exp(-value))).astype(bf16)


def along(block, axis, step, group):
    count = lax.axis_size(axis)
    pairs = [(i, i - i % group + (i + step) % group) for i in range(count)]
    return lax.ppermute(block, axis, pairs)


def others(block, axis):
    count = lax.axis_size(axis)
    return [along(block, axis, k, count) for k in range(1, count)]


def part_kernel(members, tp, at_ref, *refs):
    *refs, own_ref, sent_ref, row_ref = refs
    near, far, weights = refs[:members], refs[members : members + tp - 1], refs[members + tp - 1 :]
    subs, length, _ = near[0].shape
    parts = len(weights)
    half, layer = at_ref[0], at_ref[1]
    for away in range(tp):
        other = lax.rem(half + tp - away, tp)
        for sub in range(subs):
            slot = lax.rem(layer + parts - (other * subs + sub), parts)
            for k in range(members):
                block = far[away - 1][k, sub] if away else near[k][sub]
                row_ref[slot, k * length : (k + 1) * length, :] = block
    for k in range(members):
        here = slice(k * length, (k + 1) * length)
        total = mm(row_ref[0, here, :], weights[0][...])
        for slot in range(1, parts):
            total = total + mm(row_ref[slot, here, :], weights[slot][...])
        if k == 0:
            own_ref[...] = total
        else:
            sent_ref[k - 1] = total.astype(bf16)


def probability_kernel(head, me_ref, *refs):
    *mixed_refs, gain_ref, weight_ref, affine_ref, out_ref = refs
    tp = len(mixed_refs)
    length, channels = mixed_refs[0].shape
    square = jnp.zeros((length, 1), f32)
    for ref in mixed_refs:
        value = ref[...].astype(f32)
        square = square + jnp.sum(value * value, axis=1, keepdims=True)
    scale = lax.rsqrt(square / (channels * tp) + 1e-06)
    z_total = jnp.zeros((length, head), f32)
    for k, ref in enumerate(mixed_refs):
        at = lax.rem(me_ref[0] + tp - k, tp)
        normed = (ref[...].astype(f32) * scale * gain_ref[pl.ds(at, 1), :]).astype(bf16)
        rows = pl.ds(pl.multiple_of(at * channels, channels), channels)
        z_total = z_total + mm(normed, weight_ref[rows, :])
    affine = affine_ref[...]
    queries = (z_total * affine[0:1] + affine[1:2]).astype(bf16)
    key_rows = (z_total * affine[2:3] + affine[3:4]).astype(bf16)
    row = lax.broadcasted_iota(jnp.int32, (STRETCH, STRETCH), 0)
    col = lax.broadcasted_iota(jnp.int32, (STRETCH, STRETCH), 1)
    for low in range(0, length, STRETCH):
        here = slice(low, low + STRETCH)
        scores = lax.dot_general(
            queries[here], key_rows[here], (((1,), (1,)), ((), ())), preferred_element_type=f32
        ) * (1.0 / head**0.5)
        scores = jnp.where(row >= col, scores, -1e30)
        weights = jnp.exp(scores - jnp.max(scores, axis=1, keepdims=True))
        out_ref[here, :] = (weights / jnp.sum(weights, axis=1, keepdims=True)).astype(bf16)


def attend_kernel(own_ref, *refs):
    *parts, probability_ref, out_ref = refs
    total = own_ref[...]
    for part in parts:
        total = total + part[...].astype(f32)
    values = (total / (1.0 + jnp.exp(-total))).astype(bf16)
    for low in range(0, total.shape[0], STRETCH):
        here = slice(low, low + STRETCH)
        out_ref[here, :] = mm(probability_ref[here, :], values[here]).astype(bf16)


def body(
    tokens, norm_gain, norm_bias, ema_decay, ema_phase, ema_in, ema_out, ema_skip, rms_gain, z_weight, v_weight, qk_affine
):
    length, channels = tokens.shape
    tiles = channels // LANES
    chunks = length // CHUNK
    width = -(-(channels // GROUP) // LANES) * LANES
    place = lax.axis_index("ctx")
    peers = lax.axis_size("ctx")
    head = z_weight.shape[1]
    tp, half = lax.axis_size("tp"), lax.axis_index("tp")
    depth, columns = v_weight.shape
    blocks = channels // depth
    members = 4 if peers % 4 == 0 and blocks % 4 == 0 else 1
    layers = peers // members
    shape = jax.ShapeDtypeStruct

    all_z = lax.all_gather(z_weight, "ctx", axis=0, tiled=True)
    layer_pairs = [[(i, (i + members * k) % peers) for i in range(peers)] for k in range(layers)]
    all_v = [v_weight] + [lax.ppermute(v_weight, "ctx", layer_pairs[k]) for k in range(1, layers)]

    csum, csq, totals = call(
        sums_kernel, [shape((length, width), f32), shape((length, width), f32), shape((2, width), f32)]
    )(tokens)
    sums = lax.all_to_all(jnp.broadcast_to(totals[None], (peers, 2, width)), "ctx", 0, 0)

    def dense(a):
        return a.reshape(NDIM, tiles, LANES)

    q = jnp.stack([dense(ema_decay * jnp.cos(ema_phase)), dense(ema_decay * jnp.sin(ema_phase))], 1)
    w = jnp.stack([dense(ema_in * ema_out[0]), dense(ema_in * ema_out[1])], 1)

    normed, rows, fresh, ends = call(
        feed_kernel,
        [
            shape((members, blocks // members, length, depth), bf16),
            shape((length * tiles, LANES), f32),
            shape((chunks, NDIM, 2, tiles, LANES), f32),
            shape((NDIM, 2, tiles, LANES), f32),
        ],
        [pltpu.VMEM((CHUNK + 1, NDIM, 2, tiles, LANES), f32)],
        True,
        8,
    )(place.astype(jnp.int32).reshape(1), tokens, sums, csum, csq, norm_gain[None], norm_bias[None], q)

    more = max(1, peers // NDIM)

    def split(a):
        a = a.reshape(NDIM, 2, more, tiles // more, LANES).transpose(0, 2, 1, 3, 4)
        return a.reshape(peers, NDIM * more // peers, 2, tiles // more, LANES)

    def join(a):
        a = a.reshape(NDIM, more, 2, tiles // more, LANES).transpose(0, 2, 1, 3, 4)
        return a.reshape(NDIM, 2, tiles, LANES)

    arrived = lax.all_to_all(split(ends), "ctx", 0, 0)
    my_q = lax.dynamic_index_in_dim(split(q), place, 0, False)
    starts = call(functools.partial(scan_kernel, length), shape(arrived.shape, f32), n_in=2)(arrived, my_q)
    incoming = join(lax.all_to_all(starts, "ctx", 0, 0))

    mixed_rows = call(
        mix_kernel,
        shape((length, channels), bf16),
        [
            pltpu.VMEM((chunks, NDIM, 2, tiles, LANES), f32),
            pltpu.VMEM((CHUNK, NDIM, 2, tiles, LANES), f32),
            pltpu.VMEM((CHUNK, tiles, LANES), f32),
            pltpu.VMEM((length * tiles, LANES), f32),
        ],
        n_in=6,
    )(incoming, fresh, rows, q, w, ema_skip.reshape(tiles, LANES))

    near = [normed[0]] + [along(normed[k], "ctx", k, members) for k in range(1, members)]
    far = others(jnp.stack(near), "tp")
    own, sent = call(
        functools.partial(part_kernel, members, tp),
        [shape((length, columns), f32), shape((max(members - 1, 1), length, columns), bf16)],
        [pltpu.VMEM((layers, members * length, depth), bf16)],
        True,
        members + tp + layers,
    )(jnp.stack([half, place // members]).astype(jnp.int32), *near, *far, *all_v)
    returned = [along(sent[k - 1], "ctx", -k, members) for k in range(1, members)]

    probabilities = call(
        functools.partial(probability_kernel, head), shape((length, STRETCH), bf16), (), True, tp + 4
    )(half.astype(jnp.int32).reshape(1), mixed_rows, *others(mixed_rows, "tp"), rms_gain.reshape(tp, channels), all_z, qk_affine)
    return call(attend_kernel, shape((length, columns), bf16), n_in=members + 1)(own, *returned, probabilities)


def solution(mesh):
    in_specs = (
        P("ctx", "tp"),
        P("tp"),
        P("tp"),
        P(None, "tp"),
        P(None, "tp"),
        P(None, "tp"),
        P(None, None, "tp"),
        P("tp"),
        P(),
        P("ctx", "tp"),
        P("ctx", "tp"),
        P(None, "tp"),
    )
    return jax.shard_map(body, mesh=mesh, in_specs=in_specs, out_specs=P("ctx", "tp"), check_vma=False)
```

```python
import functools

import jax
import jax.numpy as jnp
from jax import lax
from jax.experimental import pallas as pl
from jax.experimental.pallas import tpu as pltpu
from jax.sharding import PartitionSpec as P

NDIM = 16
GROUP = 64
STRETCH = 128
CHUNK = 16
LANES = 128
epsilon = 1e-05
f32 = jnp.float32
bf16 = jnp.bfloat16
VMEM_LIMIT = 48 * 1024 * 1024


def call(kernel, outs, scratch=(), smem_first=False, n_in=1):
    specs = [pl.BlockSpec(memory_space=pltpu.VMEM) for _ in range(n_in)]
    if smem_first:
        specs[0] = pl.BlockSpec(memory_space=pltpu.SMEM)
    return pl.pallas_call(
        kernel,
        out_shape=outs,
        in_specs=specs,
        out_specs=jax.tree.map(lambda _: pl.BlockSpec(memory_space=pltpu.VMEM), outs),
        scratch_shapes=list(scratch),
        compiler_params=pltpu.CompilerParams(vmem_limit_bytes=VMEM_LIMIT),
    )


def pieces(value):
    first = value.astype(bf16)
    rest = value - first.astype(f32)
    second = rest.astype(bf16)
    third = (rest - second.astype(f32)).astype(bf16)
    return first, second, third


def mm(a, b):
    return jnp.dot(a, b, preferred_element_type=f32)


def membership(channels, width, transposed):
    shape = (width, channels) if transposed else (channels, width)
    channel = lax.broadcasted_iota(jnp.int32, shape, 1 if transposed else 0)
    group = lax.broadcasted_iota(jnp.int32, shape, 0 if transposed else 1)
    return jnp.where(channel // GROUP == group, 1.0, 0.0).astype(bf16)


def sums_kernel(x_ref, csum_ref, csq_ref, total_ref):
    length, channels = x_ref.shape
    width = csum_ref.shape[1]
    member = membership(channels, width, False)
    x = x_ref[...]
    square = x.astype(f32) * x.astype(f32)
    high = square.astype(bf16)
    low = (square - high.astype(f32)).astype(bf16)
    row_sums = mm(x, member)
    row_squares = mm(high, member) + mm(low, member)
    rows = lax.broadcasted_iota(jnp.int32, (length, length), 0)
    cols = lax.broadcasted_iota(jnp.int32, (length, length), 1)
    lower = jnp.where(rows >= cols, 1.0, 0.0).astype(bf16)
    for ref, value, at in ((csum_ref, row_sums, 0), (csq_ref, row_squares, 1)):
        one, two, three = pieces(value)
        running = mm(lower, one) + mm(lower, two) + mm(lower, three)
        ref[...] = running
        total_ref[at : at + 1, :] = running[length - 1 : length, :]


def powers_into(ref, q_ref, first_re, first_im, count):
    def one(j, _):
        q_re, q_im = q_ref[j, 0], q_ref[j, 1]
        now_re, now_im = first_re(j), first_im(j)
        for k in range(count):
            ref[k, j, 0] = now_re
            ref[k, j, 1] = now_im
            if k + 1 < count:
                now_re, now_im = now_re * q_re - now_im * q_im, now_re * q_im + now_im * q_re
        return _

    lax.fori_loop(0, NDIM, one, 0)


def feed_kernel(
    me_ref, x_ref, sums_ref, csum_ref, csq_ref, gain_ref, bias_ref, q_ref,
    normed_ref, dense_ref, fresh_ref, end_ref, power_ref,
):
    members, _, _, depth = normed_ref.shape
    length, channels = x_ref.shape
    width = csum_ref.shape[1]
    tiles = channels // LANES
    chunks = length // CHUNK
    me = me_ref[0]
    peers = sums_ref.shape[0]
    before = [jnp.zeros((1, width), f32) for _ in range(2)]
    for peer in range(peers):
        earlier = jnp.where(peer < me, 1.0, 0.0)
        for at in range(2):
            before[at] = before[at] + sums_ref[peer, at : at + 1, :] * earlier
    place = lax.broadcasted_iota(jnp.int32, (length, width), 0) + me * length + 1
    counts = place.astype(f32) * GROUP
    average = (before[0] + csum_ref[...]) / counts
    spread = jnp.maximum((before[1] + csq_ref[...]) / counts - average * average, 0.0)
    scale = lax.rsqrt(spread + epsilon)
    member = membership(channels, width, True)
    average_pieces, scale_pieces = pieces(average), pieces(scale)
    for tile in range(tiles):
        lanes = slice(tile * LANES, (tile + 1) * LANES)
        mine = member[:, lanes]
        average_wide = sum(mm(p, mine) for p in average_pieces)
        scale_wide = sum(mm(p, mine) for p in scale_pieces)
        scaled = (x_ref[:, lanes].astype(f32) - average_wide) * scale_wide
        normed = (scaled * gain_ref[:, lanes] + bias_ref[:, lanes]).astype(bf16)
        part = min(depth, LANES)
        for low in range(0, LANES, part):
            at = tile * LANES + low
            block = at // depth
            away = lax.rem(block % members + members - lax.rem(me, members), members)
            normed_ref[away, block // members, :, at % depth : at % depth + part] = normed[:, low : low + part]
        dense_ref[pl.ds(tile, length, stride=tiles), :] = normed.astype(f32)

    sub = q_ref.shape[2]
    powers_into(
        power_ref, q_ref, lambda j: jnp.ones((sub, LANES), f32), lambda j: jnp.zeros((sub, LANES), f32), CHUNK + 1
    )
    step = min(8, tiles)

    def one(j, _):
        for low in range(0, tiles, step):
            rows = slice(low, low + step)
            re = [jnp.zeros((step, LANES), f32) for _ in range(chunks)]
            im = [jnp.zeros((step, LANES), f32) for _ in range(chunks)]
            for b in range(CHUNK):
                p_re = power_ref[CHUNK - 1 - b, j, 0, rows, :]
                p_im = power_ref[CHUNK - 1 - b, j, 1, rows, :]
                for a in range(chunks):
                    at = (a * CHUNK + b) * tiles + low
                    value = dense_ref[at : at + step, :]
                    re[a] = re[a] + p_re * value
                    im[a] = im[a] + p_im * value
            q_re = power_ref[CHUNK, j, 0, rows, :]
            q_im = power_ref[CHUNK, j, 1, rows, :]
            s_re, s_im = re[0], im[0]
            for a in range(chunks):
                fresh_ref[a, j, 0, rows, :] = re[a]
                fresh_ref[a, j, 1, rows, :] = im[a]
                if a:
                    s_re, s_im = (
                        s_re * q_re - s_im * q_im + re[a],
                        s_re * q_im + s_im * q_re + im[a],
                    )
            end_ref[j, 0, rows, :] = s_re
            end_ref[j, 1, rows, :] = s_im
        return _

    lax.fori_loop(0, NDIM, one, 0)


def times(a, b):
    return a[0] * b[0] - a[1] * b[1], a[0] * b[1] + a[1] * b[0]


def scan_kernel(length, ends_ref, q_ref, out_ref):
    peers = ends_ref.shape[0]
    result, base, left = None, (q_ref[:, 0], q_ref[:, 1]), length
    while left:
        if left & 1:
            result = base if result is None else times(result, base)
        left >>= 1
        if left:
            base = times(base, base)
    state = (jnp.zeros_like(base[0]), jnp.zeros_like(base[1]))
    for peer in range(peers):
        out_ref[peer, :, 0] = state[0]
        out_ref[peer, :, 1] = state[1]
        if peer + 1 < peers:
            moved = times(state, result)
            state = (moved[0] + ends_ref[peer, :, 0], moved[1] + ends_ref[peer, :, 1])


def mix_kernel(
    incoming_ref, fresh_ref, dense_ref, q_ref, w_ref, skip_ref,
    mixed_ref, start_ref, coef_ref, tap_ref, out_ref,
):
    length, channels = mixed_ref.shape
    tiles = channels // LANES
    chunks = length // CHUNK
    step = min(8, tiles)

    def first_re(j):
        return w_ref[j, 0] * q_ref[j, 0] - w_ref[j, 1] * q_ref[j, 1]

    def first_im(j):
        return w_ref[j, 0] * q_ref[j, 1] + w_ref[j, 1] * q_ref[j, 0]

    powers_into(coef_ref, q_ref, first_re, first_im, CHUNK)
    tap = skip_ref[...]
    for j in range(NDIM):
        tap = tap + w_ref[j, 0]
    tap_ref[0] = tap

    def one_tap(k, _):
        tap = coef_ref[k, 0, 0]
        for j in range(1, NDIM):
            tap = tap + coef_ref[k, j, 0]
        tap_ref[k + 1] = tap
        return _

    lax.fori_loop(0, CHUNK - 1, one_tap, 0)

    def one(j, _):
        for low in range(0, tiles, step):
            rows = slice(low, low + step)
            q = (q_ref[j, 0, rows, :], q_ref[j, 1, rows, :])
            left = CHUNK
            while left > 1:
                q = times(q, q)
                left //= 2
            state = (incoming_ref[j, 0, rows, :], incoming_ref[j, 1, rows, :])
            for a in range(chunks):
                start_ref[a, j, 0, rows, :] = state[0]
                start_ref[a, j, 1, rows, :] = state[1]
                if a + 1 < chunks:
                    moved = times(state, q)
                    state = (
                        moved[0] + fresh_ref[a, j, 0, rows, :],
                        moved[1] + fresh_ref[a, j, 1, rows, :],
                    )
        return _

    lax.fori_loop(0, NDIM, one, 0)

    for low in range(0, tiles, step):
        rows = slice(low, low + step)
        for b in range(0, CHUNK, 2):
            total = [[jnp.zeros((step, LANES), f32) for _ in range(chunks)] for _ in range(2)]

            def carry(j, total, b=b, rows=rows):
                total = [list(t) for t in total]
                coefs = [(coef_ref[b + i, j, 0, rows, :], coef_ref[b + i, j, 1, rows, :]) for i in range(2)]
                for a in range(chunks):
                    re, im = start_ref[a, j, 0, rows, :], start_ref[a, j, 1, rows, :]
                    for i in range(2):
                        total[i][a] = total[i][a] + coefs[i][0] * re - coefs[i][1] * im
                return total

            total = lax.fori_loop(0, NDIM, carry, total, unroll=4)
            for s in range(b + 2):
                for i in range(2):
                    if s > b + i:
                        continue
                    tap = tap_ref[b + i - s, rows, :]
                    for a in range(chunks):
                        at = (a * CHUNK + s) * tiles + low
                        total[i][a] = total[i][a] + tap * dense_ref[at : at + step, :]
            for i in range(2):
                for a in range(chunks):
                    at = (a * CHUNK + b + i) * tiles + low
                    out_ref[at : at + step, :] = total[i][a]
    for tile in range(tiles):
        lanes = slice(tile * LANES, (tile + 1) * LANES)
        value = out_ref[pl.ds(tile, length, stride=tiles), :]
        mixed_ref[:, lanes] = (value / (1.0 + jnp.exp(-value))).astype(bf16)


def along(block, axis, step, group):
    count = lax.axis_size(axis)
    pairs = [(i, i - i % group + (i + step) % group) for i in range(count)]
    return lax.ppermute(block, axis, pairs)


def others(block, axis):
    count = lax.axis_size(axis)
    return [along(block, axis, k, count) for k in range(1, count)]


def part_kernel(members, tp, half_ref, *refs):
    *refs, weight_ref, own_ref, sent_ref, row_ref = refs
    near, far = refs[:members], refs[members:]
    subs, length, depth = near[0].shape
    for away in range(tp):
        other = lax.rem(half_ref[0] + tp - away, tp)
        for sub in range(subs):
            for k in range(members):
                block = far[away - 1][k, sub] if away else near[k][sub]
                row_ref[other * subs + sub, k * length : (k + 1) * length, :] = block
    for k in range(members):
        here = slice(k * length, (k + 1) * length)
        total = mm(row_ref[0, here, :], weight_ref[:depth, :])
        for slot in range(1, row_ref.shape[0]):
            total = total + mm(row_ref[slot, here, :], weight_ref[slot * depth : (slot + 1) * depth, :])
        if k == 0:
            own_ref[...] = total
        else:
            sent_ref[k - 1] = total.astype(bf16)


def probability_kernel(members, at_ref, *refs):
    *refs, gain_ref, affine_ref, out_ref, row_ref = refs
    weights, mixed_refs = refs[:members], refs[members:]
    tp = len(mixed_refs)
    layers, depth, head = weights[0].shape
    length, channels = mixed_refs[0].shape
    half, member, layer = at_ref[0], at_ref[1], at_ref[2]
    square = jnp.zeros((length, 1), f32)
    for ref in mixed_refs:
        value = ref[...].astype(f32)
        square = square + jnp.sum(value * value, axis=1, keepdims=True)
    scale = lax.rsqrt(square / (channels * tp) + 1e-06)
    blocks = channels // depth
    for k, ref in enumerate(mixed_refs):
        at = lax.rem(half + tp - k, tp)
        normed = (ref[...].astype(f32) * scale * gain_ref[pl.ds(at, 1), :]).astype(bf16)
        for block in range(blocks):
            row_ref[at * blocks + block] = normed[:, block * depth : (block + 1) * depth]
    z_total = jnp.zeros((length, head), f32)
    for m in range(members):
        for k in range(layers):
            block = lax.rem(layer + layers - k, layers) * members + lax.rem(member + members - m, members)
            z_total = z_total + mm(row_ref[block], weights[m][k])
    affine = affine_ref[...]
    queries = (z_total * affine[0:1] + affine[1:2]).astype(bf16)
    key_rows = (z_total * affine[2:3] + affine[3:4]).astype(bf16)
    row = lax.broadcasted_iota(jnp.int32, (STRETCH, STRETCH), 0)
    col = lax.broadcasted_iota(jnp.int32, (STRETCH, STRETCH), 1)
    for low in range(0, length, STRETCH):
        here = slice(low, low + STRETCH)
        scores = lax.dot_general(
            queries[here], key_rows[here], (((1,), (1,)), ((), ())), preferred_element_type=f32
        ) * (1.0 / head**0.5)
        scores = jnp.where(row >= col, scores, -1e30)
        weights = jnp.exp(scores - jnp.max(scores, axis=1, keepdims=True))
        out_ref[here, :] = (weights / jnp.sum(weights, axis=1, keepdims=True)).astype(bf16)


def attend_kernel(own_ref, *refs):
    *parts, probability_ref, out_ref = refs
    total = own_ref[...]
    for part in parts:
        total = total + part[...].astype(f32)
    values = (total / (1.0 + jnp.exp(-total))).astype(bf16)
    for low in range(0, total.shape[0], STRETCH):
        here = slice(low, low + STRETCH)
        out_ref[here, :] = mm(probability_ref[here, :], values[here]).astype(bf16)


def body(
    tokens, norm_gain, norm_bias, ema_decay, ema_phase, ema_in, ema_out, ema_skip, rms_gain, z_weight, v_weight, qk_affine
):
    length, channels = tokens.shape
    tiles = channels // LANES
    chunks = length // CHUNK
    width = -(-(channels // GROUP) // LANES) * LANES
    place = lax.axis_index("ctx")
    peers = lax.axis_size("ctx")
    tp, half = lax.axis_size("tp"), lax.axis_index("tp")
    depth, columns = v_weight.shape
    blocks = channels // depth
    members = 4 if peers % 4 == 0 and blocks % 4 == 0 else 1
    layers = peers // members
    shape = jax.ShapeDtypeStruct

    member, layer = place % members, place // members
    lines = [[r + members * k for k in range(layers)] for r in range(members)]
    all_v = lax.all_gather(v_weight, "ctx", axis=0, tiled=True, axis_index_groups=lines)
    line_z = [z_weight] + [
        lax.ppermute(z_weight, "ctx", [(i, (i + members * k) % peers) for i in range(peers)])
        for k in range(1, layers)
    ]
    line_z = jnp.stack(line_z)

    csum, csq, totals = call(
        sums_kernel, [shape((length, width), f32), shape((length, width), f32), shape((2, width), f32)]
    )(tokens)
    sums = lax.all_to_all(jnp.broadcast_to(totals[None], (peers, 2, width)), "ctx", 0, 0)

    sums, line_z = lax.optimization_barrier((sums, line_z))
    all_z = [line_z] + [along(line_z, "ctx", k, members) for k in range(1, members)]

    def dense(a):
        return a.reshape(NDIM, tiles, LANES)

    q = jnp.stack([dense(ema_decay * jnp.cos(ema_phase)), dense(ema_decay * jnp.sin(ema_phase))], 1)
    w = jnp.stack([dense(ema_in * ema_out[0]), dense(ema_in * ema_out[1])], 1)

    normed, rows, fresh, ends = call(
        feed_kernel,
        [
            shape((members, blocks // members, length, depth), bf16),
            shape((length * tiles, LANES), f32),
            shape((chunks, NDIM, 2, tiles, LANES), f32),
            shape((NDIM, 2, tiles, LANES), f32),
        ],
        [pltpu.VMEM((CHUNK + 1, NDIM, 2, tiles, LANES), f32)],
        True,
        8,
    )(place.astype(jnp.int32).reshape(1), tokens, sums, csum, csq, norm_gain[None], norm_bias[None], q)

    more = max(1, peers // NDIM)

    def split(a):
        a = a.reshape(NDIM, 2, more, tiles // more, LANES).transpose(0, 2, 1, 3, 4)
        return a.reshape(peers, NDIM * more // peers, 2, tiles // more, LANES)

    def join(a):
        a = a.reshape(NDIM, more, 2, tiles // more, LANES).transpose(0, 2, 1, 3, 4)
        return a.reshape(NDIM, 2, tiles, LANES)

    arrived = lax.all_to_all(split(ends), "ctx", 0, 0)
    my_q = lax.dynamic_index_in_dim(split(q), place, 0, False)
    starts = call(functools.partial(scan_kernel, length), shape(arrived.shape, f32), n_in=2)(arrived, my_q)
    incoming = join(lax.all_to_all(starts, "ctx", 0, 0))

    mixed_rows = call(
        mix_kernel,
        shape((length, channels), bf16),
        [
            pltpu.VMEM((chunks, NDIM, 2, tiles, LANES), f32),
            pltpu.VMEM((CHUNK, NDIM, 2, tiles, LANES), f32),
            pltpu.VMEM((CHUNK, tiles, LANES), f32),
            pltpu.VMEM((length * tiles, LANES), f32),
        ],
        n_in=6,
    )(incoming, fresh, rows, q, w, ema_skip.reshape(tiles, LANES))

    near = [normed[0]] + [along(normed[k], "ctx", k, members) for k in range(1, members)]
    far = others(jnp.stack(near), "tp")
    own, sent = call(
        functools.partial(part_kernel, members, tp),
        [shape((length, columns), f32), shape((max(members - 1, 1), length, columns), bf16)],
        [pltpu.VMEM((layers, members * length, depth), bf16)],
        True,
        members + tp + 1,
    )(half.astype(jnp.int32).reshape(1), *near, *far, all_v)
    returned = [along(sent[k - 1], "ctx", -k, members) for k in range(1, members)]

    probabilities = call(
        functools.partial(probability_kernel, members),
        shape((length, STRETCH), bf16),
        [pltpu.VMEM((tp * blocks, length, depth), bf16)],
        True,
        members + tp + 3,
    )(
        jnp.stack([half, member, layer]).astype(jnp.int32),
        *all_z,
        mixed_rows,
        *others(mixed_rows, "tp"),
        rms_gain.reshape(tp, channels),
        qk_affine,
    )
    return call(attend_kernel, shape((length, columns), bf16), n_in=members + 1)(own, *returned, probabilities)


def solution(mesh):
    in_specs = (
        P("ctx", "tp"),
        P("tp"),
        P("tp"),
        P(None, "tp"),
        P(None, "tp"),
        P(None, "tp"),
        P(None, None, "tp"),
        P("tp"),
        P(),
        P("ctx", "tp"),
        P("ctx", "tp"),
        P(None, "tp"),
    )
    return jax.shard_map(body, mesh=mesh, in_specs=in_specs, out_specs=P("ctx", "tp"), check_vma=False)
```

```python
import functools

import jax
import jax.numpy as jnp
from jax import lax
from jax.experimental import pallas as pl
from jax.experimental.pallas import tpu as pltpu
from jax.sharding import PartitionSpec as P

NDIM = 16
GROUP = 64
STRETCH = 128
CHUNK = 16
LANES = 128
epsilon = 1e-05
f32 = jnp.float32
bf16 = jnp.bfloat16
VMEM_LIMIT = 64 * 1024 * 1024
CHEAP = pl.CostEstimate(flops=1, bytes_accessed=1, transcendentals=0)


def call(kernel, outs, inputs, scratch=(), copies=0, plain=0):
    hbm, vmem = pl.BlockSpec(memory_space=pltpu.HBM), pl.BlockSpec(memory_space=pltpu.VMEM)
    here = vmem if plain else hbm
    extra = [pltpu.SemaphoreType.DMA((copies,))] if copies else []
    return pl.pallas_call(
        kernel,
        out_shape=outs,
        in_specs=[pl.BlockSpec(memory_space=pltpu.SMEM)] + [here] * (len(inputs) - 1),
        out_specs=[here] * len(outs),
        scratch_shapes=list(scratch) + extra,
        compiler_params=pltpu.CompilerParams(vmem_limit_bytes=VMEM_LIMIT),
        cost_estimate=CHEAP,
    )(*inputs)


class Copies:
    def __init__(self, sems):
        self.sems, self.used = sems, 0

    def start(self, source, target):
        copy = pltpu.make_async_copy(source, target, self.sems.at[self.used])
        self.used += 1
        copy.start()
        return copy


def pieces(value):
    first = value.astype(bf16)
    rest = value - first.astype(f32)
    second = rest.astype(bf16)
    third = (rest - second.astype(f32)).astype(bf16)
    return first, second, third


def mm(a, b):
    return jnp.dot(a, b, preferred_element_type=f32)


def membership(channels, width, transposed, first):
    shape = (width, channels) if transposed else (channels, width)
    channel = lax.broadcasted_iota(jnp.int32, shape, 1 if transposed else 0) + first
    group = lax.broadcasted_iota(jnp.int32, shape, 0 if transposed else 1)
    return jnp.where(channel // GROUP == group, 1.0, 0.0).astype(bf16)


def group_sums(x, first, width):
    member = membership(x.shape[1], width, False, first)
    square = x.astype(f32) * x.astype(f32)
    high = square.astype(bf16)
    low = (square - high.astype(f32)).astype(bf16)
    return mm(x, member), mm(high, member) + mm(low, member)


def sums_kernel(at_ref, x_hbm, running_hbm, total_hbm, x_ref, running_ref, total_ref, sems):
    length, channels = x_ref.shape
    width = running_ref.shape[2]
    copies = Copies(sems)
    cut = channels // min(4, channels // LANES)
    loads = [copies.start(x_hbm.at[:, low : low + cut], x_ref.at[:, low : low + cut]) for low in range(0, channels, cut)]
    rows = lax.broadcasted_iota(jnp.int32, (length, length), 0)
    cols = lax.broadcasted_iota(jnp.int32, (length, length), 1)
    lower = jnp.where(rows >= cols, 1.0, 0.0).astype(bf16)
    sums = [jnp.zeros((length, width), f32)] * 2
    for at, load in enumerate(loads):
        load.wait()
        new = group_sums(x_ref[:, at * cut : (at + 1) * cut], at * cut, width)
        sums = [old + more for old, more in zip(sums, new)]
    for at in range(2):
        one, two, three = pieces(sums[at])
        running = mm(lower, one) + mm(lower, two) + mm(lower, three)
        running_ref[at] = running
        for peer in range(total_ref.shape[0]):
            total_ref[peer, at : at + 1, :] = running[length - 1 : length, :]
    stores = [copies.start(total_ref, total_hbm), copies.start(running_ref, running_hbm)]
    for store in stores:
        store.wait()


def times(a, b):
    return a[0] * b[0] - a[1] * b[1], a[0] * b[1] + a[1] * b[0]


def row_pair(ref, j, tiles):
    start = pl.multiple_of(j * (2 * tiles), 2 * tiles)
    return ref[pl.ds(start, tiles), :], ref[pl.ds(start + tiles, tiles), :]


def powers_into(ref, first, factor, count):
    def one(j, _):
        q, now = factor(j), first(j)
        for k in range(count):
            ref[k, j, 0], ref[k, j, 1] = now
            if k + 1 < count:
                now = times(now, q)
        return _

    lax.fori_loop(0, NDIM, one, 0)


def feed_kernel(members, at_ref, *refs):
    x_hbm, sums_hbm, running_hbm, gain_hbm, bias_hbm, decay_hbm, phase_hbm, in_hbm, out_hbm = refs[:9]
    near_hbm, (dense_hbm, fresh_hbm, end_hbm, q_hbm, w_hbm) = refs[9 : 9 + members], refs[9 + members : 14 + members]
    (
        x_ref, sums_ref, running_ref, gain_ref, bias_ref, decay_ref, phase_ref, in_ref, out_ref,
        normed_ref, dense_ref, fresh_ref, end_ref, q_ref, w_ref, power_ref, sems,
    ) = refs[14 + members :]
    copies = Copies(sems)
    loads = [
        copies.start(a, b)
        for a, b in (
            (decay_hbm, decay_ref), (phase_hbm, phase_ref), (running_hbm, running_ref), (sums_hbm, sums_ref), (x_hbm, x_ref),
            (gain_hbm, gain_ref), (bias_hbm, bias_ref), (in_hbm, in_ref), (out_hbm, out_ref),
        )
    ]
    length, channels = x_ref.shape
    width = running_ref.shape[2]
    tiles = channels // LANES
    chunks = length // CHUNK
    subs, _, depth = near_hbm[0].shape
    me = at_ref[0]
    peers = sums_ref.shape[0]

    loads[0].wait()
    loads[1].wait()
    for tile in range(tiles):
        lanes = slice(tile * LANES, (tile + 1) * LANES)
        phase, decay = phase_ref[:, lanes], decay_ref[:, lanes]
        parts = (decay * jnp.cos(phase), decay * jnp.sin(phase))
        for part in range(2):
            q_ref[pl.ds(part * tiles + tile, NDIM, stride=2 * tiles), :] = parts[part]
    stores = [copies.start(q_ref, q_hbm)]
    one, zero = jnp.ones((tiles, LANES), f32), jnp.zeros((tiles, LANES), f32)
    powers_into(power_ref, lambda j: (one, zero), lambda j: row_pair(q_ref, j, tiles), CHUNK + 1)

    for load in loads[2:7]:
        load.wait()
    before = [jnp.zeros((1, width), f32) for _ in range(2)]
    for peer in range(peers):
        earlier = jnp.where(peer < me, 1.0, 0.0)
        for at in range(2):
            before[at] = before[at] + sums_ref[peer, at : at + 1, :] * earlier
    place = lax.broadcasted_iota(jnp.int32, (length, width), 0) + me * length + 1
    counts = place.astype(f32) * GROUP
    average = (before[0] + running_ref[0]) / counts
    spread = jnp.maximum((before[1] + running_ref[1]) / counts - average * average, 0.0)
    scale = lax.rsqrt(spread + epsilon)
    member = membership(channels, width, True, 0)
    average_pieces, scale_pieces = pieces(average), pieces(scale)
    for tile in range(tiles):
        lanes = slice(tile * LANES, (tile + 1) * LANES)
        mine = member[:, lanes]
        average_wide = sum(mm(p, mine) for p in average_pieces)
        scale_wide = sum(mm(p, mine) for p in scale_pieces)
        scaled = (x_ref[:, lanes].astype(f32) - average_wide) * scale_wide
        normed = (scaled * gain_ref[:, lanes] + bias_ref[:, lanes]).astype(bf16)
        part = min(depth, LANES)
        for low in range(0, LANES, part):
            at = tile * LANES + low
            normed_ref[at // depth, :, at % depth : at % depth + part] = normed[:, low : low + part]
        dense_ref[pl.ds(tile, length, stride=tiles), :] = normed.astype(f32)
    for away, ref in enumerate(near_hbm):
        to = lax.rem(me + away, members)
        for sub in range(subs):
            stores.append(copies.start(normed_ref.at[sub * members + to], ref.at[sub]))
    stores.append(copies.start(dense_ref, dense_hbm))

    loads[7].wait()
    loads[8].wait()
    for tile in range(tiles):
        lanes = slice(tile * LANES, (tile + 1) * LANES)
        for part in range(2):
            w_ref[pl.ds(part * tiles + tile, NDIM, stride=2 * tiles), :] = in_ref[:, lanes] * out_ref[part, :, lanes]
    stores.append(copies.start(w_ref, w_hbm))
    step = min(8, tiles)
    first_sem = copies.used

    def send(j):
        return pltpu.make_async_copy(fresh_ref.at[j], fresh_hbm.at[j], sems.at[first_sem + j])

    def one(j, _):
        for low in range(0, tiles, step):
            rows = slice(low, low + step)
            re = [jnp.zeros((step, LANES), f32) for _ in range(chunks)]
            im = [jnp.zeros((step, LANES), f32) for _ in range(chunks)]
            for b in range(CHUNK):
                p_re = power_ref[CHUNK - 1 - b, j, 0, rows, :]
                p_im = power_ref[CHUNK - 1 - b, j, 1, rows, :]
                for a in range(chunks):
                    at = (a * CHUNK + b) * tiles + low
                    value = dense_ref[at : at + step, :]
                    re[a] = re[a] + p_re * value
                    im[a] = im[a] + p_im * value
            q = (power_ref[CHUNK, j, 0, rows, :], power_ref[CHUNK, j, 1, rows, :])
            state = (re[0], im[0])
            for a in range(chunks):
                fresh_ref[j, a, 0, rows, :] = re[a]
                fresh_ref[j, a, 1, rows, :] = im[a]
                if a:
                    moved = times(state, q)
                    state = (moved[0] + re[a], moved[1] + im[a])
            end_ref[j, 0, rows, :], end_ref[j, 1, rows, :] = state
        send(j).start()
        return _

    lax.fori_loop(0, NDIM, one, 0)
    ends = pltpu.make_async_copy(end_ref, end_hbm, sems.at[first_sem + NDIM])
    ends.start()
    for store in stores:
        store.wait()
    lax.fori_loop(0, NDIM, lambda j, c: (send(j).wait(), c)[1], 0)
    ends.wait()


def scan_kernel(length, at_ref, ends_ref, q_ref, out_ref):
    peers = ends_ref.shape[0]
    result, base, left = None, (q_ref[:, 0], q_ref[:, 1]), length
    while left:
        if left & 1:
            result = base if result is None else times(result, base)
        left >>= 1
        if left:
            base = times(base, base)
    state = (jnp.zeros_like(base[0]), jnp.zeros_like(base[1]))
    for peer in range(peers):
        out_ref[peer, :, 0], out_ref[peer, :, 1] = state
        if peer + 1 < peers:
            moved = times(state, result)
            state = (moved[0] + ends_ref[peer, :, 0], moved[1] + ends_ref[peer, :, 1])


def mix_kernel(
    at_ref, incoming_hbm, fresh_hbm, dense_hbm, q_hbm, w_hbm, skip_hbm, mixed_hbm,
    incoming_ref, fresh_ref, dense_ref, q_ref, w_ref, skip_ref, mixed_ref, start_ref, coef_ref, tap_ref, out_ref, sems,
):
    copies = Copies(sems)
    loads = [
        copies.start(a, b)
        for a, b in (
            (q_hbm, q_ref), (w_hbm, w_ref), (skip_hbm, skip_ref), (incoming_hbm, incoming_ref), (fresh_hbm, fresh_ref), (dense_hbm, dense_ref),
        )
    ]
    length, channels = mixed_ref.shape
    tiles = channels // LANES
    chunks = length // CHUNK
    step = min(8, tiles)
    for load in loads[:3]:
        load.wait()
    powers_into(
        coef_ref,
        lambda j: times(row_pair(w_ref, j, tiles), row_pair(q_ref, j, tiles)),
        lambda j: row_pair(q_ref, j, tiles),
        CHUNK,
    )
    tap = skip_ref[...]
    for j in range(NDIM):
        tap = tap + row_pair(w_ref, j, tiles)[0]
    tap_ref[0] = tap

    def one_tap(k, _):
        tap = coef_ref[k, 0, 0]
        for j in range(1, NDIM):
            tap = tap + coef_ref[k, j, 0]
        tap_ref[k + 1] = tap
        return _

    lax.fori_loop(0, CHUNK - 1, one_tap, 0)
    for load in loads[3:]:
        load.wait()

    def one(j, _):
        q = row_pair(q_ref, j, tiles)
        left = CHUNK
        while left > 1:
            q = times(q, q)
            left //= 2
        state = (incoming_ref[j, 0], incoming_ref[j, 1])
        for a in range(chunks):
            start_ref[a, j, 0], start_ref[a, j, 1] = state
            if a + 1 < chunks:
                moved = times(state, q)
                state = (moved[0] + fresh_ref[j, a, 0], moved[1] + fresh_ref[j, a, 1])
        return _

    lax.fori_loop(0, NDIM, one, 0)

    for low in range(0, tiles, step):
        rows = slice(low, low + step)
        for b in range(0, CHUNK, 2):
            total = [[jnp.zeros((step, LANES), f32) for _ in range(chunks)] for _ in range(2)]

            def carry(j, total, b=b, rows=rows):
                total = [list(t) for t in total]
                coefs = [(coef_ref[b + i, j, 0, rows, :], coef_ref[b + i, j, 1, rows, :]) for i in range(2)]
                for a in range(chunks):
                    re, im = start_ref[a, j, 0, rows, :], start_ref[a, j, 1, rows, :]
                    for i in range(2):
                        total[i][a] = total[i][a] + coefs[i][0] * re - coefs[i][1] * im
                return total

            total = lax.fori_loop(0, NDIM, carry, total, unroll=4)
            for s in range(b + 2):
                for i in range(2):
                    if s > b + i:
                        continue
                    tap = tap_ref[b + i - s, rows, :]
                    for a in range(chunks):
                        at = (a * CHUNK + s) * tiles + low
                        total[i][a] = total[i][a] + tap * dense_ref[at : at + step, :]
            for i in range(2):
                for a in range(chunks):
                    at = (a * CHUNK + b + i) * tiles + low
                    out_ref[at : at + step, :] = total[i][a]
        for tile in range(low, low + step):
            lanes = slice(tile * LANES, (tile + 1) * LANES)
            value = out_ref[pl.ds(tile, length, stride=tiles), :]
            mixed_ref[:, lanes] = (value / (1.0 + jnp.exp(-value))).astype(bf16)
        lanes = slice(low * LANES, (low + step) * LANES)
        loads.append(copies.start(mixed_ref.at[:, lanes], mixed_hbm.at[:, lanes]))
    for store in loads[6:]:
        store.wait()


def along(block, axis, step, group):
    count = lax.axis_size(axis)
    pairs = [(i, i - i % group + (i + step) % group) for i in range(count)]
    return lax.ppermute(block, axis, pairs)


def ring_of(layers):
    return [0, *range(1, layers, 2), *reversed(range(2, layers, 2))]


def ring_on(block, members, layers, step):
    ring = ring_of(layers)
    pairs = [
        (ring[k] * members + r, ring[(k + step) % layers] * members + r) for k in range(layers) for r in range(members)
    ]
    return lax.ppermute(block, "ctx", pairs)


def ring_steps(layers):
    return [0, *[(-1) ** (k + 1) * -((k + 1) // 2) for k in range(1, layers)]]


def others(block, axis):
    count = lax.axis_size(axis)
    return [along(block, axis, k, count) for k in range(1, count)]


def part_kernel(members, tp, layers, at_ref, *refs):
    blocks_hbm, refs = refs[: members * tp], refs[members * tp :]
    weights_hbm, refs = refs[:layers], refs[layers:]
    own_hbm, sent_hbm, refs = refs[0], refs[1:members], refs[members:]
    row_ref, weight_ref, own_ref, sent_ref, sems = refs
    copies = Copies(sems)
    subs, length, depth = blocks_hbm[0].shape
    half, ring_at = at_ref[1], at_ref[2]
    loads = [copies.start(weight, weight_ref.at[at]) for at, weight in enumerate(weights_hbm)]
    for away in range(tp):
        other = lax.rem(half + tp - away, tp)
        for k in range(members):
            for sub in range(subs):
                to = row_ref.at[other * subs + sub, k * length : (k + 1) * length, :]
                loads.append(copies.start(blocks_hbm[away * members + k].at[sub], to))
    ring = ring_of(layers)
    blocks = []
    for step in ring_steps(layers):
        at = lax.rem(ring_at + layers + step, layers)
        block = jnp.int32(0)
        for place, layer in enumerate(ring):
            block = jnp.where(at == place, layer, block)
        blocks.append(block)
    for load in loads:
        load.wait()
    stores = []
    for k in [*range(1, members), 0]:
        here = slice(k * length, (k + 1) * length)
        total = mm(row_ref[blocks[0], here, :], weight_ref[0])
        for back in range(1, layers):
            total = total + mm(row_ref[blocks[back], here, :], weight_ref[back])
        if k == 0:
            own_ref[...] = total
            stores.append(copies.start(own_ref, own_hbm))
        else:
            sent_ref[k - 1] = total.astype(bf16)
            stores.append(copies.start(sent_ref.at[k - 1], sent_hbm[k - 1]))
    for store in stores:
        store.wait()


def attend_kernel(members, tp, at_ref, *refs):
    weights_hbm, refs = refs[:members], refs[members:]
    mixed_hbm, refs = refs[:tp], refs[tp:]
    parts_hbm, refs = refs[: members - 1], refs[members - 1 :]
    own_hbm, gain_hbm, affine_hbm, result_hbm = refs[:4]
    weight_ref, mixed_ref, part_ref, own_ref, gain_ref, affine_ref, row_ref, value_ref, result_ref, sems = refs[4:]
    copies = Copies(sems)
    loads = [copies.start(a, mixed_ref.at[k]) for k, a in enumerate(mixed_hbm)]
    loads += [copies.start(gain_hbm, gain_ref), copies.start(affine_hbm, affine_ref)]
    first = len(loads)
    loads += [copies.start(a, weight_ref.at[k]) for k, a in enumerate(weights_hbm)]
    second = len(loads)
    loads += [copies.start(own_hbm, own_ref)] + [copies.start(a, part_ref.at[k]) for k, a in enumerate(parts_hbm)]
    _, layers, depth, head = weight_ref.shape
    _, length, channels = mixed_ref.shape
    place, half = at_ref[0], at_ref[1]
    member, layer = lax.rem(place, members), lax.div(place, members)
    blocks = channels // depth

    for load in loads[:first]:
        load.wait()
    square = jnp.zeros((length, 1), f32)
    for k in range(tp):
        value = mixed_ref[k].astype(f32)
        square = square + jnp.sum(value * value, axis=1, keepdims=True)
    scale = lax.rsqrt(square / (channels * tp) + 1e-06)
    for k in range(tp):
        at = lax.rem(half + tp - k, tp)
        gain = gain_ref[:, pl.ds(pl.multiple_of(at * channels, LANES), channels)]
        normed = (mixed_ref[k].astype(f32) * scale * gain).astype(bf16)
        for block in range(blocks):
            row_ref[at * blocks + block] = normed[:, block * depth : (block + 1) * depth]
    for load in loads[first:second]:
        load.wait()
    z_total = jnp.zeros((length, head), f32)
    for m in range(members):
        for k in range(layers):
            block = lax.rem(layer + layers - k, layers) * members + lax.rem(member + members - m, members)
            z_total = z_total + mm(row_ref[block], weight_ref[m, k])
    queries = (z_total * affine_ref[0:1, :] + affine_ref[1:2, :]).astype(bf16)
    key_rows = (z_total * affine_ref[2:3, :] + affine_ref[3:4, :]).astype(bf16)

    for load in loads[second:]:
        load.wait()
    total = own_ref[...]
    for k in range(members - 1):
        total = total + part_ref[k].astype(f32)
    value_ref[...] = (total / (1.0 + jnp.exp(-total))).astype(bf16)
    row = lax.broadcasted_iota(jnp.int32, (STRETCH, STRETCH), 0)
    col = lax.broadcasted_iota(jnp.int32, (STRETCH, STRETCH), 1)
    for low in range(0, length, STRETCH):
        here = slice(low, low + STRETCH)
        scores = lax.dot_general(
            queries[here], key_rows[here], (((1,), (1,)), ((), ())), preferred_element_type=f32
        ) * (1.0 / head**0.5)
        scores = jnp.where(row >= col, scores, -1e30)
        weights = jnp.exp(scores - jnp.max(scores, axis=1, keepdims=True))
        probabilities = (weights / jnp.sum(weights, axis=1, keepdims=True)).astype(bf16)
        result_ref[here, :] = mm(probabilities, value_ref[here, :]).astype(bf16)
    copies.start(result_ref, result_hbm).wait()


def body(
    tokens, norm_gain, norm_bias, ema_decay, ema_phase, ema_in, ema_out, ema_skip, rms_gain, z_weight, v_weight, qk_affine
):
    length, channels = tokens.shape
    tiles = channels // LANES
    chunks = length // CHUNK
    width = -(-(channels // GROUP) // LANES) * LANES
    place, peers = lax.axis_index("ctx"), lax.axis_size("ctx")
    half, tp = lax.axis_index("tp"), lax.axis_size("tp")
    depth, columns = v_weight.shape
    head = z_weight.shape[1]
    blocks = channels // depth
    members = 4 if peers % 4 == 0 and blocks % 4 == 0 else 1
    layers = peers // members
    subs = blocks // members
    shape, vmem = jax.ShapeDtypeStruct, pltpu.VMEM
    ring_at = sum(jnp.where(place // members == at, k, 0) for k, at in enumerate(ring_of(layers)))
    here = jnp.stack([place, half, ring_at]).astype(jnp.int32)

    running, totals = call(
        sums_kernel,
        [shape((2, length, width), f32), shape((peers, 2, width), f32)],
        [here, tokens],
        [vmem((length, channels), bf16), vmem((2, length, width), f32), vmem((peers, 2, width), f32)],
        8,
    )
    line_z = [z_weight] + [
        lax.ppermute(z_weight, "ctx", [(i, (i + members * k) % peers) for i in range(peers)])
        for k in range(1, layers)
    ]
    totals, line_z, v_weight = lax.optimization_barrier((totals, line_z, v_weight))
    sums = lax.all_to_all(totals, "ctx", 0, 0)
    line_z = jnp.stack(line_z)
    all_z = [line_z] + [along(line_z, "ctx", k, members) for k in range(1, members)]
    all_v = [v_weight]
    if layers > 1:
        all_v.append(ring_on(v_weight, members, layers, 1))
    sums, all_z, all_v = lax.optimization_barrier((sums, all_z, all_v))
    for k in range(2, layers):
        all_v.append(ring_on(all_v[max(k - 2, 0)], members, layers, (-1) ** (k + 1)))

    rows = NDIM * 2 * tiles
    *near, dense, fresh, ends, q, w = call(
        functools.partial(feed_kernel, members),
        [shape((subs, length, depth), bf16)] * members
        + [
            shape((length * tiles, LANES), f32),
            shape((NDIM, chunks, 2, tiles, LANES), f32),
            shape((NDIM, 2, tiles, LANES), f32),
            shape((rows, LANES), f32),
            shape((rows, LANES), f32),
        ],
        [here, tokens, sums, running, norm_gain[None], norm_bias[None], ema_decay, ema_phase, ema_in, ema_out],
        [
            vmem((length, channels), bf16),
            vmem((peers, 2, width), f32),
            vmem((2, length, width), f32),
            vmem((1, channels), f32),
            vmem((1, channels), f32),
            vmem((NDIM, channels), f32),
            vmem((NDIM, channels), f32),
            vmem((NDIM, channels), f32),
            vmem((2, NDIM, channels), f32),
            vmem((blocks, length, depth), bf16),
            vmem((length * tiles, LANES), f32),
            vmem((NDIM, chunks, 2, tiles, LANES), f32),
            vmem((NDIM, 2, tiles, LANES), f32),
            vmem((rows, LANES), f32),
            vmem((rows, LANES), f32),
            vmem((CHUNK + 1, NDIM, 2, tiles, LANES), f32),
        ],
        9 + 3 + blocks + NDIM + 1,
    )
    more = max(1, peers // NDIM)

    def split(a):
        a = a.reshape(NDIM, 2, more, tiles // more, LANES).transpose(0, 2, 1, 3, 4)
        return a.reshape(peers, NDIM * more // peers, 2, tiles // more, LANES)

    def join(a):
        a = a.reshape(NDIM, more, 2, tiles // more, LANES).transpose(0, 2, 1, 3, 4)
        return a.reshape(NDIM, 2, tiles, LANES)

    arrived = lax.all_to_all(split(ends), "ctx", 0, 0)
    near = near[:1] + [along(near[k], "ctx", k, members) for k in range(1, members)]
    far = [along(block, "tp", k, tp) for k in range(1, tp) for block in near]
    my_q = lax.dynamic_index_in_dim(split(q.reshape(NDIM, 2, tiles, LANES)), place, 0, False)
    arrived, all_v, far, my_q = lax.optimization_barrier((arrived, all_v, far, my_q))
    (starts,) = call(functools.partial(scan_kernel, length), [shape(arrived.shape, f32)], [here, arrived, my_q], plain=1)
    incoming = lax.all_to_all(starts, "ctx", 0, 0)

    own, *sent = call(
        functools.partial(part_kernel, members, tp, layers),
        [shape((length, columns), f32)] + [shape((length, columns), bf16)] * (members - 1),
        [here, *near, *far, *all_v],
        [
            vmem((layers, members * length, depth), bf16),
            vmem((layers, depth, columns), bf16),
            vmem((length, columns), f32),
            vmem((max(members - 1, 1), length, columns), bf16),
        ],
        layers + tp * members * subs + members,
    )
    returned = [along(block, "ctx", -k, members) for k, block in enumerate(sent, 1)]
    incoming, own = lax.optimization_barrier((incoming, own))

    (mixed_rows,) = call(
        mix_kernel,
        [shape((length, channels), bf16)],
        [here, join(incoming), fresh, dense, q, w, ema_skip.reshape(tiles, LANES)],
        [
            vmem((NDIM, 2, tiles, LANES), f32),
            vmem((NDIM, chunks, 2, tiles, LANES), f32),
            vmem((length * tiles, LANES), f32),
            vmem((rows, LANES), f32),
            vmem((rows, LANES), f32),
            vmem((tiles, LANES), f32),
            vmem((length, channels), bf16),
            vmem((chunks, NDIM, 2, tiles, LANES), f32),
            vmem((CHUNK, NDIM, 2, tiles, LANES), f32),
            vmem((CHUNK, tiles, LANES), f32),
            vmem((length * tiles, LANES), f32),
        ],
        6 + max(1, tiles // 8),
    )
    mixed_rows, returned = lax.optimization_barrier((mixed_rows, returned))
    (result,) = call(
        functools.partial(attend_kernel, members, tp),
        [shape((length, columns), bf16)],
        [here, *all_z, mixed_rows, *others(mixed_rows, "tp"), *returned, own, rms_gain[None], qk_affine],
        [
            vmem((members, layers, depth, head), bf16),
            vmem((tp, length, channels), bf16),
            vmem((max(members - 1, 1), length, columns), bf16),
            vmem((length, columns), f32),
            vmem((1, tp * channels), f32),
            vmem((4, head), f32),
            vmem((tp * blocks, length, depth), bf16),
            vmem((length, columns), bf16),
            vmem((length, columns), bf16),
        ],
        tp + 2 + 2 * members + 1,
    )
    return result


def solution(mesh):
    in_specs = (
        P("ctx", "tp"),
        P("tp"),
        P("tp"),
        P(None, "tp"),
        P(None, "tp"),
        P(None, "tp"),
        P(None, None, "tp"),
        P("tp"),
        P(),
        P("ctx", "tp"),
        P("ctx", "tp"),
        P(None, "tp"),
    )
    return jax.shard_map(body, mesh=mesh, in_specs=in_specs, out_specs=P("ctx", "tp"), check_vma=False)
```

```python
import functools

import jax
import jax.numpy as jnp
from jax import lax
from jax.experimental import pallas as pl
from jax.experimental.pallas import tpu as pltpu
from jax.sharding import PartitionSpec as P

NDIM = 16
GROUP = 64
STRETCH = 128
CHUNK = 16
LANES = 128
epsilon = 1e-05
f32 = jnp.float32
bf16 = jnp.bfloat16
MIB = 1024 * 1024
VMEM_LIMIT = 64 * MIB
CHEAP = pl.CostEstimate(flops=1, bytes_accessed=1, transcendentals=0)


def call(kernel, outs, inputs, scratch=(), copies=0, plain=0, grant=VMEM_LIMIT):
    hbm, vmem = pl.BlockSpec(memory_space=pltpu.HBM), pl.BlockSpec(memory_space=pltpu.VMEM)
    here = vmem if plain else hbm
    extra = [pltpu.SemaphoreType.DMA((copies,))] if copies else []
    return pl.pallas_call(
        kernel,
        out_shape=outs,
        in_specs=[here] * len(inputs),
        out_specs=[here] * len(outs),
        scratch_shapes=list(scratch) + extra,
        compiler_params=pltpu.CompilerParams(vmem_limit_bytes=grant),
        cost_estimate=CHEAP,
    )(*inputs)


class Copies:
    def __init__(self, sems):
        self.sems, self.used = sems, 0

    def start(self, source, target):
        copy = pltpu.make_async_copy(source, target, self.sems.at[self.used])
        self.used += 1
        copy.start()
        return copy


def pieces(value):
    first = value.astype(bf16)
    rest = value - first.astype(f32)
    second = rest.astype(bf16)
    third = (rest - second.astype(f32)).astype(bf16)
    return first, second, third


def mm(a, b):
    return jnp.dot(a, b, preferred_element_type=f32)


def membership(channels, width, transposed, first):
    shape = (width, channels) if transposed else (channels, width)
    channel = lax.broadcasted_iota(jnp.int32, shape, 1 if transposed else 0) + first
    group = lax.broadcasted_iota(jnp.int32, shape, 0 if transposed else 1)
    return jnp.where(channel // GROUP == group, 1.0, 0.0).astype(bf16)


def group_sums(x, first, width):
    member = membership(x.shape[1], width, False, first)
    square = x.astype(f32) * x.astype(f32)
    high = square.astype(bf16)
    low = (square - high.astype(f32)).astype(bf16)
    return mm(x, member), mm(high, member) + mm(low, member)


def sums_kernel(x_ref, running_ref, total_ref):
    length, channels = x_ref.shape
    width = running_ref.shape[2]
    rows = lax.broadcasted_iota(jnp.int32, (length, length), 0)
    cols = lax.broadcasted_iota(jnp.int32, (length, length), 1)
    lower = jnp.where(rows >= cols, 1.0, 0.0).astype(bf16)
    for at, value in enumerate(group_sums(x_ref[...], 0, width)):
        one, two, three = pieces(value)
        running = mm(lower, one) + mm(lower, two) + mm(lower, three)
        running_ref[at] = running
        for peer in range(total_ref.shape[0]):
            total_ref[peer, at : at + 1, :] = running[length - 1 : length, :]


def times(a, b):
    return a[0] * b[0] - a[1] * b[1], a[0] * b[1] + a[1] * b[0]


def row_pair(ref, j, tiles):
    start = pl.multiple_of(j * (2 * tiles), 2 * tiles)
    return ref[pl.ds(start, tiles), :], ref[pl.ds(start + tiles, tiles), :]


def powers_into(ref, first, factor, count):
    def one(j, _):
        q, now = factor(j), first(j)
        for k in range(count):
            ref[k, j, 0], ref[k, j, 1] = now
            if k + 1 < count:
                now = times(now, q)
        return _

    lax.fori_loop(0, NDIM, one, 0)


def feed_kernel(members, *refs):
    x_hbm, sums_hbm, running_hbm, gain_hbm, bias_hbm, decay_hbm, phase_hbm, in_hbm, out_hbm = refs[:9]
    near_hbm, (dense_hbm, fresh_hbm, end_hbm, q_hbm, w_hbm) = refs[9 : 9 + members], refs[9 + members : 14 + members]
    (
        x_ref, sums_ref, running_ref, gain_ref, bias_ref, decay_ref, phase_ref, in_ref, out_ref,
        normed_ref, dense_ref, fresh_ref, end_ref, q_ref, w_ref, power_ref, sems,
    ) = refs[14 + members :]
    copies = Copies(sems)
    loads = [
        copies.start(a, b)
        for a, b in (
            (decay_hbm, decay_ref), (phase_hbm, phase_ref), (running_hbm, running_ref), (sums_hbm, sums_ref), (x_hbm, x_ref),
            (gain_hbm, gain_ref), (bias_hbm, bias_ref), (in_hbm, in_ref), (out_hbm, out_ref),
        )
    ]
    length, channels = x_ref.shape
    width = running_ref.shape[2]
    tiles = channels // LANES
    chunks = length // CHUNK
    subs, _, depth = near_hbm[0].shape
    me = lax.axis_index("ctx")
    peers = sums_ref.shape[0]

    loads[0].wait()
    loads[1].wait()
    for tile in range(tiles):
        lanes = slice(tile * LANES, (tile + 1) * LANES)
        phase, decay = phase_ref[:, lanes], decay_ref[:, lanes]
        parts = (decay * jnp.cos(phase), decay * jnp.sin(phase))
        for part in range(2):
            q_ref[pl.ds(part * tiles + tile, NDIM, stride=2 * tiles), :] = parts[part]
    stores = [copies.start(q_ref, q_hbm)]
    one, zero = jnp.ones((tiles, LANES), f32), jnp.zeros((tiles, LANES), f32)
    powers_into(power_ref, lambda j: (one, zero), lambda j: row_pair(q_ref, j, tiles), CHUNK + 1)

    for load in loads[2:7]:
        load.wait()
    before = [jnp.zeros((1, width), f32) for _ in range(2)]
    for peer in range(peers):
        earlier = jnp.where(peer < me, 1.0, 0.0)
        for at in range(2):
            before[at] = before[at] + sums_ref[peer, at : at + 1, :] * earlier
    place = lax.broadcasted_iota(jnp.int32, (length, width), 0) + me * length + 1
    counts = place.astype(f32) * GROUP
    average = (before[0] + running_ref[0]) / counts
    spread = jnp.maximum((before[1] + running_ref[1]) / counts - average * average, 0.0)
    scale = lax.rsqrt(spread + epsilon)
    member = membership(channels, width, True, 0)
    average_pieces, scale_pieces = pieces(average), pieces(scale)
    for tile in range(tiles):
        lanes = slice(tile * LANES, (tile + 1) * LANES)
        mine = member[:, lanes]
        average_wide = sum(mm(p, mine) for p in average_pieces)
        scale_wide = sum(mm(p, mine) for p in scale_pieces)
        scaled = (x_ref[:, lanes].astype(f32) - average_wide) * scale_wide
        normed = (scaled * gain_ref[:, lanes] + bias_ref[:, lanes]).astype(bf16)
        part = min(depth, LANES)
        for low in range(0, LANES, part):
            at = tile * LANES + low
            normed_ref[at // depth, :, at % depth : at % depth + part] = normed[:, low : low + part]
        dense_ref[pl.ds(tile, length, stride=tiles), :] = normed.astype(f32)
    for away, ref in enumerate(near_hbm):
        to = lax.rem(me + away, members)
        for sub in range(subs):
            stores.append(copies.start(normed_ref.at[sub * members + to], ref.at[sub]))
    stores.append(copies.start(dense_ref, dense_hbm))

    loads[7].wait()
    loads[8].wait()
    for tile in range(tiles):
        lanes = slice(tile * LANES, (tile + 1) * LANES)
        for part in range(2):
            w_ref[pl.ds(part * tiles + tile, NDIM, stride=2 * tiles), :] = in_ref[:, lanes] * out_ref[part, :, lanes]
    stores.append(copies.start(w_ref, w_hbm))
    step = min(8, tiles)
    first_sem = copies.used

    def send(j):
        return pltpu.make_async_copy(fresh_ref.at[j], fresh_hbm.at[j], sems.at[first_sem + j])

    def one(j, _):
        for low in range(0, tiles, step):
            rows = slice(low, low + step)
            re = [jnp.zeros((step, LANES), f32) for _ in range(chunks)]
            im = [jnp.zeros((step, LANES), f32) for _ in range(chunks)]
            for b in range(CHUNK):
                p_re = power_ref[CHUNK - 1 - b, j, 0, rows, :]
                p_im = power_ref[CHUNK - 1 - b, j, 1, rows, :]
                for a in range(chunks):
                    at = (a * CHUNK + b) * tiles + low
                    value = dense_ref[at : at + step, :]
                    re[a] = re[a] + p_re * value
                    im[a] = im[a] + p_im * value
            q = (power_ref[CHUNK, j, 0, rows, :], power_ref[CHUNK, j, 1, rows, :])
            state = (re[0], im[0])
            for a in range(chunks):
                fresh_ref[j, a, 0, rows, :] = re[a]
                fresh_ref[j, a, 1, rows, :] = im[a]
                if a:
                    moved = times(state, q)
                    state = (moved[0] + re[a], moved[1] + im[a])
            end_ref[j, 0, rows, :], end_ref[j, 1, rows, :] = state
        send(j).start()
        return _

    lax.fori_loop(0, NDIM, one, 0)
    ends = pltpu.make_async_copy(end_ref, end_hbm, sems.at[first_sem + NDIM])
    ends.start()
    for store in stores:
        store.wait()
    lax.fori_loop(0, NDIM, lambda j, c: (send(j).wait(), c)[1], 0)
    ends.wait()


def scan_kernel(length, ends_ref, q_ref, out_ref):
    peers = ends_ref.shape[0]
    result, base, left = None, (q_ref[:, 0], q_ref[:, 1]), length
    while left:
        if left & 1:
            result = base if result is None else times(result, base)
        left >>= 1
        if left:
            base = times(base, base)
    state = (jnp.zeros_like(base[0]), jnp.zeros_like(base[1]))
    for peer in range(peers):
        out_ref[peer, :, 0], out_ref[peer, :, 1] = state
        if peer + 1 < peers:
            moved = times(state, result)
            state = (moved[0] + ends_ref[peer, :, 0], moved[1] + ends_ref[peer, :, 1])


def mix_kernel(
    incoming_hbm, fresh_hbm, dense_hbm, q_hbm, w_hbm, skip_hbm, mixed_hbm,
    incoming_ref, fresh_ref, dense_ref, q_ref, w_ref, skip_ref, mixed_ref, start_ref, coef_ref, tap_ref, out_ref, sems,
):
    copies = Copies(sems)
    loads = [
        copies.start(a, b)
        for a, b in (
            (q_hbm, q_ref), (w_hbm, w_ref), (skip_hbm, skip_ref), (incoming_hbm, incoming_ref), (fresh_hbm, fresh_ref), (dense_hbm, dense_ref),
        )
    ]
    length, channels = mixed_ref.shape
    tiles = channels // LANES
    chunks = length // CHUNK
    step = min(8, tiles)
    for load in loads[:3]:
        load.wait()
    powers_into(
        coef_ref,
        lambda j: times(row_pair(w_ref, j, tiles), row_pair(q_ref, j, tiles)),
        lambda j: row_pair(q_ref, j, tiles),
        CHUNK,
    )
    tap = skip_ref[...]
    for j in range(NDIM):
        tap = tap + row_pair(w_ref, j, tiles)[0]
    tap_ref[0] = tap

    def one_tap(k, _):
        tap = coef_ref[k, 0, 0]
        for j in range(1, NDIM):
            tap = tap + coef_ref[k, j, 0]
        tap_ref[k + 1] = tap
        return _

    lax.fori_loop(0, CHUNK - 1, one_tap, 0)
    for load in loads[3:]:
        load.wait()

    def one(j, _):
        q = row_pair(q_ref, j, tiles)
        left = CHUNK
        while left > 1:
            q = times(q, q)
            left //= 2
        state = (incoming_ref[j, 0], incoming_ref[j, 1])
        for a in range(chunks):
            start_ref[a, j, 0], start_ref[a, j, 1] = state
            if a + 1 < chunks:
                moved = times(state, q)
                state = (moved[0] + fresh_ref[j, a, 0], moved[1] + fresh_ref[j, a, 1])
        return _

    lax.fori_loop(0, NDIM, one, 0)

    for low in range(0, tiles, step):
        rows = slice(low, low + step)
        for b in range(0, CHUNK, 2):
            total = [[jnp.zeros((step, LANES), f32) for _ in range(chunks)] for _ in range(2)]

            def carry(j, total, b=b, rows=rows):
                total = [list(t) for t in total]
                coefs = [(coef_ref[b + i, j, 0, rows, :], coef_ref[b + i, j, 1, rows, :]) for i in range(2)]
                for a in range(chunks):
                    re, im = start_ref[a, j, 0, rows, :], start_ref[a, j, 1, rows, :]
                    for i in range(2):
                        total[i][a] = total[i][a] + coefs[i][0] * re - coefs[i][1] * im
                return total

            total = lax.fori_loop(0, NDIM, carry, total, unroll=4)
            for s in range(b + 2):
                for i in range(2):
                    if s > b + i:
                        continue
                    tap = tap_ref[b + i - s, rows, :]
                    for a in range(chunks):
                        at = (a * CHUNK + s) * tiles + low
                        total[i][a] = total[i][a] + tap * dense_ref[at : at + step, :]
            for i in range(2):
                for a in range(chunks):
                    at = (a * CHUNK + b + i) * tiles + low
                    out_ref[at : at + step, :] = total[i][a]
        for tile in range(low, low + step):
            lanes = slice(tile * LANES, (tile + 1) * LANES)
            value = out_ref[pl.ds(tile, length, stride=tiles), :]
            mixed_ref[:, lanes] = (value / (1.0 + jnp.exp(-value))).astype(bf16)
        lanes = slice(low * LANES, (low + step) * LANES)
        loads.append(copies.start(mixed_ref.at[:, lanes], mixed_hbm.at[:, lanes]))
    for store in loads[6:]:
        store.wait()


def along(block, axis, step, group):
    count = lax.axis_size(axis)
    pairs = [(i, i - i % group + (i + step) % group) for i in range(count)]
    return lax.ppermute(block, axis, pairs)


def ring_of(layers):
    return [0, *range(1, layers, 2), *reversed(range(2, layers, 2))]


def ring_on(block, members, layers, step):
    ring = ring_of(layers)
    pairs = [
        (ring[k] * members + r, ring[(k + step) % layers] * members + r) for k in range(layers) for r in range(members)
    ]
    return lax.ppermute(block, "ctx", pairs)


def ring_steps(layers):
    return [0, *[(-1) ** (k + 1) * -((k + 1) // 2) for k in range(1, layers)]]


def others(block, axis):
    count = lax.axis_size(axis)
    return [along(block, axis, k, count) for k in range(1, count)]


def part_kernel(members, tp, layers, *refs):
    blocks_hbm, refs = refs[: members * tp], refs[members * tp :]
    weights_hbm, refs = refs[:layers], refs[layers:]
    own_hbm, sent_hbm, refs = refs[0], refs[1:members], refs[members:]
    row_ref, weight_ref, own_ref, sent_ref, sems = refs
    copies = Copies(sems)
    subs, length, depth = blocks_hbm[0].shape
    half, place = lax.axis_index("tp"), lax.axis_index("ctx")
    ring_at = sum(jnp.where(place // members == at, k, 0) for k, at in enumerate(ring_of(layers)))
    loads = [copies.start(weight, weight_ref.at[at]) for at, weight in enumerate(weights_hbm)]
    for away in range(tp):
        other = lax.rem(half + tp - away, tp)
        for k in range(members):
            for sub in range(subs):
                to = row_ref.at[other * subs + sub, k * length : (k + 1) * length, :]
                loads.append(copies.start(blocks_hbm[away * members + k].at[sub], to))
    ring = ring_of(layers)
    blocks = []
    for step in ring_steps(layers):
        at = lax.rem(ring_at + layers + step, layers)
        block = jnp.int32(0)
        for place, layer in enumerate(ring):
            block = jnp.where(at == place, layer, block)
        blocks.append(block)
    for load in loads:
        load.wait()
    stores = []
    for k in [*range(1, members), 0]:
        here = slice(k * length, (k + 1) * length)
        total = mm(row_ref[blocks[0], here, :], weight_ref[0])
        for back in range(1, layers):
            total = total + mm(row_ref[blocks[back], here, :], weight_ref[back])
        if k == 0:
            own_ref[...] = total
            stores.append(copies.start(own_ref, own_hbm))
        else:
            sent_ref[k - 1] = total.astype(bf16)
            stores.append(copies.start(sent_ref.at[k - 1], sent_hbm[k - 1]))
    for store in stores:
        store.wait()


def attend_kernel(members, tp, *refs):
    weights_hbm, refs = refs[:members], refs[members:]
    mixed_hbm, refs = refs[:tp], refs[tp:]
    parts_hbm, refs = refs[: members - 1], refs[members - 1 :]
    own_hbm, gain_hbm, affine_hbm, result_hbm = refs[:4]
    weight_ref, mixed_ref, part_ref, own_ref, gain_ref, affine_ref, row_ref, value_ref, result_ref, sems = refs[4:]
    copies = Copies(sems)
    loads = [copies.start(a, mixed_ref.at[k]) for k, a in enumerate(mixed_hbm)]
    loads += [copies.start(gain_hbm, gain_ref), copies.start(affine_hbm, affine_ref)]
    first = len(loads)
    loads += [copies.start(a, weight_ref.at[k]) for k, a in enumerate(weights_hbm)]
    second = len(loads)
    loads += [copies.start(own_hbm, own_ref)] + [copies.start(a, part_ref.at[k]) for k, a in enumerate(parts_hbm)]
    _, layers, depth, head = weight_ref.shape
    _, length, channels = mixed_ref.shape
    place, half = lax.axis_index("ctx"), lax.axis_index("tp")
    member, layer = lax.rem(place, members), lax.div(place, members)
    blocks = channels // depth

    for load in loads[:first]:
        load.wait()
    square = jnp.zeros((length, 1), f32)
    for k in range(tp):
        value = mixed_ref[k].astype(f32)
        square = square + jnp.sum(value * value, axis=1, keepdims=True)
    scale = lax.rsqrt(square / (channels * tp) + 1e-06)
    for k in range(tp):
        at = lax.rem(half + tp - k, tp)
        gain = gain_ref[:, pl.ds(pl.multiple_of(at * channels, LANES), channels)]
        normed = (mixed_ref[k].astype(f32) * scale * gain).astype(bf16)
        for block in range(blocks):
            row_ref[at * blocks + block] = normed[:, block * depth : (block + 1) * depth]
    for load in loads[first:second]:
        load.wait()
    z_total = jnp.zeros((length, head), f32)
    for m in range(members):
        for k in range(layers):
            block = lax.rem(layer + layers - k, layers) * members + lax.rem(member + members - m, members)
            z_total = z_total + mm(row_ref[block], weight_ref[m, k])
    queries = (z_total * affine_ref[0:1, :] + affine_ref[1:2, :]).astype(bf16)
    key_rows = (z_total * affine_ref[2:3, :] + affine_ref[3:4, :]).astype(bf16)

    for load in loads[second:]:
        load.wait()
    total = own_ref[...]
    for k in range(members - 1):
        total = total + part_ref[k].astype(f32)
    value_ref[...] = (total / (1.0 + jnp.exp(-total))).astype(bf16)
    row = lax.broadcasted_iota(jnp.int32, (STRETCH, STRETCH), 0)
    col = lax.broadcasted_iota(jnp.int32, (STRETCH, STRETCH), 1)
    for low in range(0, length, STRETCH):
        here = slice(low, low + STRETCH)
        scores = lax.dot_general(
            queries[here], key_rows[here], (((1,), (1,)), ((), ())), preferred_element_type=f32
        ) * (1.0 / head**0.5)
        scores = jnp.where(row >= col, scores, -1e30)
        weights = jnp.exp(scores - jnp.max(scores, axis=1, keepdims=True))
        probabilities = (weights / jnp.sum(weights, axis=1, keepdims=True)).astype(bf16)
        result_ref[:] = mm(probabilities, value_ref[:]).astype(bf16)
    copies.start(result_ref, result_hbm).wait()


def body(
    tokens, norm_gain, norm_bias, ema_decay, ema_phase, ema_in, ema_out, ema_skip, rms_gain, z_weight, v_weight, qk_affine
):
    length, channels = tokens.shape
    tiles = channels // LANES
    chunks = length // CHUNK
    width = -(-(channels // GROUP) // LANES) * LANES
    place, peers = lax.axis_index("ctx"), lax.axis_size("ctx")
    half, tp = lax.axis_index("tp"), lax.axis_size("tp")
    depth, columns = v_weight.shape
    head = z_weight.shape[1]
    blocks = channels // depth
    members = 4 if peers % 4 == 0 and blocks % 4 == 0 else 1
    layers = peers // members
    subs = blocks // members
    shape, vmem = jax.ShapeDtypeStruct, pltpu.VMEM

    running, totals = call(
        sums_kernel,
        [shape((2, length, width), f32), shape((peers, 2, width), f32)],
        [tokens],
        plain=1,
        grant=16 * MIB,
    )
    all_v = [v_weight]
    if layers > 1:
        all_v.append(ring_on(v_weight, members, layers, 1))
    sums = lax.all_to_all(totals, "ctx", 0, 0)
    line_z = [z_weight] + [
        lax.ppermute(z_weight, "ctx", [(i, (i + members * k) % peers) for i in range(peers)])
        for k in range(1, layers)
    ]
    line_z = jnp.stack(line_z)
    sums, all_v, line_z = lax.optimization_barrier((sums, all_v, line_z))
    if layers > 2:
        all_v.append(ring_on(v_weight, members, layers, -1))
    all_z = [line_z] + [along(line_z, "ctx", k, members) for k in range(1, members)]

    rows = NDIM * 2 * tiles
    *near, dense, fresh, ends, q, w = call(
        functools.partial(feed_kernel, members),
        [shape((subs, length, depth), bf16)] * members
        + [
            shape((length * tiles, LANES), f32),
            shape((NDIM, chunks, 2, tiles, LANES), f32),
            shape((NDIM, 2, tiles, LANES), f32),
            shape((rows, LANES), f32),
            shape((rows, LANES), f32),
        ],
        [tokens, sums, running, norm_gain[None], norm_bias[None], ema_decay, ema_phase, ema_in, ema_out],
        [
            vmem((length, channels), bf16),
            vmem((peers, 2, width), f32),
            vmem((2, length, width), f32),
            vmem((1, channels), f32),
            vmem((1, channels), f32),
            vmem((NDIM, channels), f32),
            vmem((NDIM, channels), f32),
            vmem((NDIM, channels), f32),
            vmem((2, NDIM, channels), f32),
            vmem((blocks, length, depth), bf16),
            vmem((length * tiles, LANES), f32),
            vmem((NDIM, chunks, 2, tiles, LANES), f32),
            vmem((NDIM, 2, tiles, LANES), f32),
            vmem((rows, LANES), f32),
            vmem((rows, LANES), f32),
            vmem((CHUNK + 1, NDIM, 2, tiles, LANES), f32),
        ],
        9 + 3 + blocks + NDIM + 1,
    )
    more = max(1, peers // NDIM)

    def split(a):
        a = a.reshape(NDIM, 2, more, tiles // more, LANES).transpose(0, 2, 1, 3, 4)
        return a.reshape(peers, NDIM * more // peers, 2, tiles // more, LANES)

    def join(a):
        a = a.reshape(NDIM, more, 2, tiles // more, LANES).transpose(0, 2, 1, 3, 4)
        return a.reshape(NDIM, 2, tiles, LANES)

    arrived = lax.all_to_all(split(ends), "ctx", 0, 0)
    near, all_z = lax.optimization_barrier((near, all_z))
    near = near[:1] + [along(near[k], "ctx", k, members) for k in range(1, members)]
    near, all_v[1] = lax.optimization_barrier((near, all_v[1]))
    for k in range(3, layers):
        all_v.append(ring_on(all_v[k - 2], members, layers, (-1) ** (k + 1)))
    far = [along(block, "tp", k, tp) for k in range(1, tp) for block in near]
    my_q = lax.dynamic_index_in_dim(split(q.reshape(NDIM, 2, tiles, LANES)), place, 0, False)
    arrived, far, my_q, all_v[2] = lax.optimization_barrier((arrived, far, my_q, all_v[2]))
    (starts,) = call(functools.partial(scan_kernel, length), [shape(arrived.shape, f32)], [arrived, my_q], plain=1, grant=16 * MIB)
    incoming = lax.all_to_all(starts, "ctx", 0, 0)

    own, *sent = call(
        functools.partial(part_kernel, members, tp, layers),
        [shape((length, columns), f32)] + [shape((length, columns), bf16)] * (members - 1),
        [*near, *far, *all_v],
        [
            vmem((layers, members * length, depth), bf16),
            vmem((layers, depth, columns), bf16),
            vmem((length, columns), f32),
            vmem((max(members - 1, 1), length, columns), bf16),
        ],
        layers + tp * members * subs + members,
    )
    returned = [along(block, "ctx", -k, members) for k, block in enumerate(sent, 1)]
    incoming, own = lax.optimization_barrier((incoming, own))

    (mixed_rows,) = call(
        mix_kernel,
        [shape((length, channels), bf16)],
        [join(incoming), fresh, dense, q, w, ema_skip.reshape(tiles, LANES)],
        [
            vmem((NDIM, 2, tiles, LANES), f32),
            vmem((NDIM, chunks, 2, tiles, LANES), f32),
            vmem((length * tiles, LANES), f32),
            vmem((rows, LANES), f32),
            vmem((rows, LANES), f32),
            vmem((tiles, LANES), f32),
            vmem((length, channels), bf16),
            vmem((chunks, NDIM, 2, tiles, LANES), f32),
            vmem((CHUNK, NDIM, 2, tiles, LANES), f32),
            vmem((CHUNK, tiles, LANES), f32),
            vmem((length * tiles, LANES), f32),
        ],
        6 + max(1, tiles // 8),
    )
    mixed_rows, returned = lax.optimization_barrier((mixed_rows, returned))
    apart = others(mixed_rows, "tp")
    (result,) = call(
        functools.partial(attend_kernel, members, tp),
        [shape((length, columns), bf16)],
        [*all_z, mixed_rows, *apart, *returned, own, rms_gain[None], qk_affine],
        [
            vmem((members, layers, depth, head), bf16),
            vmem((tp, length, channels), bf16),
            vmem((max(members - 1, 1), length, columns), bf16),
            vmem((length, columns), f32),
            vmem((1, tp * channels), f32),
            vmem((4, head), f32),
            vmem((tp * blocks, length, depth), bf16),
            vmem((length, columns), bf16),
            vmem((length, columns), bf16),
        ],
        tp + 2 + 2 * members + 1,
    )
    return result


def solution(mesh):
    in_specs = (
        P("ctx", "tp"),
        P("tp"),
        P("tp"),
        P(None, "tp"),
        P(None, "tp"),
        P(None, "tp"),
        P(None, None, "tp"),
        P("tp"),
        P(),
        P("ctx", "tp"),
        P("ctx", "tp"),
        P(None, "tp"),
    )
    return jax.shard_map(body, mesh=mesh, in_specs=in_specs, out_specs=P("ctx", "tp"), check_vma=False)
```

```python
import functools

import jax
import jax.numpy as jnp
from jax import lax
from jax.experimental import pallas as pl
from jax.experimental.pallas import tpu as pltpu
from jax.sharding import PartitionSpec as P

NDIM = 16
GROUP = 64
STRETCH = 128
CHUNK = 16
LANES = 128
epsilon = 1e-05
f32 = jnp.float32
bf16 = jnp.bfloat16
MIB = 1024 * 1024
VMEM_LIMIT = 64 * MIB
CHEAP = pl.CostEstimate(flops=1, bytes_accessed=1, transcendentals=0)


def call(kernel, outs, inputs, scratch=(), copies=0, plain=0, grant=VMEM_LIMIT):
    hbm, vmem = pl.BlockSpec(memory_space=pltpu.HBM), pl.BlockSpec(memory_space=pltpu.VMEM)
    here = vmem if plain else hbm
    extra = [pltpu.SemaphoreType.DMA((copies,))] if copies else []
    return pl.pallas_call(
        kernel,
        out_shape=outs,
        in_specs=[here] * len(inputs),
        out_specs=[here] * len(outs),
        scratch_shapes=list(scratch) + extra,
        compiler_params=pltpu.CompilerParams(vmem_limit_bytes=grant),
        cost_estimate=CHEAP,
    )(*inputs)


class Copies:
    def __init__(self, sems):
        self.sems, self.used = sems, 0

    def start(self, source, target):
        copy = pltpu.make_async_copy(source, target, self.sems.at[self.used])
        self.used += 1
        copy.start()
        return copy


def pieces(value):
    first = value.astype(bf16)
    rest = value - first.astype(f32)
    second = rest.astype(bf16)
    third = (rest - second.astype(f32)).astype(bf16)
    return first, second, third


def mm(a, b):
    return jnp.dot(a, b, preferred_element_type=f32)


def membership(channels, width, transposed, first):
    shape = (width, channels) if transposed else (channels, width)
    channel = lax.broadcasted_iota(jnp.int32, shape, 1 if transposed else 0) + first
    group = lax.broadcasted_iota(jnp.int32, shape, 0 if transposed else 1)
    return jnp.where(channel // GROUP == group, 1.0, 0.0).astype(bf16)


def group_sums(x, first, width):
    member = membership(x.shape[1], width, False, first)
    square = x.astype(f32) * x.astype(f32)
    high = square.astype(bf16)
    low = (square - high.astype(f32)).astype(bf16)
    return mm(x, member), mm(high, member) + mm(low, member)


def sums_kernel(x_ref, running_ref, total_ref):
    length, channels = x_ref.shape
    width = running_ref.shape[2]
    rows = lax.broadcasted_iota(jnp.int32, (length, length), 0)
    cols = lax.broadcasted_iota(jnp.int32, (length, length), 1)
    lower = jnp.where(rows >= cols, 1.0, 0.0).astype(bf16)
    for at, value in enumerate(group_sums(x_ref[...], 0, width)):
        one, two, three = pieces(value)
        running = mm(lower, one) + mm(lower, two) + mm(lower, three)
        running_ref[at] = running
        for peer in range(total_ref.shape[0]):
            total_ref[peer, at : at + 1, :] = running[length - 1 : length, :]


def times(a, b):
    return a[0] * b[0] - a[1] * b[1], a[0] * b[1] + a[1] * b[0]


def row_pair(ref, j, tiles):
    start = pl.multiple_of(j * (2 * tiles), 2 * tiles)
    return ref[pl.ds(start, tiles), :], ref[pl.ds(start + tiles, tiles), :]


def powers_into(ref, first, factor, count):
    def one(j, _):
        q, now = factor(j), first(j)
        for k in range(count):
            ref[k, j, 0], ref[k, j, 1] = now
            if k + 1 < count:
                now = times(now, q)
        return _

    lax.fori_loop(0, NDIM, one, 0)


def feed_kernel(members, *refs):
    x_hbm, sums_hbm, running_hbm, gain_hbm, bias_hbm, decay_hbm, phase_hbm, in_hbm, out_hbm = refs[:9]
    near_hbm, (dense_hbm, fresh_hbm, end_hbm, q_hbm, w_hbm) = refs[9 : 9 + members], refs[9 + members : 14 + members]
    (
        x_ref, sums_ref, running_ref, gain_ref, bias_ref, decay_ref, phase_ref, in_ref, out_ref,
        normed_ref, dense_ref, fresh_ref, end_ref, q_ref, w_ref, power_ref, sems,
    ) = refs[14 + members :]
    copies = Copies(sems)
    loads = [
        copies.start(a, b)
        for a, b in (
            (decay_hbm, decay_ref), (phase_hbm, phase_ref), (running_hbm, running_ref), (sums_hbm, sums_ref), (x_hbm, x_ref),
            (gain_hbm, gain_ref), (bias_hbm, bias_ref), (in_hbm, in_ref), (out_hbm, out_ref),
        )
    ]
    length, channels = x_ref.shape
    width = running_ref.shape[2]
    tiles = channels // LANES
    chunks = length // CHUNK
    subs, _, depth = near_hbm[0].shape
    me = lax.axis_index("ctx")
    peers = sums_ref.shape[0]

    loads[0].wait()
    loads[1].wait()
    for tile in range(tiles):
        lanes = slice(tile * LANES, (tile + 1) * LANES)
        phase, decay = phase_ref[:, lanes], decay_ref[:, lanes]
        parts = (decay * jnp.cos(phase), decay * jnp.sin(phase))
        for part in range(2):
            q_ref[pl.ds(part * tiles + tile, NDIM, stride=2 * tiles), :] = parts[part]
    stores = [copies.start(q_ref, q_hbm)]
    one, zero = jnp.ones((tiles, LANES), f32), jnp.zeros((tiles, LANES), f32)
    powers_into(power_ref, lambda j: (one, zero), lambda j: row_pair(q_ref, j, tiles), CHUNK + 1)

    for load in loads[2:7]:
        load.wait()
    before = [jnp.zeros((1, width), f32) for _ in range(2)]
    for peer in range(peers):
        earlier = jnp.where(peer < me, 1.0, 0.0)
        for at in range(2):
            before[at] = before[at] + sums_ref[peer, at : at + 1, :] * earlier
    place = lax.broadcasted_iota(jnp.int32, (length, width), 0) + me * length + 1
    counts = place.astype(f32) * GROUP
    average = (before[0] + running_ref[0]) / counts
    spread = jnp.maximum((before[1] + running_ref[1]) / counts - average * average, 0.0)
    scale = lax.rsqrt(spread + epsilon)
    member = membership(channels, width, True, 0)
    average_pieces, scale_pieces = pieces(average), pieces(scale)
    for tile in range(tiles):
        lanes = slice(tile * LANES, (tile + 1) * LANES)
        mine = member[:, lanes]
        average_wide = sum(mm(p, mine) for p in average_pieces)
        scale_wide = sum(mm(p, mine) for p in scale_pieces)
        scaled = (x_ref[:, lanes].astype(f32) - average_wide) * scale_wide
        normed = (scaled * gain_ref[:, lanes] + bias_ref[:, lanes]).astype(bf16)
        part = min(depth, LANES)
        for low in range(0, LANES, part):
            at = tile * LANES + low
            normed_ref[at // depth, :, at % depth : at % depth + part] = normed[:, low : low + part]
        dense_ref[pl.ds(tile, length, stride=tiles), :] = normed.astype(f32)
    for away, ref in enumerate(near_hbm):
        to = lax.rem(me + away, members)
        for sub in range(subs):
            stores.append(copies.start(normed_ref.at[sub * members + to], ref.at[sub]))
    stores.append(copies.start(dense_ref, dense_hbm))

    loads[7].wait()
    loads[8].wait()
    for tile in range(tiles):
        lanes = slice(tile * LANES, (tile + 1) * LANES)
        for part in range(2):
            w_ref[pl.ds(part * tiles + tile, NDIM, stride=2 * tiles), :] = in_ref[:, lanes] * out_ref[part, :, lanes]
    stores.append(copies.start(w_ref, w_hbm))
    step = min(8, tiles)
    first_sem = copies.used

    def send(j):
        return pltpu.make_async_copy(fresh_ref.at[j], fresh_hbm.at[j], sems.at[first_sem + j])

    def one(j, _):
        for low in range(0, tiles, step):
            rows = slice(low, low + step)
            re = [jnp.zeros((step, LANES), f32) for _ in range(chunks)]
            im = [jnp.zeros((step, LANES), f32) for _ in range(chunks)]
            for b in range(CHUNK):
                p_re = power_ref[CHUNK - 1 - b, j, 0, rows, :]
                p_im = power_ref[CHUNK - 1 - b, j, 1, rows, :]
                for a in range(chunks):
                    at = (a * CHUNK + b) * tiles + low
                    value = dense_ref[at : at + step, :]
                    re[a] = re[a] + p_re * value
                    im[a] = im[a] + p_im * value
            q = (power_ref[CHUNK, j, 0, rows, :], power_ref[CHUNK, j, 1, rows, :])
            state = (re[0], im[0])
            for a in range(chunks):
                fresh_ref[j, a, 0, rows, :] = re[a]
                fresh_ref[j, a, 1, rows, :] = im[a]
                if a:
                    moved = times(state, q)
                    state = (moved[0] + re[a], moved[1] + im[a])
            end_ref[j, 0, rows, :], end_ref[j, 1, rows, :] = state
        send(j).start()
        return _

    lax.fori_loop(0, NDIM, one, 0)
    ends = pltpu.make_async_copy(end_ref, end_hbm, sems.at[first_sem + NDIM])
    ends.start()
    for store in stores:
        store.wait()
    lax.fori_loop(0, NDIM, lambda j, c: (send(j).wait(), c)[1], 0)
    ends.wait()


def scan_kernel(length, ends_ref, q_ref, out_ref):
    peers = ends_ref.shape[0]
    result, base, left = None, (q_ref[:, 0], q_ref[:, 1]), length
    while left:
        if left & 1:
            result = base if result is None else times(result, base)
        left >>= 1
        if left:
            base = times(base, base)
    state = (jnp.zeros_like(base[0]), jnp.zeros_like(base[1]))
    for peer in range(peers):
        out_ref[peer, :, 0], out_ref[peer, :, 1] = state
        if peer + 1 < peers:
            moved = times(state, result)
            state = (moved[0] + ends_ref[peer, :, 0], moved[1] + ends_ref[peer, :, 1])


def mix_kernel(
    incoming_hbm, fresh_hbm, dense_hbm, q_hbm, w_hbm, skip_hbm, mixed_hbm,
    incoming_ref, fresh_ref, dense_ref, q_ref, w_ref, skip_ref, mixed_ref, start_ref, coef_ref, tap_ref, out_ref, sems,
):
    copies = Copies(sems)
    loads = [
        copies.start(a, b)
        for a, b in (
            (q_hbm, q_ref), (w_hbm, w_ref), (skip_hbm, skip_ref), (incoming_hbm, incoming_ref), (fresh_hbm, fresh_ref), (dense_hbm, dense_ref),
        )
    ]
    length, channels = mixed_ref.shape
    tiles = channels // LANES
    chunks = length // CHUNK
    step = min(8, tiles)
    for load in loads[:3]:
        load.wait()
    powers_into(
        coef_ref,
        lambda j: times(row_pair(w_ref, j, tiles), row_pair(q_ref, j, tiles)),
        lambda j: row_pair(q_ref, j, tiles),
        CHUNK,
    )
    tap = skip_ref[...]
    for j in range(NDIM):
        tap = tap + row_pair(w_ref, j, tiles)[0]
    tap_ref[0] = tap

    def one_tap(k, _):
        tap = coef_ref[k, 0, 0]
        for j in range(1, NDIM):
            tap = tap + coef_ref[k, j, 0]
        tap_ref[k + 1] = tap
        return _

    lax.fori_loop(0, CHUNK - 1, one_tap, 0)
    for load in loads[3:]:
        load.wait()

    def one(j, _):
        q = row_pair(q_ref, j, tiles)
        left = CHUNK
        while left > 1:
            q = times(q, q)
            left //= 2
        state = (incoming_ref[j, 0], incoming_ref[j, 1])
        for a in range(chunks):
            start_ref[a, j, 0], start_ref[a, j, 1] = state
            if a + 1 < chunks:
                moved = times(state, q)
                state = (moved[0] + fresh_ref[j, a, 0], moved[1] + fresh_ref[j, a, 1])
        return _

    lax.fori_loop(0, NDIM, one, 0)

    for low in range(0, tiles, step):
        rows = slice(low, low + step)
        for b in range(0, CHUNK, 2):
            total = [[jnp.zeros((step, LANES), f32) for _ in range(chunks)] for _ in range(2)]

            def carry(j, total, b=b, rows=rows):
                total = [list(t) for t in total]
                coefs = [(coef_ref[b + i, j, 0, rows, :], coef_ref[b + i, j, 1, rows, :]) for i in range(2)]
                for a in range(chunks):
                    re, im = start_ref[a, j, 0, rows, :], start_ref[a, j, 1, rows, :]
                    for i in range(2):
                        total[i][a] = total[i][a] + coefs[i][0] * re - coefs[i][1] * im
                return total

            total = lax.fori_loop(0, NDIM, carry, total, unroll=4)
            for s in range(b + 2):
                for i in range(2):
                    if s > b + i:
                        continue
                    tap = tap_ref[b + i - s, rows, :]
                    for a in range(chunks):
                        at = (a * CHUNK + s) * tiles + low
                        total[i][a] = total[i][a] + tap * dense_ref[at : at + step, :]
            for i in range(2):
                for a in range(chunks):
                    at = (a * CHUNK + b + i) * tiles + low
                    out_ref[at : at + step, :] = total[i][a]
        for tile in range(low, low + step):
            lanes = slice(tile * LANES, (tile + 1) * LANES)
            value = out_ref[pl.ds(tile, length, stride=tiles), :]
            mixed_ref[:, lanes] = (value / (1.0 + jnp.exp(-value))).astype(bf16)
        lanes = slice(low * LANES, (low + step) * LANES)
        loads.append(copies.start(mixed_ref.at[:, lanes], mixed_hbm.at[:, lanes]))
    for store in loads[6:]:
        store.wait()


def along(block, axis, step, group):
    count = lax.axis_size(axis)
    pairs = [(i, i - i % group + (i + step) % group) for i in range(count)]
    return lax.ppermute(block, axis, pairs)


def ring_of(layers):
    return [0, *range(1, layers, 2), *reversed(range(2, layers, 2))]


def ring_on(block, members, layers, step):
    ring = ring_of(layers)
    pairs = [
        (ring[k] * members + r, ring[(k + step) % layers] * members + r) for k in range(layers) for r in range(members)
    ]
    return lax.ppermute(block, "ctx", pairs)


def ring_steps(layers):
    return [0, *[(-1) ** (k + 1) * -((k + 1) // 2) for k in range(1, layers)]]


def others(block, axis):
    count = lax.axis_size(axis)
    return [along(block, axis, k, count) for k in range(1, count)]


def part_kernel(members, tp, layers, *refs):
    blocks_hbm, refs = refs[: members * tp], refs[members * tp :]
    weights_hbm, refs = refs[:layers], refs[layers:]
    own_hbm, sent_hbm, refs = refs[0], refs[1:members], refs[members:]
    row_ref, weight_ref, own_ref, sent_ref, sems = refs
    copies = Copies(sems)
    subs, length, depth = blocks_hbm[0].shape
    half, place = lax.axis_index("tp"), lax.axis_index("ctx")
    ring_at = sum(jnp.where(place // members == at, k, 0) for k, at in enumerate(ring_of(layers)))
    loads = [copies.start(weight, weight_ref.at[at]) for at, weight in enumerate(weights_hbm)]
    for away in range(tp):
        other = lax.rem(half + tp - away, tp)
        for k in range(members):
            for sub in range(subs):
                to = row_ref.at[other * subs + sub, k * length : (k + 1) * length, :]
                loads.append(copies.start(blocks_hbm[away * members + k].at[sub], to))
    ring = ring_of(layers)
    blocks = []
    for step in ring_steps(layers):
        at = lax.rem(ring_at + layers + step, layers)
        block = jnp.int32(0)
        for place, layer in enumerate(ring):
            block = jnp.where(at == place, layer, block)
        blocks.append(block)
    for load in loads:
        load.wait()
    stores = []
    for k in [*range(1, members), 0]:
        here = slice(k * length, (k + 1) * length)
        total = mm(row_ref[blocks[0], here, :], weight_ref[0])
        for back in range(1, layers):
            total = total + mm(row_ref[blocks[back], here, :], weight_ref[back])
        if k == 0:
            own_ref[...] = total
            stores.append(copies.start(own_ref, own_hbm))
        else:
            sent_ref[k - 1] = total.astype(bf16)
            stores.append(copies.start(sent_ref.at[k - 1], sent_hbm[k - 1]))
    for store in stores:
        store.wait()


def attend_kernel(members, tp, *refs):
    weights_hbm, refs = refs[:members], refs[members:]
    mixed_hbm, refs = refs[:tp], refs[tp:]
    parts_hbm, refs = refs[: members - 1], refs[members - 1 :]
    own_hbm, gain_hbm, affine_hbm, result_hbm = refs[:4]
    weight_ref, mixed_ref, part_ref, own_ref, gain_ref, affine_ref, row_ref, value_ref, result_ref, sems = refs[4:]
    copies = Copies(sems)
    loads = [copies.start(a, mixed_ref.at[k]) for k, a in enumerate(mixed_hbm)]
    loads += [copies.start(gain_hbm, gain_ref), copies.start(affine_hbm, affine_ref)]
    first = len(loads)
    loads += [copies.start(a, weight_ref.at[k]) for k, a in enumerate(weights_hbm)]
    second = len(loads)
    loads += [copies.start(own_hbm, own_ref)] + [copies.start(a, part_ref.at[k]) for k, a in enumerate(parts_hbm)]
    _, layers, depth, head = weight_ref.shape
    _, length, channels = mixed_ref.shape
    place, half = lax.axis_index("ctx"), lax.axis_index("tp")
    member, layer = lax.rem(place, members), lax.div(place, members)
    blocks = channels // depth

    for load in loads[:first]:
        load.wait()
    square = jnp.zeros((length, 1), f32)
    for k in range(tp):
        value = mixed_ref[k].astype(f32)
        square = square + jnp.sum(value * value, axis=1, keepdims=True)
    scale = lax.rsqrt(square / (channels * tp) + 1e-06)
    for k in range(tp):
        at = lax.rem(half + tp - k, tp)
        gain = gain_ref[:, pl.ds(pl.multiple_of(at * channels, LANES), channels)]
        normed = (mixed_ref[k].astype(f32) * scale * gain).astype(bf16)
        for block in range(blocks):
            row_ref[at * blocks + block] = normed[:, block * depth : (block + 1) * depth]
    for load in loads[first:second]:
        load.wait()
    z_total = jnp.zeros((length, head), f32)
    for m in range(members):
        for k in range(layers):
            block = lax.rem(layer + layers - k, layers) * members + lax.rem(member + members - m, members)
            z_total = z_total + mm(row_ref[block], weight_ref[m, k])
    queries = (z_total * affine_ref[0:1, :] + affine_ref[1:2, :]).astype(bf16)
    key_rows = (z_total * affine_ref[2:3, :] + affine_ref[3:4, :]).astype(bf16)

    for load in loads[second:]:
        load.wait()
    total = own_ref[...]
    for k in range(members - 1):
        total = total + part_ref[k].astype(f32)
    value_ref[...] = (total / (1.0 + jnp.exp(-total))).astype(bf16)
    row = lax.broadcasted_iota(jnp.int32, (STRETCH, STRETCH), 0)
    col = lax.broadcasted_iota(jnp.int32, (STRETCH, STRETCH), 1)
    for low in range(0, length, STRETCH):
        here = slice(low, low + STRETCH)
        scores = lax.dot_general(
            queries[here], key_rows[here], (((1,), (1,)), ((), ())), preferred_element_type=f32
        ) * (1.0 / head**0.5)
        scores = jnp.where(row >= col, scores, -1e30)
        weights = jnp.exp(scores - jnp.max(scores, axis=1, keepdims=True))
        probabilities = (weights / jnp.sum(weights, axis=1, keepdims=True)).astype(bf16)
        result_ref[:] = mm(probabilities, value_ref[:]).astype(bf16)
    copies.start(result_ref, result_hbm).wait()


def body(
    tokens, norm_gain, norm_bias, ema_decay, ema_phase, ema_in, ema_out, ema_skip, rms_gain, z_weight, v_weight, qk_affine
):
    length, channels = tokens.shape
    tiles = channels // LANES
    chunks = length // CHUNK
    width = -(-(channels // GROUP) // LANES) * LANES
    place, peers = lax.axis_index("ctx"), lax.axis_size("ctx")
    half, tp = lax.axis_index("tp"), lax.axis_size("tp")
    depth, columns = v_weight.shape
    head = z_weight.shape[1]
    blocks = channels // depth
    members = 4 if peers % 4 == 0 and blocks % 4 == 0 else 1
    layers = peers // members
    subs = blocks // members
    shape, vmem = jax.ShapeDtypeStruct, pltpu.VMEM

    running, totals = call(
        sums_kernel,
        [shape((2, length, width), f32), shape((peers, 2, width), f32)],
        [tokens],
        plain=1,
        grant=16 * MIB,
    )
    sums = lax.all_to_all(totals, "ctx", 0, 0)
    line_z = [z_weight] + [
        lax.ppermute(z_weight, "ctx", [(i, (i + members * k) % peers) for i in range(peers)])
        for k in range(1, layers)
    ]
    line_z = jnp.stack(line_z)
    sums, v_weight, line_z = lax.optimization_barrier((sums, v_weight, line_z))
    all_v = [v_weight] + [ring_on(v_weight, members, layers, (-1) ** (k + 1)) for k in range(1, min(layers, 3))]
    all_z = [line_z] + [along(line_z, "ctx", k, members) for k in range(1, members)]

    rows = NDIM * 2 * tiles
    *near, dense, fresh, ends, q, w = call(
        functools.partial(feed_kernel, members),
        [shape((subs, length, depth), bf16)] * members
        + [
            shape((length * tiles, LANES), f32),
            shape((NDIM, chunks, 2, tiles, LANES), f32),
            shape((NDIM, 2, tiles, LANES), f32),
            shape((rows, LANES), f32),
            shape((rows, LANES), f32),
        ],
        [tokens, sums, running, norm_gain[None], norm_bias[None], ema_decay, ema_phase, ema_in, ema_out],
        [
            vmem((length, channels), bf16),
            vmem((peers, 2, width), f32),
            vmem((2, length, width), f32),
            vmem((1, channels), f32),
            vmem((1, channels), f32),
            vmem((NDIM, channels), f32),
            vmem((NDIM, channels), f32),
            vmem((NDIM, channels), f32),
            vmem((2, NDIM, channels), f32),
            vmem((blocks, length, depth), bf16),
            vmem((length * tiles, LANES), f32),
            vmem((NDIM, chunks, 2, tiles, LANES), f32),
            vmem((NDIM, 2, tiles, LANES), f32),
            vmem((rows, LANES), f32),
            vmem((rows, LANES), f32),
            vmem((CHUNK + 1, NDIM, 2, tiles, LANES), f32),
        ],
        9 + 3 + blocks + NDIM + 1,
    )
    more = max(1, peers // NDIM)

    def split(a):
        a = a.reshape(NDIM, 2, more, tiles // more, LANES).transpose(0, 2, 1, 3, 4)
        return a.reshape(peers, NDIM * more // peers, 2, tiles // more, LANES)

    def join(a):
        a = a.reshape(NDIM, more, 2, tiles // more, LANES).transpose(0, 2, 1, 3, 4)
        return a.reshape(NDIM, 2, tiles, LANES)

    arrived = lax.all_to_all(split(ends), "ctx", 0, 0)
    near, all_z = lax.optimization_barrier((near, all_z))
    near = near[:1] + [along(near[k], "ctx", k, members) for k in range(1, members)]
    near, all_v[1] = lax.optimization_barrier((near, all_v[1]))
    for k in range(3, layers):
        all_v.append(ring_on(all_v[k - 2], members, layers, (-1) ** (k + 1)))
    far = [along(block, "tp", k, tp) for k in range(1, tp) for block in near]
    my_q = lax.dynamic_index_in_dim(split(q.reshape(NDIM, 2, tiles, LANES)), place, 0, False)
    arrived, far, my_q, all_v[2] = lax.optimization_barrier((arrived, far, my_q, all_v[2]))
    (starts,) = call(functools.partial(scan_kernel, length), [shape(arrived.shape, f32)], [arrived, my_q], plain=1, grant=16 * MIB)
    incoming = lax.all_to_all(starts, "ctx", 0, 0)

    own, *sent = call(
        functools.partial(part_kernel, members, tp, layers),
        [shape((length, columns), f32)] + [shape((length, columns), bf16)] * (members - 1),
        [*near, *far, *all_v],
        [
            vmem((layers, members * length, depth), bf16),
            vmem((layers, depth, columns), bf16),
            vmem((length, columns), f32),
            vmem((max(members - 1, 1), length, columns), bf16),
        ],
        layers + tp * members * subs + members,
    )
    returned = [along(block, "ctx", -k, members) for k, block in enumerate(sent, 1)]
    incoming, own = lax.optimization_barrier((incoming, own))

    (mixed_rows,) = call(
        mix_kernel,
        [shape((length, channels), bf16)],
        [join(incoming), fresh, dense, q, w, ema_skip.reshape(tiles, LANES)],
        [
            vmem((NDIM, 2, tiles, LANES), f32),
            vmem((NDIM, chunks, 2, tiles, LANES), f32),
            vmem((length * tiles, LANES), f32),
            vmem((rows, LANES), f32),
            vmem((rows, LANES), f32),
            vmem((tiles, LANES), f32),
            vmem((length, channels), bf16),
            vmem((chunks, NDIM, 2, tiles, LANES), f32),
            vmem((CHUNK, NDIM, 2, tiles, LANES), f32),
            vmem((CHUNK, tiles, LANES), f32),
            vmem((length * tiles, LANES), f32),
        ],
        6 + max(1, tiles // 8),
    )
    mixed_rows, returned = lax.optimization_barrier((mixed_rows, returned))
    apart = others(mixed_rows, "tp")
    (result,) = call(
        functools.partial(attend_kernel, members, tp),
        [shape((length, columns), bf16)],
        [*all_z, mixed_rows, *apart, *returned, own, rms_gain[None], qk_affine],
        [
            vmem((members, layers, depth, head), bf16),
            vmem((tp, length, channels), bf16),
            vmem((max(members - 1, 1), length, columns), bf16),
            vmem((length, columns), f32),
            vmem((1, tp * channels), f32),
            vmem((4, head), f32),
            vmem((tp * blocks, length, depth), bf16),
            vmem((length, columns), bf16),
            vmem((length, columns), bf16),
        ],
        tp + 2 + 2 * members + 1,
    )
    return result


def solution(mesh):
    in_specs = (
        P("ctx", "tp"),
        P("tp"),
        P("tp"),
        P(None, "tp"),
        P(None, "tp"),
        P(None, "tp"),
        P(None, None, "tp"),
        P("tp"),
        P(),
        P("ctx", "tp"),
        P("ctx", "tp"),
        P(None, "tp"),
    )
    return jax.shard_map(body, mesh=mesh, in_specs=in_specs, out_specs=P("ctx", "tp"), check_vma=False)
```

```python
import functools

import jax
import jax.numpy as jnp
from jax import lax
from jax.experimental import pallas as pl
from jax.experimental.pallas import tpu as pltpu
from jax.sharding import PartitionSpec as P

NDIM = 16
GROUP = 64
STRETCH = 128
CHUNK = 16
LANES = 128
epsilon = 1e-05
f32 = jnp.float32
bf16 = jnp.bfloat16
MIB = 1024 * 1024
VMEM_LIMIT = 64 * MIB
CHEAP = pl.CostEstimate(flops=1, bytes_accessed=1, transcendentals=0)


def call(kernel, outs, inputs, scratch=(), copies=0, plain=0, grant=VMEM_LIMIT):
    hbm, vmem = pl.BlockSpec(memory_space=pltpu.HBM), pl.BlockSpec(memory_space=pltpu.VMEM)
    here = vmem if plain else hbm
    extra = [pltpu.SemaphoreType.DMA((copies,))] if copies else []
    return pl.pallas_call(
        kernel,
        out_shape=outs,
        in_specs=[here] * len(inputs),
        out_specs=[here] * len(outs),
        scratch_shapes=list(scratch) + extra,
        compiler_params=pltpu.CompilerParams(vmem_limit_bytes=grant),
        cost_estimate=CHEAP,
    )(*inputs)


class Copies:
    def __init__(self, sems):
        self.sems, self.used = sems, 0

    def start(self, source, target):
        copy = pltpu.make_async_copy(source, target, self.sems.at[self.used])
        self.used += 1
        copy.start()
        return copy


def pieces(value):
    first = value.astype(bf16)
    rest = value - first.astype(f32)
    second = rest.astype(bf16)
    third = (rest - second.astype(f32)).astype(bf16)
    return first, second, third


def mm(a, b):
    return jnp.dot(a, b, preferred_element_type=f32)


def membership(channels, width, transposed, first):
    shape = (width, channels) if transposed else (channels, width)
    channel = lax.broadcasted_iota(jnp.int32, shape, 1 if transposed else 0) + first
    group = lax.broadcasted_iota(jnp.int32, shape, 0 if transposed else 1)
    return jnp.where(channel // GROUP == group, 1.0, 0.0).astype(bf16)


def group_sums(x, first, width):
    member = membership(x.shape[1], width, False, first)
    square = x.astype(f32) * x.astype(f32)
    high = square.astype(bf16)
    low = (square - high.astype(f32)).astype(bf16)
    return mm(x, member), mm(high, member) + mm(low, member)


def sums_kernel(x_ref, running_ref, total_ref):
    length, channels = x_ref.shape
    width = running_ref.shape[2]
    rows = lax.broadcasted_iota(jnp.int32, (length, length), 0)
    cols = lax.broadcasted_iota(jnp.int32, (length, length), 1)
    lower = jnp.where(rows >= cols, 1.0, 0.0).astype(bf16)
    for at, value in enumerate(group_sums(x_ref[...], 0, width)):
        one, two, three = pieces(value)
        running = mm(lower, one) + mm(lower, two) + mm(lower, three)
        running_ref[at] = running
        for peer in range(total_ref.shape[0]):
            total_ref[peer, at : at + 1, :] = running[length - 1 : length, :]


def times(a, b):
    return a[0] * b[0] - a[1] * b[1], a[0] * b[1] + a[1] * b[0]


def row_pair(ref, j, tiles):
    start = pl.multiple_of(j * (2 * tiles), 2 * tiles)
    return ref[pl.ds(start, tiles), :], ref[pl.ds(start + tiles, tiles), :]


def powers_into(ref, first, factor, count):
    def one(j, _):
        q, now = factor(j), first(j)
        for k in range(count):
            ref[k, j, 0], ref[k, j, 1] = now
            if k + 1 < count:
                now = times(now, q)
        return _

    lax.fori_loop(0, NDIM, one, 0)


def feed_kernel(members, *refs):
    x_hbm, sums_hbm, running_hbm, gain_hbm, bias_hbm, decay_hbm, phase_hbm, in_hbm, out_hbm = refs[:9]
    near_hbm, (dense_hbm, fresh_hbm, end_hbm, q_hbm, w_hbm) = refs[9 : 9 + members], refs[9 + members : 14 + members]
    (
        x_ref, sums_ref, running_ref, gain_ref, bias_ref, decay_ref, phase_ref, in_ref, out_ref,
        normed_ref, dense_ref, fresh_ref, end_ref, q_ref, w_ref, power_ref, sems,
    ) = refs[14 + members :]
    copies = Copies(sems)
    loads = [
        copies.start(a, b)
        for a, b in (
            (decay_hbm, decay_ref), (phase_hbm, phase_ref), (running_hbm, running_ref), (sums_hbm, sums_ref), (x_hbm, x_ref),
            (gain_hbm, gain_ref), (bias_hbm, bias_ref), (in_hbm, in_ref), (out_hbm, out_ref),
        )
    ]
    length, channels = x_ref.shape
    width = running_ref.shape[2]
    tiles = channels // LANES
    chunks = length // CHUNK
    subs, _, depth = near_hbm[0].shape
    me = lax.axis_index("ctx")
    peers = sums_ref.shape[0]

    loads[0].wait()
    loads[1].wait()
    for tile in range(tiles):
        lanes = slice(tile * LANES, (tile + 1) * LANES)
        phase, decay = phase_ref[:, lanes], decay_ref[:, lanes]
        parts = (decay * jnp.cos(phase), decay * jnp.sin(phase))
        for part in range(2):
            q_ref[pl.ds(part * tiles + tile, NDIM, stride=2 * tiles), :] = parts[part]
    stores = [copies.start(q_ref, q_hbm)]
    one, zero = jnp.ones((tiles, LANES), f32), jnp.zeros((tiles, LANES), f32)
    powers_into(power_ref, lambda j: (one, zero), lambda j: row_pair(q_ref, j, tiles), CHUNK + 1)

    for load in loads[2:7]:
        load.wait()
    before = [jnp.zeros((1, width), f32) for _ in range(2)]
    for peer in range(peers):
        earlier = jnp.where(peer < me, 1.0, 0.0)
        for at in range(2):
            before[at] = before[at] + sums_ref[peer, at : at + 1, :] * earlier
    place = lax.broadcasted_iota(jnp.int32, (length, width), 0) + me * length + 1
    counts = place.astype(f32) * GROUP
    average = (before[0] + running_ref[0]) / counts
    spread = jnp.maximum((before[1] + running_ref[1]) / counts - average * average, 0.0)
    scale = lax.rsqrt(spread + epsilon)
    member = membership(channels, width, True, 0)
    average_pieces, scale_pieces = pieces(average), pieces(scale)
    for tile in range(tiles):
        lanes = slice(tile * LANES, (tile + 1) * LANES)
        mine = member[:, lanes]
        average_wide = sum(mm(p, mine) for p in average_pieces)
        scale_wide = sum(mm(p, mine) for p in scale_pieces)
        scaled = (x_ref[:, lanes].astype(f32) - average_wide) * scale_wide
        normed = (scaled * gain_ref[:, lanes] + bias_ref[:, lanes]).astype(bf16)
        part = min(depth, LANES)
        for low in range(0, LANES, part):
            at = tile * LANES + low
            normed_ref[at // depth, :, at % depth : at % depth + part] = normed[:, low : low + part]
        dense_ref[pl.ds(tile, length, stride=tiles), :] = normed.astype(f32)
    for away, ref in enumerate(near_hbm):
        to = lax.rem(me + away, members)
        for sub in range(subs):
            stores.append(copies.start(normed_ref.at[sub * members + to], ref.at[sub]))
    stores.append(copies.start(dense_ref, dense_hbm))

    loads[7].wait()
    loads[8].wait()
    for tile in range(tiles):
        lanes = slice(tile * LANES, (tile + 1) * LANES)
        for part in range(2):
            w_ref[pl.ds(part * tiles + tile, NDIM, stride=2 * tiles), :] = in_ref[:, lanes] * out_ref[part, :, lanes]
    stores.append(copies.start(w_ref, w_hbm))
    step = min(8, tiles)
    first_sem = copies.used

    def send(j):
        return pltpu.make_async_copy(fresh_ref.at[j], fresh_hbm.at[j], sems.at[first_sem + j])

    def one(j, _):
        for low in range(0, tiles, step):
            rows = slice(low, low + step)
            re = [jnp.zeros((step, LANES), f32) for _ in range(chunks)]
            im = [jnp.zeros((step, LANES), f32) for _ in range(chunks)]
            for b in range(CHUNK):
                p_re = power_ref[CHUNK - 1 - b, j, 0, rows, :]
                p_im = power_ref[CHUNK - 1 - b, j, 1, rows, :]
                for a in range(chunks):
                    at = (a * CHUNK + b) * tiles + low
                    value = dense_ref[at : at + step, :]
                    re[a] = re[a] + p_re * value
                    im[a] = im[a] + p_im * value
            q = (power_ref[CHUNK, j, 0, rows, :], power_ref[CHUNK, j, 1, rows, :])
            state = (re[0], im[0])
            for a in range(chunks):
                fresh_ref[j, a, 0, rows, :] = re[a]
                fresh_ref[j, a, 1, rows, :] = im[a]
                if a:
                    moved = times(state, q)
                    state = (moved[0] + re[a], moved[1] + im[a])
            end_ref[j, 0, rows, :], end_ref[j, 1, rows, :] = state
        send(j).start()
        return _

    lax.fori_loop(0, NDIM, one, 0)
    ends = pltpu.make_async_copy(end_ref, end_hbm, sems.at[first_sem + NDIM])
    ends.start()
    for store in stores:
        store.wait()
    lax.fori_loop(0, NDIM, lambda j, c: (send(j).wait(), c)[1], 0)
    ends.wait()


def scan_kernel(length, ends_ref, q_ref, out_ref):
    peers = ends_ref.shape[0]
    result, base, left = None, (q_ref[:, 0], q_ref[:, 1]), length
    while left:
        if left & 1:
            result = base if result is None else times(result, base)
        left >>= 1
        if left:
            base = times(base, base)
    state = (jnp.zeros_like(base[0]), jnp.zeros_like(base[1]))
    for peer in range(peers):
        out_ref[peer, :, 0], out_ref[peer, :, 1] = state
        if peer + 1 < peers:
            moved = times(state, result)
            state = (moved[0] + ends_ref[peer, :, 0], moved[1] + ends_ref[peer, :, 1])


def mix_kernel(
    incoming_hbm, fresh_hbm, dense_hbm, q_hbm, w_hbm, skip_hbm, mixed_hbm,
    incoming_ref, fresh_ref, dense_ref, q_ref, w_ref, skip_ref, mixed_ref, start_ref, coef_ref, tap_ref, out_ref, sems,
):
    copies = Copies(sems)
    loads = [
        copies.start(a, b)
        for a, b in (
            (q_hbm, q_ref), (w_hbm, w_ref), (skip_hbm, skip_ref), (incoming_hbm, incoming_ref), (fresh_hbm, fresh_ref), (dense_hbm, dense_ref),
        )
    ]
    length, channels = mixed_ref.shape
    tiles = channels // LANES
    chunks = length // CHUNK
    step = min(8, tiles)
    for load in loads[:3]:
        load.wait()
    powers_into(
        coef_ref,
        lambda j: times(row_pair(w_ref, j, tiles), row_pair(q_ref, j, tiles)),
        lambda j: row_pair(q_ref, j, tiles),
        CHUNK,
    )
    tap = skip_ref[...]
    for j in range(NDIM):
        tap = tap + row_pair(w_ref, j, tiles)[0]
    tap_ref[0] = tap

    def one_tap(k, _):
        tap = coef_ref[k, 0, 0]
        for j in range(1, NDIM):
            tap = tap + coef_ref[k, j, 0]
        tap_ref[k + 1] = tap
        return _

    lax.fori_loop(0, CHUNK - 1, one_tap, 0)
    for load in loads[3:5]:
        load.wait()

    def one(j, _):
        q = row_pair(q_ref, j, tiles)
        left = CHUNK
        while left > 1:
            q = times(q, q)
            left //= 2
        state = (incoming_ref[j, 0], incoming_ref[j, 1])
        for a in range(chunks):
            start_ref[a, j, 0], start_ref[a, j, 1] = state
            if a + 1 < chunks:
                moved = times(state, q)
                state = (moved[0] + fresh_ref[j, a, 0], moved[1] + fresh_ref[j, a, 1])
        return _

    lax.fori_loop(0, NDIM, one, 0)

    loads[5].wait()
    for low in range(0, tiles, step):
        rows = slice(low, low + step)
        for b in range(0, CHUNK, 2):
            total = [[jnp.zeros((step, LANES), f32) for _ in range(chunks)] for _ in range(2)]

            def carry(j, total, b=b, rows=rows):
                total = [list(t) for t in total]
                coefs = [(coef_ref[b + i, j, 0, rows, :], coef_ref[b + i, j, 1, rows, :]) for i in range(2)]
                for a in range(chunks):
                    re, im = start_ref[a, j, 0, rows, :], start_ref[a, j, 1, rows, :]
                    for i in range(2):
                        total[i][a] = total[i][a] + coefs[i][0] * re - coefs[i][1] * im
                return total

            total = lax.fori_loop(0, NDIM, carry, total, unroll=4)
            for s in range(b + 2):
                for i in range(2):
                    if s > b + i:
                        continue
                    tap = tap_ref[b + i - s, rows, :]
                    for a in range(chunks):
                        at = (a * CHUNK + s) * tiles + low
                        total[i][a] = total[i][a] + tap * dense_ref[at : at + step, :]
            for i in range(2):
                for a in range(chunks):
                    at = (a * CHUNK + b + i) * tiles + low
                    out_ref[at : at + step, :] = total[i][a]
        for tile in range(low, low + step):
            lanes = slice(tile * LANES, (tile + 1) * LANES)
            value = out_ref[pl.ds(tile, length, stride=tiles), :]
            mixed_ref[:, lanes] = (value / (1.0 + jnp.exp(-value))).astype(bf16)
        lanes = slice(low * LANES, (low + step) * LANES)
        loads.append(copies.start(mixed_ref.at[:, lanes], mixed_hbm.at[:, lanes]))
    for store in loads[6:]:
        store.wait()


def along(block, axis, step, group):
    count = lax.axis_size(axis)
    pairs = [(i, i - i % group + (i + step) % group) for i in range(count)]
    return lax.ppermute(block, axis, pairs)


def ring_of(layers):
    return [0, *range(1, layers, 2), *reversed(range(2, layers, 2))]


def ring_on(block, members, layers, step):
    ring = ring_of(layers)
    pairs = [
        (ring[k] * members + r, ring[(k + step) % layers] * members + r) for k in range(layers) for r in range(members)
    ]
    return lax.ppermute(block, "ctx", pairs)


def ring_steps(layers):
    return [0, *[(-1) ** (k + 1) * -((k + 1) // 2) for k in range(1, layers)]]


def others(block, axis):
    count = lax.axis_size(axis)
    return [along(block, axis, k, count) for k in range(1, count)]


def part_kernel(members, tp, layers, *refs):
    blocks_hbm, refs = refs[: members * tp], refs[members * tp :]
    weights_hbm, refs = refs[:layers], refs[layers:]
    own_hbm, sent_hbm, refs = refs[0], refs[1:members], refs[members:]
    row_ref, weight_ref, own_ref, sent_ref, sems = refs
    copies = Copies(sems)
    subs, length, depth = blocks_hbm[0].shape
    half, place = lax.axis_index("tp"), lax.axis_index("ctx")
    ring_at = sum(jnp.where(place // members == at, k, 0) for k, at in enumerate(ring_of(layers)))
    loads = []
    for away in range(tp):
        other = lax.rem(half + tp - away, tp)
        for k in range(members):
            for sub in range(subs):
                to = row_ref.at[other * subs + sub, k * length : (k + 1) * length, :]
                loads.append(copies.start(blocks_hbm[away * members + k].at[sub], to))
    later = [copies.start(weight, weight_ref.at[at]) for at, weight in enumerate(weights_hbm)]
    ring = ring_of(layers)
    blocks = []
    for step in ring_steps(layers):
        at = lax.rem(ring_at + layers + step, layers)
        block = jnp.int32(0)
        for place, layer in enumerate(ring):
            block = jnp.where(at == place, layer, block)
        blocks.append(block)
    for load in loads:
        load.wait()
    stores = []
    for k in range(members):
        here = slice(k * length, (k + 1) * length)
        total = None
        for back in range(layers):
            if k == 0:
                later[back].wait()
            product = mm(row_ref[blocks[back], here, :], weight_ref[back])
            total = product if total is None else total + product
        if k == 0:
            own_ref[...] = total
            stores.append(copies.start(own_ref, own_hbm))
        else:
            sent_ref[k - 1] = total.astype(bf16)
            stores.append(copies.start(sent_ref.at[k - 1], sent_hbm[k - 1]))
    for store in stores:
        store.wait()


def attend_kernel(members, tp, *refs):
    weights_hbm, refs = refs[:members], refs[members:]
    mixed_hbm, refs = refs[:tp], refs[tp:]
    parts_hbm, refs = refs[: members - 1], refs[members - 1 :]
    own_hbm, gain_hbm, affine_hbm, result_hbm = refs[:4]
    weight_ref, mixed_ref, part_ref, own_ref, gain_ref, affine_ref, row_ref, value_ref, result_ref, sems = refs[4:]
    copies = Copies(sems)
    loads = [copies.start(a, mixed_ref.at[k]) for k, a in enumerate(mixed_hbm)]
    loads += [copies.start(gain_hbm, gain_ref), copies.start(affine_hbm, affine_ref)]
    first = len(loads)
    loads += [copies.start(a, weight_ref.at[k]) for k, a in enumerate(weights_hbm)]
    second = len(loads)
    loads += [copies.start(own_hbm, own_ref)] + [copies.start(a, part_ref.at[k]) for k, a in enumerate(parts_hbm)]
    _, layers, depth, head = weight_ref.shape
    _, length, channels = mixed_ref.shape
    place, half = lax.axis_index("ctx"), lax.axis_index("tp")
    member, layer = lax.rem(place, members), lax.div(place, members)
    blocks = channels // depth

    for load in loads[:first]:
        load.wait()
    square = jnp.zeros((length, 1), f32)
    for k in range(tp):
        value = mixed_ref[k].astype(f32)
        square = square + jnp.sum(value * value, axis=1, keepdims=True)
    scale = lax.rsqrt(square / (channels * tp) + 1e-06)
    for k in range(tp):
        at = lax.rem(half + tp - k, tp)
        gain = gain_ref[:, pl.ds(pl.multiple_of(at * channels, LANES), channels)]
        normed = (mixed_ref[k].astype(f32) * scale * gain).astype(bf16)
        for block in range(blocks):
            row_ref[at * blocks + block] = normed[:, block * depth : (block + 1) * depth]
    for load in loads[first:second]:
        load.wait()
    z_total = jnp.zeros((length, head), f32)
    for m in range(members):
        for k in range(layers):
            block = lax.rem(layer + layers - k, layers) * members + lax.rem(member + members - m, members)
            z_total = z_total + mm(row_ref[block], weight_ref[m, k])
    queries = (z_total * affine_ref[0:1, :] + affine_ref[1:2, :]).astype(bf16)
    key_rows = (z_total * affine_ref[2:3, :] + affine_ref[3:4, :]).astype(bf16)

    for load in loads[second:]:
        load.wait()
    total = own_ref[...]
    for k in range(members - 1):
        total = total + part_ref[k].astype(f32)
    value_ref[...] = (total / (1.0 + jnp.exp(-total))).astype(bf16)
    row = lax.broadcasted_iota(jnp.int32, (STRETCH, STRETCH), 0)
    col = lax.broadcasted_iota(jnp.int32, (STRETCH, STRETCH), 1)
    for low in range(0, length, STRETCH):
        here = slice(low, low + STRETCH)
        scores = lax.dot_general(
            queries[here], key_rows[here], (((1,), (1,)), ((), ())), preferred_element_type=f32
        ) * (1.0 / head**0.5)
        scores = jnp.where(row >= col, scores, -1e30)
        weights = jnp.exp(scores - jnp.max(scores, axis=1, keepdims=True))
        probabilities = (weights / jnp.sum(weights, axis=1, keepdims=True)).astype(bf16)
        result_ref[:] = mm(probabilities, value_ref[:]).astype(bf16)
    copies.start(result_ref, result_hbm).wait()


def body(
    tokens, norm_gain, norm_bias, ema_decay, ema_phase, ema_in, ema_out, ema_skip, rms_gain, z_weight, v_weight, qk_affine
):
    length, channels = tokens.shape
    tiles = channels // LANES
    chunks = length // CHUNK
    width = -(-(channels // GROUP) // LANES) * LANES
    place, peers = lax.axis_index("ctx"), lax.axis_size("ctx")
    half, tp = lax.axis_index("tp"), lax.axis_size("tp")
    depth, columns = v_weight.shape
    head = z_weight.shape[1]
    blocks = channels // depth
    members = 4 if peers % 4 == 0 and blocks % 4 == 0 else 1
    layers = peers // members
    subs = blocks // members
    shape, vmem = jax.ShapeDtypeStruct, pltpu.VMEM

    running, totals = call(
        sums_kernel,
        [shape((2, length, width), f32), shape((peers, 2, width), f32)],
        [tokens],
        plain=1,
        grant=16 * MIB,
    )
    sums = lax.all_to_all(totals, "ctx", 0, 0)
    line_z = [z_weight] + [
        lax.ppermute(z_weight, "ctx", [(i, (i + members * k) % peers) for i in range(peers)])
        for k in range(1, layers)
    ]
    line_z = jnp.stack(line_z)
    sums, v_weight = lax.optimization_barrier((sums, v_weight))
    all_v = [v_weight] + [ring_on(v_weight, members, layers, (-1) ** (k + 1)) for k in range(1, min(layers, 3))]
    all_z = [line_z] + [along(line_z, "ctx", k, members) for k in range(1, members)]

    rows = NDIM * 2 * tiles
    *near, dense, fresh, ends, q, w = call(
        functools.partial(feed_kernel, members),
        [shape((subs, length, depth), bf16)] * members
        + [
            shape((length * tiles, LANES), f32),
            shape((NDIM, chunks, 2, tiles, LANES), f32),
            shape((NDIM, 2, tiles, LANES), f32),
            shape((rows, LANES), f32),
            shape((rows, LANES), f32),
        ],
        [tokens, sums, running, norm_gain[None], norm_bias[None], ema_decay, ema_phase, ema_in, ema_out],
        [
            vmem((length, channels), bf16),
            vmem((peers, 2, width), f32),
            vmem((2, length, width), f32),
            vmem((1, channels), f32),
            vmem((1, channels), f32),
            vmem((NDIM, channels), f32),
            vmem((NDIM, channels), f32),
            vmem((NDIM, channels), f32),
            vmem((2, NDIM, channels), f32),
            vmem((blocks, length, depth), bf16),
            vmem((length * tiles, LANES), f32),
            vmem((NDIM, chunks, 2, tiles, LANES), f32),
            vmem((NDIM, 2, tiles, LANES), f32),
            vmem((rows, LANES), f32),
            vmem((rows, LANES), f32),
            vmem((CHUNK + 1, NDIM, 2, tiles, LANES), f32),
        ],
        9 + 3 + blocks + NDIM + 1,
    )
    more = max(1, peers // NDIM)

    def split(a):
        a = a.reshape(NDIM, 2, more, tiles // more, LANES).transpose(0, 2, 1, 3, 4)
        return a.reshape(peers, NDIM * more // peers, 2, tiles // more, LANES)

    def join(a):
        a = a.reshape(NDIM, more, 2, tiles // more, LANES).transpose(0, 2, 1, 3, 4)
        return a.reshape(NDIM, 2, tiles, LANES)

    arrived = lax.all_to_all(split(ends), "ctx", 0, 0)
    near, all_z = lax.optimization_barrier((near, all_z))
    near = near[:1] + [along(near[k], "ctx", k, members) for k in range(1, members)]
    my_q = lax.dynamic_index_in_dim(split(q.reshape(NDIM, 2, tiles, LANES)), place, 0, False)
    near, all_v[1], my_q = lax.optimization_barrier((near, all_v[1], my_q))
    for k in range(3, layers):
        all_v.append(ring_on(all_v[k - 2], members, layers, (-1) ** (k + 1)))
    far = [along(block, "tp", k, tp) for k in range(1, tp) for block in near]
    arrived, far, my_q, all_v[2] = lax.optimization_barrier((arrived, far, my_q, all_v[2]))
    (starts,) = call(functools.partial(scan_kernel, length), [shape(arrived.shape, f32)], [arrived, my_q], plain=1, grant=16 * MIB)
    incoming = lax.all_to_all(starts, "ctx", 0, 0)

    own, *sent = call(
        functools.partial(part_kernel, members, tp, layers),
        [shape((length, columns), f32)] + [shape((length, columns), bf16)] * (members - 1),
        [*near, *far, *all_v],
        [
            vmem((layers, members * length, depth), bf16),
            vmem((layers, depth, columns), bf16),
            vmem((length, columns), f32),
            vmem((max(members - 1, 1), length, columns), bf16),
        ],
        layers + tp * members * subs + members,
    )
    returned = [along(block, "ctx", -k, members) for k, block in enumerate(sent, 1)]
    incoming, own = lax.optimization_barrier((incoming, own))

    (mixed_rows,) = call(
        mix_kernel,
        [shape((length, channels), bf16)],
        [join(incoming), fresh, dense, q, w, ema_skip.reshape(tiles, LANES)],
        [
            vmem((NDIM, 2, tiles, LANES), f32),
            vmem((NDIM, chunks, 2, tiles, LANES), f32),
            vmem((length * tiles, LANES), f32),
            vmem((rows, LANES), f32),
            vmem((rows, LANES), f32),
            vmem((tiles, LANES), f32),
            vmem((length, channels), bf16),
            vmem((chunks, NDIM, 2, tiles, LANES), f32),
            vmem((CHUNK, NDIM, 2, tiles, LANES), f32),
            vmem((CHUNK, tiles, LANES), f32),
            vmem((length * tiles, LANES), f32),
        ],
        6 + max(1, tiles // 8),
    )
    mixed_rows, returned = lax.optimization_barrier((mixed_rows, returned))
    apart = others(mixed_rows, "tp")
    (result,) = call(
        functools.partial(attend_kernel, members, tp),
        [shape((length, columns), bf16)],
        [*all_z, mixed_rows, *apart, *returned, own, rms_gain[None], qk_affine],
        [
            vmem((members, layers, depth, head), bf16),
            vmem((tp, length, channels), bf16),
            vmem((max(members - 1, 1), length, columns), bf16),
            vmem((length, columns), f32),
            vmem((1, tp * channels), f32),
            vmem((4, head), f32),
            vmem((tp * blocks, length, depth), bf16),
            vmem((length, columns), bf16),
            vmem((length, columns), bf16),
        ],
        tp + 2 + 2 * members + 1,
    )
    return result


def solution(mesh):
    in_specs = (
        P("ctx", "tp"),
        P("tp"),
        P("tp"),
        P(None, "tp"),
        P(None, "tp"),
        P(None, "tp"),
        P(None, None, "tp"),
        P("tp"),
        P(),
        P("ctx", "tp"),
        P("ctx", "tp"),
        P(None, "tp"),
    )
    return jax.shard_map(body, mesh=mesh, in_specs=in_specs, out_specs=P("ctx", "tp"), check_vma=False)
```

```python
import functools

import jax
import jax.numpy as jnp
from jax import lax
from jax.experimental import pallas as pl
from jax.experimental.pallas import tpu as pltpu
from jax.sharding import PartitionSpec as P

NDIM = 16
GROUP = 64
STRETCH = 128
CHUNK = 16
LANES = 128
epsilon = 1e-05
f32 = jnp.float32
bf16 = jnp.bfloat16
MIB = 1024 * 1024
VMEM_LIMIT = 64 * MIB
CHEAP = pl.CostEstimate(flops=1, bytes_accessed=1, transcendentals=0)


def call(kernel, outs, inputs, scratch=(), copies=0, plain=0, grant=VMEM_LIMIT):
    hbm, vmem = pl.BlockSpec(memory_space=pltpu.HBM), pl.BlockSpec(memory_space=pltpu.VMEM)
    here = vmem if plain else hbm
    extra = [pltpu.SemaphoreType.DMA((copies,))] if copies else []
    return pl.pallas_call(
        kernel,
        out_shape=outs,
        in_specs=[here] * len(inputs),
        out_specs=[here] * len(outs),
        scratch_shapes=list(scratch) + extra,
        compiler_params=pltpu.CompilerParams(vmem_limit_bytes=grant),
        cost_estimate=CHEAP,
    )(*inputs)


class Copies:
    def __init__(self, sems):
        self.sems, self.used = sems, 0

    def start(self, source, target):
        copy = pltpu.make_async_copy(source, target, self.sems.at[self.used])
        self.used += 1
        copy.start()
        return copy


def pieces(value):
    first = value.astype(bf16)
    rest = value - first.astype(f32)
    second = rest.astype(bf16)
    third = (rest - second.astype(f32)).astype(bf16)
    return first, second, third


def mm(a, b):
    return jnp.dot(a, b, preferred_element_type=f32)


def membership(channels, width, transposed, first):
    shape = (width, channels) if transposed else (channels, width)
    channel = lax.broadcasted_iota(jnp.int32, shape, 1 if transposed else 0) + first
    group = lax.broadcasted_iota(jnp.int32, shape, 0 if transposed else 1)
    return jnp.where(channel // GROUP == group, 1.0, 0.0).astype(bf16)


def group_sums(x, first, width):
    member = membership(x.shape[1], width, False, first)
    square = x.astype(f32) * x.astype(f32)
    high = square.astype(bf16)
    low = (square - high.astype(f32)).astype(bf16)
    return mm(x, member), mm(high, member) + mm(low, member)


def sums_kernel(x_ref, running_ref, total_ref):
    length, channels = x_ref.shape
    width = running_ref.shape[2]
    rows = lax.broadcasted_iota(jnp.int32, (length, length), 0)
    cols = lax.broadcasted_iota(jnp.int32, (length, length), 1)
    lower = jnp.where(rows >= cols, 1.0, 0.0).astype(bf16)
    for at, value in enumerate(group_sums(x_ref[...], 0, width)):
        one, two, three = pieces(value)
        running = mm(lower, one) + mm(lower, two) + mm(lower, three)
        running_ref[at] = running
        for peer in range(total_ref.shape[0]):
            total_ref[peer, at : at + 1, :] = running[length - 1 : length, :]


def times(a, b):
    return a[0] * b[0] - a[1] * b[1], a[0] * b[1] + a[1] * b[0]


def row_pair(ref, j, tiles):
    start = pl.multiple_of(j * (2 * tiles), 2 * tiles)
    return ref[pl.ds(start, tiles), :], ref[pl.ds(start + tiles, tiles), :]


def powers_into(ref, first, factor, count):
    def one(j, _):
        q, now = factor(j), first(j)
        for k in range(count):
            ref[k, j, 0], ref[k, j, 1] = now
            if k + 1 < count:
                now = times(now, q)
        return _

    lax.fori_loop(0, NDIM, one, 0)


def partner(member, step):
    low, high = lax.rem(member, 2), lax.div(member, 2)
    return (1 - low if step & 1 else low) + 2 * (1 - high if step & 2 else high)


def feed_kernel(members, *refs):
    x_hbm, sums_hbm, running_hbm, gain_hbm, bias_hbm, decay_hbm, phase_hbm, in_hbm, out_hbm = refs[:9]
    near_hbm, (dense_hbm, fresh_hbm, end_hbm, q_hbm, w_hbm) = refs[9 : 9 + members], refs[9 + members : 14 + members]
    (
        x_ref, sums_ref, running_ref, gain_ref, bias_ref, decay_ref, phase_ref, in_ref, out_ref,
        normed_ref, dense_ref, fresh_ref, end_ref, q_ref, w_ref, power_ref, sems,
    ) = refs[14 + members :]
    copies = Copies(sems)
    loads = [
        copies.start(a, b)
        for a, b in (
            (decay_hbm, decay_ref), (phase_hbm, phase_ref), (running_hbm, running_ref), (sums_hbm, sums_ref), (x_hbm, x_ref),
            (gain_hbm, gain_ref), (bias_hbm, bias_ref), (in_hbm, in_ref), (out_hbm, out_ref),
        )
    ]
    length, channels = x_ref.shape
    width = running_ref.shape[2]
    tiles = channels // LANES
    chunks = length // CHUNK
    subs, _, depth = near_hbm[0].shape
    me = lax.axis_index("ctx")
    peers = sums_ref.shape[0]

    loads[0].wait()
    loads[1].wait()
    for tile in range(tiles):
        lanes = slice(tile * LANES, (tile + 1) * LANES)
        phase, decay = phase_ref[:, lanes], decay_ref[:, lanes]
        parts = (decay * jnp.cos(phase), decay * jnp.sin(phase))
        for part in range(2):
            q_ref[pl.ds(part * tiles + tile, NDIM, stride=2 * tiles), :] = parts[part]
    stores = [copies.start(q_ref, q_hbm)]
    one, zero = jnp.ones((tiles, LANES), f32), jnp.zeros((tiles, LANES), f32)
    powers_into(power_ref, lambda j: (one, zero), lambda j: row_pair(q_ref, j, tiles), CHUNK + 1)

    for load in loads[2:7]:
        load.wait()
    before = [jnp.zeros((1, width), f32) for _ in range(2)]
    for peer in range(peers):
        earlier = jnp.where(peer < me, 1.0, 0.0)
        for at in range(2):
            before[at] = before[at] + sums_ref[peer, at : at + 1, :] * earlier
    place = lax.broadcasted_iota(jnp.int32, (length, width), 0) + me * length + 1
    counts = place.astype(f32) * GROUP
    average = (before[0] + running_ref[0]) / counts
    spread = jnp.maximum((before[1] + running_ref[1]) / counts - average * average, 0.0)
    scale = lax.rsqrt(spread + epsilon)
    member = membership(channels, width, True, 0)
    average_pieces, scale_pieces = pieces(average), pieces(scale)
    for tile in range(tiles):
        lanes = slice(tile * LANES, (tile + 1) * LANES)
        mine = member[:, lanes]
        average_wide = sum(mm(p, mine) for p in average_pieces)
        scale_wide = sum(mm(p, mine) for p in scale_pieces)
        scaled = (x_ref[:, lanes].astype(f32) - average_wide) * scale_wide
        normed = (scaled * gain_ref[:, lanes] + bias_ref[:, lanes]).astype(bf16)
        part = min(depth, LANES)
        for low in range(0, LANES, part):
            at = tile * LANES + low
            normed_ref[at // depth, :, at % depth : at % depth + part] = normed[:, low : low + part]
        dense_ref[pl.ds(tile, length, stride=tiles), :] = normed.astype(f32)
    for away, ref in enumerate(near_hbm):
        to = partner(lax.rem(me, members), away)
        for sub in range(subs):
            stores.append(copies.start(normed_ref.at[sub * members + to], ref.at[sub]))
    stores.append(copies.start(dense_ref, dense_hbm))

    loads[7].wait()
    loads[8].wait()
    for tile in range(tiles):
        lanes = slice(tile * LANES, (tile + 1) * LANES)
        for part in range(2):
            w_ref[pl.ds(part * tiles + tile, NDIM, stride=2 * tiles), :] = in_ref[:, lanes] * out_ref[part, :, lanes]
    stores.append(copies.start(w_ref, w_hbm))
    step = min(8, tiles)
    first_sem = copies.used

    def send(j):
        return pltpu.make_async_copy(fresh_ref.at[j], fresh_hbm.at[j], sems.at[first_sem + j])

    def one(j, _):
        for low in range(0, tiles, step):
            rows = slice(low, low + step)
            re = [jnp.zeros((step, LANES), f32) for _ in range(chunks)]
            im = [jnp.zeros((step, LANES), f32) for _ in range(chunks)]
            for b in range(CHUNK):
                p_re = power_ref[CHUNK - 1 - b, j, 0, rows, :]
                p_im = power_ref[CHUNK - 1 - b, j, 1, rows, :]
                for a in range(chunks):
                    at = (a * CHUNK + b) * tiles + low
                    value = dense_ref[at : at + step, :]
                    re[a] = re[a] + p_re * value
                    im[a] = im[a] + p_im * value
            q = (power_ref[CHUNK, j, 0, rows, :], power_ref[CHUNK, j, 1, rows, :])
            state = (re[0], im[0])
            for a in range(chunks):
                fresh_ref[j, a, 0, rows, :] = re[a]
                fresh_ref[j, a, 1, rows, :] = im[a]
                if a:
                    moved = times(state, q)
                    state = (moved[0] + re[a], moved[1] + im[a])
            end_ref[j, 0, rows, :], end_ref[j, 1, rows, :] = state
        send(j).start()
        return _

    lax.fori_loop(0, NDIM, one, 0)
    ends = pltpu.make_async_copy(end_ref, end_hbm, sems.at[first_sem + NDIM])
    ends.start()
    for store in stores:
        store.wait()
    lax.fori_loop(0, NDIM, lambda j, c: (send(j).wait(), c)[1], 0)
    ends.wait()


def scan_kernel(length, ends_ref, q_ref, out_ref):
    peers = ends_ref.shape[0]
    result, base, left = None, (q_ref[:, 0], q_ref[:, 1]), length
    while left:
        if left & 1:
            result = base if result is None else times(result, base)
        left >>= 1
        if left:
            base = times(base, base)
    state = (jnp.zeros_like(base[0]), jnp.zeros_like(base[1]))
    for peer in range(peers):
        out_ref[peer, :, 0], out_ref[peer, :, 1] = state
        if peer + 1 < peers:
            moved = times(state, result)
            state = (moved[0] + ends_ref[peer, :, 0], moved[1] + ends_ref[peer, :, 1])


def mix_kernel(
    incoming_hbm, fresh_hbm, dense_hbm, q_hbm, w_hbm, skip_hbm, mixed_hbm,
    incoming_ref, fresh_ref, dense_ref, q_ref, w_ref, skip_ref, mixed_ref, start_ref, coef_ref, tap_ref, out_ref, sems,
):
    copies = Copies(sems)
    loads = [
        copies.start(a, b)
        for a, b in (
            (q_hbm, q_ref), (w_hbm, w_ref), (skip_hbm, skip_ref), (incoming_hbm, incoming_ref), (fresh_hbm, fresh_ref), (dense_hbm, dense_ref),
        )
    ]
    length, channels = mixed_ref.shape
    tiles = channels // LANES
    chunks = length // CHUNK
    step = min(8, tiles)
    for load in loads[:3]:
        load.wait()
    powers_into(
        coef_ref,
        lambda j: times(row_pair(w_ref, j, tiles), row_pair(q_ref, j, tiles)),
        lambda j: row_pair(q_ref, j, tiles),
        CHUNK,
    )
    tap = skip_ref[...]
    for j in range(NDIM):
        tap = tap + row_pair(w_ref, j, tiles)[0]
    tap_ref[0] = tap

    def one_tap(k, _):
        tap = coef_ref[k, 0, 0]
        for j in range(1, NDIM):
            tap = tap + coef_ref[k, j, 0]
        tap_ref[k + 1] = tap
        return _

    lax.fori_loop(0, CHUNK - 1, one_tap, 0)
    for load in loads[3:5]:
        load.wait()

    def one(j, _):
        q = row_pair(q_ref, j, tiles)
        left = CHUNK
        while left > 1:
            q = times(q, q)
            left //= 2
        state = (incoming_ref[j, 0], incoming_ref[j, 1])
        for a in range(chunks):
            start_ref[a, j, 0], start_ref[a, j, 1] = state
            if a + 1 < chunks:
                moved = times(state, q)
                state = (moved[0] + fresh_ref[j, a, 0], moved[1] + fresh_ref[j, a, 1])
        return _

    lax.fori_loop(0, NDIM, one, 0)

    loads[5].wait()
    for low in range(0, tiles, step):
        rows = slice(low, low + step)
        for b in range(0, CHUNK, 2):
            total = [[jnp.zeros((step, LANES), f32) for _ in range(chunks)] for _ in range(2)]

            def carry(j, total, b=b, rows=rows):
                total = [list(t) for t in total]
                coefs = [(coef_ref[b + i, j, 0, rows, :], coef_ref[b + i, j, 1, rows, :]) for i in range(2)]
                for a in range(chunks):
                    re, im = start_ref[a, j, 0, rows, :], start_ref[a, j, 1, rows, :]
                    for i in range(2):
                        total[i][a] = total[i][a] + coefs[i][0] * re - coefs[i][1] * im
                return total

            total = lax.fori_loop(0, NDIM, carry, total, unroll=4)
            for s in range(b + 2):
                for i in range(2):
                    if s > b + i:
                        continue
                    tap = tap_ref[b + i - s, rows, :]
                    for a in range(chunks):
                        at = (a * CHUNK + s) * tiles + low
                        total[i][a] = total[i][a] + tap * dense_ref[at : at + step, :]
            for i in range(2):
                for a in range(chunks):
                    at = (a * CHUNK + b + i) * tiles + low
                    out_ref[at : at + step, :] = total[i][a]
        for tile in range(low, low + step):
            lanes = slice(tile * LANES, (tile + 1) * LANES)
            value = out_ref[pl.ds(tile, length, stride=tiles), :]
            mixed_ref[:, lanes] = (value / (1.0 + jnp.exp(-value))).astype(bf16)
        lanes = slice(low * LANES, (low + step) * LANES)
        loads.append(copies.start(mixed_ref.at[:, lanes], mixed_hbm.at[:, lanes]))
    for store in loads[6:]:
        store.wait()


def along(block, axis, step, group):
    count = lax.axis_size(axis)
    pairs = [(i, i - i % group + (i + step) % group) for i in range(count)]
    return lax.ppermute(block, axis, pairs)


def swap(block, step, group):
    return lax.ppermute(block, "ctx", [(i, i - i % group + (i % group ^ step)) for i in range(lax.axis_size("ctx"))])


def ring_of(layers):
    return [0, *range(1, layers, 2), *reversed(range(2, layers, 2))]


def ring_on(block, members, layers, step):
    ring = ring_of(layers)
    pairs = [
        (ring[k] * members + r, ring[(k + step) % layers] * members + r) for k in range(layers) for r in range(members)
    ]
    return lax.ppermute(block, "ctx", pairs)


def ring_steps(layers):
    return [0, *[(-1) ** (k + 1) * -((k + 1) // 2) for k in range(1, layers)]]


def others(block, axis):
    count = lax.axis_size(axis)
    return [along(block, axis, k, count) for k in range(1, count)]


def part_kernel(members, tp, layers, *refs):
    blocks_hbm, refs = refs[: members * tp], refs[members * tp :]
    weights_hbm, refs = refs[:layers], refs[layers:]
    own_hbm, sent_hbm, refs = refs[0], refs[1:members], refs[members:]
    row_ref, weight_ref, own_ref, sent_ref, sems = refs
    copies = Copies(sems)
    subs, length, depth = blocks_hbm[0].shape
    half, place = lax.axis_index("tp"), lax.axis_index("ctx")
    ring_at = sum(jnp.where(place // members == at, k, 0) for k, at in enumerate(ring_of(layers)))
    loads = []
    for away in range(tp):
        other = lax.rem(half + tp - away, tp)
        for k in range(members):
            for sub in range(subs):
                to = row_ref.at[other * subs + sub, k * length : (k + 1) * length, :]
                loads.append(copies.start(blocks_hbm[away * members + k].at[sub], to))
    later = [copies.start(weight, weight_ref.at[at]) for at, weight in enumerate(weights_hbm)]
    ring = ring_of(layers)
    blocks = []
    for step in ring_steps(layers):
        at = lax.rem(ring_at + layers + step, layers)
        block = jnp.int32(0)
        for place, layer in enumerate(ring):
            block = jnp.where(at == place, layer, block)
        blocks.append(block)
    for load in loads:
        load.wait()
    stores = []
    for k in range(members):
        here = slice(k * length, (k + 1) * length)
        total = None
        for back in range(layers):
            if k == 0:
                later[back].wait()
            product = mm(row_ref[blocks[back], here, :], weight_ref[back])
            total = product if total is None else total + product
        if k == 0:
            own_ref[...] = total
            stores.append(copies.start(own_ref, own_hbm))
        else:
            sent_ref[k - 1] = total.astype(bf16)
            stores.append(copies.start(sent_ref.at[k - 1], sent_hbm[k - 1]))
    for store in stores:
        store.wait()


def attend_kernel(members, tp, *refs):
    weights_hbm, refs = refs[:members], refs[members:]
    mixed_hbm, refs = refs[:tp], refs[tp:]
    parts_hbm, refs = refs[: members - 1], refs[members - 1 :]
    own_hbm, gain_hbm, affine_hbm, result_hbm = refs[:4]
    weight_ref, mixed_ref, part_ref, own_ref, gain_ref, affine_ref, row_ref, value_ref, result_ref, sems = refs[4:]
    copies = Copies(sems)
    loads = [copies.start(a, mixed_ref.at[k]) for k, a in enumerate(mixed_hbm)]
    loads += [copies.start(gain_hbm, gain_ref), copies.start(affine_hbm, affine_ref)]
    first = len(loads)
    loads += [copies.start(a, weight_ref.at[k]) for k, a in enumerate(weights_hbm)]
    second = len(loads)
    loads += [copies.start(own_hbm, own_ref)] + [copies.start(a, part_ref.at[k]) for k, a in enumerate(parts_hbm)]
    _, layers, depth, head = weight_ref.shape
    _, length, channels = mixed_ref.shape
    place, half = lax.axis_index("ctx"), lax.axis_index("tp")
    member, layer = lax.rem(place, members), lax.div(place, members)
    blocks = channels // depth

    for load in loads[:first]:
        load.wait()
    square = jnp.zeros((length, 1), f32)
    for k in range(tp):
        value = mixed_ref[k].astype(f32)
        square = square + jnp.sum(value * value, axis=1, keepdims=True)
    scale = lax.rsqrt(square / (channels * tp) + 1e-06)
    for k in range(tp):
        at = lax.rem(half + tp - k, tp)
        gain = gain_ref[:, pl.ds(pl.multiple_of(at * channels, LANES), channels)]
        normed = (mixed_ref[k].astype(f32) * scale * gain).astype(bf16)
        for block in range(blocks):
            row_ref[at * blocks + block] = normed[:, block * depth : (block + 1) * depth]
    for load in loads[first:second]:
        load.wait()
    z_total = jnp.zeros((length, head), f32)
    for m in range(members):
        for k in range(layers):
            block = lax.rem(layer + layers - k, layers) * members + partner(member, m)
            z_total = z_total + mm(row_ref[block], weight_ref[m, k])
    queries = (z_total * affine_ref[0:1, :] + affine_ref[1:2, :]).astype(bf16)
    key_rows = (z_total * affine_ref[2:3, :] + affine_ref[3:4, :]).astype(bf16)

    for load in loads[second:]:
        load.wait()
    total = own_ref[...]
    for k in range(members - 1):
        total = total + part_ref[k].astype(f32)
    value_ref[...] = (total / (1.0 + jnp.exp(-total))).astype(bf16)
    row = lax.broadcasted_iota(jnp.int32, (STRETCH, STRETCH), 0)
    col = lax.broadcasted_iota(jnp.int32, (STRETCH, STRETCH), 1)
    for low in range(0, length, STRETCH):
        here = slice(low, low + STRETCH)
        scores = lax.dot_general(
            queries[here], key_rows[here], (((1,), (1,)), ((), ())), preferred_element_type=f32
        ) * (1.0 / head**0.5)
        scores = jnp.where(row >= col, scores, -1e30)
        weights = jnp.exp(scores - jnp.max(scores, axis=1, keepdims=True))
        probabilities = (weights / jnp.sum(weights, axis=1, keepdims=True)).astype(bf16)
        result_ref[:] = mm(probabilities, value_ref[:]).astype(bf16)
    copies.start(result_ref, result_hbm).wait()


def body(
    tokens, norm_gain, norm_bias, ema_decay, ema_phase, ema_in, ema_out, ema_skip, rms_gain, z_weight, v_weight, qk_affine
):
    length, channels = tokens.shape
    tiles = channels // LANES
    chunks = length // CHUNK
    width = -(-(channels // GROUP) // LANES) * LANES
    place, peers = lax.axis_index("ctx"), lax.axis_size("ctx")
    half, tp = lax.axis_index("tp"), lax.axis_size("tp")
    depth, columns = v_weight.shape
    head = z_weight.shape[1]
    blocks = channels // depth
    members = 4 if peers % 4 == 0 and blocks % 4 == 0 else 1
    layers = peers // members
    subs = blocks // members
    shape, vmem = jax.ShapeDtypeStruct, pltpu.VMEM

    running, totals = call(
        sums_kernel,
        [shape((2, length, width), f32), shape((peers, 2, width), f32)],
        [tokens],
        plain=1,
        grant=16 * MIB,
    )
    sums = lax.all_to_all(totals, "ctx", 0, 0)
    line_z = [z_weight] + [
        lax.ppermute(z_weight, "ctx", [(i, (i + members * k) % peers) for i in range(peers)])
        for k in range(1, layers)
    ]
    line_z = jnp.stack(line_z)
    sums, v_weight = lax.optimization_barrier((sums, v_weight))
    all_v = [v_weight] + [ring_on(v_weight, members, layers, (-1) ** (k + 1)) for k in range(1, min(layers, 3))]
    all_z = [line_z] + [swap(line_z, k, members) for k in range(1, members)]

    rows = NDIM * 2 * tiles
    *near, dense, fresh, ends, q, w = call(
        functools.partial(feed_kernel, members),
        [shape((subs, length, depth), bf16)] * members
        + [
            shape((length * tiles, LANES), f32),
            shape((NDIM, chunks, 2, tiles, LANES), f32),
            shape((NDIM, 2, tiles, LANES), f32),
            shape((rows, LANES), f32),
            shape((rows, LANES), f32),
        ],
        [tokens, sums, running, norm_gain[None], norm_bias[None], ema_decay, ema_phase, ema_in, ema_out],
        [
            vmem((length, channels), bf16),
            vmem((peers, 2, width), f32),
            vmem((2, length, width), f32),
            vmem((1, channels), f32),
            vmem((1, channels), f32),
            vmem((NDIM, channels), f32),
            vmem((NDIM, channels), f32),
            vmem((NDIM, channels), f32),
            vmem((2, NDIM, channels), f32),
            vmem((blocks, length, depth), bf16),
            vmem((length * tiles, LANES), f32),
            vmem((NDIM, chunks, 2, tiles, LANES), f32),
            vmem((NDIM, 2, tiles, LANES), f32),
            vmem((rows, LANES), f32),
            vmem((rows, LANES), f32),
            vmem((CHUNK + 1, NDIM, 2, tiles, LANES), f32),
        ],
        9 + 3 + blocks + NDIM + 1,
    )
    more = max(1, peers // NDIM)

    def split(a):
        a = a.reshape(NDIM, 2, more, tiles // more, LANES).transpose(0, 2, 1, 3, 4)
        return a.reshape(peers, NDIM * more // peers, 2, tiles // more, LANES)

    def join(a):
        a = a.reshape(NDIM, more, 2, tiles // more, LANES).transpose(0, 2, 1, 3, 4)
        return a.reshape(NDIM, 2, tiles, LANES)

    arrived = lax.all_to_all(split(ends), "ctx", 0, 0)
    near, all_z = lax.optimization_barrier((near, all_z))
    near = near[:1] + [swap(near[k], k, members) for k in range(1, members)]
    my_q = lax.dynamic_index_in_dim(split(q.reshape(NDIM, 2, tiles, LANES)), place, 0, False)
    near, all_v[1], my_q = lax.optimization_barrier((near, all_v[1], my_q))
    for k in range(3, layers):
        all_v.append(ring_on(all_v[k - 2], members, layers, (-1) ** (k + 1)))
    far = [along(block, "tp", k, tp) for k in range(1, tp) for block in near]
    arrived, far, my_q, all_v[2] = lax.optimization_barrier((arrived, far, my_q, all_v[2]))
    (starts,) = call(functools.partial(scan_kernel, length), [shape(arrived.shape, f32)], [arrived, my_q], plain=1, grant=16 * MIB)
    incoming = lax.all_to_all(starts, "ctx", 0, 0)

    own, *sent = call(
        functools.partial(part_kernel, members, tp, layers),
        [shape((length, columns), f32)] + [shape((length, columns), bf16)] * (members - 1),
        [*near, *far, *all_v],
        [
            vmem((layers, members * length, depth), bf16),
            vmem((layers, depth, columns), bf16),
            vmem((length, columns), f32),
            vmem((max(members - 1, 1), length, columns), bf16),
        ],
        layers + tp * members * subs + members,
    )
    returned = [swap(block, k, members) for k, block in enumerate(sent, 1)]
    incoming, own = lax.optimization_barrier((incoming, own))

    (mixed_rows,) = call(
        mix_kernel,
        [shape((length, channels), bf16)],
        [join(incoming), fresh, dense, q, w, ema_skip.reshape(tiles, LANES)],
        [
            vmem((NDIM, 2, tiles, LANES), f32),
            vmem((NDIM, chunks, 2, tiles, LANES), f32),
            vmem((length * tiles, LANES), f32),
            vmem((rows, LANES), f32),
            vmem((rows, LANES), f32),
            vmem((tiles, LANES), f32),
            vmem((length, channels), bf16),
            vmem((chunks, NDIM, 2, tiles, LANES), f32),
            vmem((CHUNK, NDIM, 2, tiles, LANES), f32),
            vmem((CHUNK, tiles, LANES), f32),
            vmem((length * tiles, LANES), f32),
        ],
        6 + max(1, tiles // 8),
    )
    mixed_rows, returned = lax.optimization_barrier((mixed_rows, returned))
    apart = others(mixed_rows, "tp")
    (result,) = call(
        functools.partial(attend_kernel, members, tp),
        [shape((length, columns), bf16)],
        [*all_z, mixed_rows, *apart, *returned, own, rms_gain[None], qk_affine],
        [
            vmem((members, layers, depth, head), bf16),
            vmem((tp, length, channels), bf16),
            vmem((max(members - 1, 1), length, columns), bf16),
            vmem((length, columns), f32),
            vmem((1, tp * channels), f32),
            vmem((4, head), f32),
            vmem((tp * blocks, length, depth), bf16),
            vmem((length, columns), bf16),
            vmem((length, columns), bf16),
        ],
        tp + 2 + 2 * members + 1,
    )
    return result


def solution(mesh):
    in_specs = (
        P("ctx", "tp"),
        P("tp"),
        P("tp"),
        P(None, "tp"),
        P(None, "tp"),
        P(None, "tp"),
        P(None, None, "tp"),
        P("tp"),
        P(),
        P("ctx", "tp"),
        P("ctx", "tp"),
        P(None, "tp"),
    )
    return jax.shard_map(body, mesh=mesh, in_specs=in_specs, out_specs=P("ctx", "tp"), check_vma=False)
```

```python
import functools

import jax
import jax.numpy as jnp
from jax import lax
from jax.experimental import pallas as pl
from jax.experimental.pallas import tpu as pltpu
from jax.sharding import PartitionSpec as P

NDIM = 16
GROUP = 64
STRETCH = 128
CHUNK = 16
LANES = 128
epsilon = 1e-05
f32 = jnp.float32
bf16 = jnp.bfloat16
MIB = 1024 * 1024
VMEM_LIMIT = 64 * MIB
CHEAP = pl.CostEstimate(flops=1, bytes_accessed=1, transcendentals=0)


def call(kernel, outs, inputs, scratch=(), copies=0, plain=0, grant=VMEM_LIMIT):
    hbm, vmem = pl.BlockSpec(memory_space=pltpu.HBM), pl.BlockSpec(memory_space=pltpu.VMEM)
    here = vmem if plain else hbm
    extra = [pltpu.SemaphoreType.DMA((copies,))] if copies else []
    return pl.pallas_call(
        kernel,
        out_shape=outs,
        in_specs=[here] * len(inputs),
        out_specs=[here] * len(outs),
        scratch_shapes=list(scratch) + extra,
        compiler_params=pltpu.CompilerParams(vmem_limit_bytes=grant),
        cost_estimate=CHEAP,
    )(*inputs)


class Copies:
    def __init__(self, sems):
        self.sems, self.used = sems, 0

    def start(self, source, target):
        copy = pltpu.make_async_copy(source, target, self.sems.at[self.used])
        self.used += 1
        copy.start()
        return copy


def pieces(value):
    first = value.astype(bf16)
    rest = value - first.astype(f32)
    second = rest.astype(bf16)
    third = (rest - second.astype(f32)).astype(bf16)
    return first, second, third


def mm(a, b):
    return jnp.dot(a, b, preferred_element_type=f32)


def membership(channels, width, transposed, first):
    shape = (width, channels) if transposed else (channels, width)
    channel = lax.broadcasted_iota(jnp.int32, shape, 1 if transposed else 0) + first
    group = lax.broadcasted_iota(jnp.int32, shape, 0 if transposed else 1)
    return jnp.where(channel // GROUP == group, 1.0, 0.0).astype(bf16)


def group_sums(x, first, width):
    member = membership(x.shape[1], width, False, first)
    square = x.astype(f32) * x.astype(f32)
    high = square.astype(bf16)
    low = (square - high.astype(f32)).astype(bf16)
    return mm(x, member), mm(high, member) + mm(low, member)


def sums_kernel(x_ref, running_ref, total_ref):
    length, channels = x_ref.shape
    width = running_ref.shape[2]
    rows = lax.broadcasted_iota(jnp.int32, (length, length), 0)
    cols = lax.broadcasted_iota(jnp.int32, (length, length), 1)
    lower = jnp.where(rows >= cols, 1.0, 0.0).astype(bf16)
    for at, value in enumerate(group_sums(x_ref[...], 0, width)):
        one, two, three = pieces(value)
        running = mm(lower, one) + mm(lower, two) + mm(lower, three)
        running_ref[at] = running
        for peer in range(total_ref.shape[0]):
            total_ref[peer, at : at + 1, :] = running[length - 1 : length, :]


def times(a, b):
    return a[0] * b[0] - a[1] * b[1], a[0] * b[1] + a[1] * b[0]


def row_pair(ref, j, tiles):
    start = pl.multiple_of(j * (2 * tiles), 2 * tiles)
    return ref[pl.ds(start, tiles), :], ref[pl.ds(start + tiles, tiles), :]


def powers_into(ref, first, factor, count):
    def one(j, _):
        q, now = factor(j), first(j)
        for k in range(count):
            ref[k, j, 0], ref[k, j, 1] = now
            if k + 1 < count:
                now = times(now, q)
        return _

    lax.fori_loop(0, NDIM, one, 0)


def partner(member, step):
    low, high = lax.rem(member, 2), lax.div(member, 2)
    return (1 - low if step & 1 else low) + 2 * (1 - high if step & 2 else high)


def feed_kernel(members, *refs):
    x_hbm, sums_hbm, running_hbm, gain_hbm, bias_hbm, decay_hbm, phase_hbm, in_hbm, out_hbm = refs[:9]
    near_hbm, (dense_hbm, fresh_hbm, end_hbm, q_hbm, w_hbm) = refs[9 : 9 + members], refs[9 + members : 14 + members]
    (
        x_ref, sums_ref, running_ref, gain_ref, bias_ref, decay_ref, phase_ref, in_ref, out_ref,
        normed_ref, dense_ref, fresh_ref, end_ref, q_ref, w_ref, power_ref, sems,
    ) = refs[14 + members :]
    copies = Copies(sems)
    loads = [
        copies.start(a, b)
        for a, b in (
            (decay_hbm, decay_ref), (phase_hbm, phase_ref), (running_hbm, running_ref), (sums_hbm, sums_ref), (x_hbm, x_ref),
            (gain_hbm, gain_ref), (bias_hbm, bias_ref), (in_hbm, in_ref), (out_hbm, out_ref),
        )
    ]
    length, channels = x_ref.shape
    width = running_ref.shape[2]
    tiles = channels // LANES
    chunks = length // CHUNK
    subs, _, depth = near_hbm[0].shape
    me = lax.axis_index("ctx")
    peers = sums_ref.shape[0]

    loads[0].wait()
    loads[1].wait()
    for tile in range(tiles):
        lanes = slice(tile * LANES, (tile + 1) * LANES)
        phase, decay = phase_ref[:, lanes], decay_ref[:, lanes]
        parts = (decay * jnp.cos(phase), decay * jnp.sin(phase))
        for part in range(2):
            q_ref[pl.ds(part * tiles + tile, NDIM, stride=2 * tiles), :] = parts[part]
    stores = [copies.start(q_ref, q_hbm)]
    one, zero = jnp.ones((tiles, LANES), f32), jnp.zeros((tiles, LANES), f32)
    powers_into(power_ref, lambda j: (one, zero), lambda j: row_pair(q_ref, j, tiles), CHUNK + 1)

    for load in loads[2:7]:
        load.wait()
    before = [jnp.zeros((1, width), f32) for _ in range(2)]
    for peer in range(peers):
        earlier = jnp.where(peer < me, 1.0, 0.0)
        for at in range(2):
            before[at] = before[at] + sums_ref[peer, at : at + 1, :] * earlier
    place = lax.broadcasted_iota(jnp.int32, (length, width), 0) + me * length + 1
    counts = place.astype(f32) * GROUP
    average = (before[0] + running_ref[0]) / counts
    spread = jnp.maximum((before[1] + running_ref[1]) / counts - average * average, 0.0)
    scale = lax.rsqrt(spread + epsilon)
    member = membership(channels, width, True, 0)
    average_pieces, scale_pieces = pieces(average), pieces(scale)
    for tile in range(tiles):
        lanes = slice(tile * LANES, (tile + 1) * LANES)
        mine = member[:, lanes]
        average_wide = sum(mm(p, mine) for p in average_pieces)
        scale_wide = sum(mm(p, mine) for p in scale_pieces)
        scaled = (x_ref[:, lanes].astype(f32) - average_wide) * scale_wide
        normed = (scaled * gain_ref[:, lanes] + bias_ref[:, lanes]).astype(bf16)
        part = min(depth, LANES)
        for low in range(0, LANES, part):
            at = tile * LANES + low
            normed_ref[at // depth, :, at % depth : at % depth + part] = normed[:, low : low + part]
        dense_ref[pl.ds(tile, length, stride=tiles), :] = normed.astype(f32)
    for away, ref in enumerate(near_hbm):
        to = partner(lax.rem(me, members), away)
        for sub in range(subs):
            stores.append(copies.start(normed_ref.at[sub * members + to], ref.at[sub]))
    stores.append(copies.start(dense_ref, dense_hbm))

    loads[7].wait()
    loads[8].wait()
    for tile in range(tiles):
        lanes = slice(tile * LANES, (tile + 1) * LANES)
        for part in range(2):
            w_ref[pl.ds(part * tiles + tile, NDIM, stride=2 * tiles), :] = in_ref[:, lanes] * out_ref[part, :, lanes]
    stores.append(copies.start(w_ref, w_hbm))
    step = min(8, tiles)
    first_sem = copies.used

    def send(j):
        return pltpu.make_async_copy(fresh_ref.at[j], fresh_hbm.at[j], sems.at[first_sem + j])

    def one(j, _):
        for low in range(0, tiles, step):
            rows = slice(low, low + step)
            re = [jnp.zeros((step, LANES), f32) for _ in range(chunks)]
            im = [jnp.zeros((step, LANES), f32) for _ in range(chunks)]
            for b in range(CHUNK):
                p_re = power_ref[CHUNK - 1 - b, j, 0, rows, :]
                p_im = power_ref[CHUNK - 1 - b, j, 1, rows, :]
                for a in range(chunks):
                    at = (a * CHUNK + b) * tiles + low
                    value = dense_ref[at : at + step, :]
                    re[a] = re[a] + p_re * value
                    im[a] = im[a] + p_im * value
            q = (power_ref[CHUNK, j, 0, rows, :], power_ref[CHUNK, j, 1, rows, :])
            state = (re[0], im[0])
            for a in range(chunks):
                fresh_ref[j, a, 0, rows, :] = re[a]
                fresh_ref[j, a, 1, rows, :] = im[a]
                if a:
                    moved = times(state, q)
                    state = (moved[0] + re[a], moved[1] + im[a])
            end_ref[j, 0, rows, :], end_ref[j, 1, rows, :] = state
        send(j).start()
        return _

    lax.fori_loop(0, NDIM, one, 0)
    ends = pltpu.make_async_copy(end_ref, end_hbm, sems.at[first_sem + NDIM])
    ends.start()
    for store in stores:
        store.wait()
    lax.fori_loop(0, NDIM, lambda j, c: (send(j).wait(), c)[1], 0)
    ends.wait()


def scan_kernel(length, ends_ref, q_ref, out_ref):
    peers = ends_ref.shape[0]
    result, base, left = None, (q_ref[:, 0], q_ref[:, 1]), length
    while left:
        if left & 1:
            result = base if result is None else times(result, base)
        left >>= 1
        if left:
            base = times(base, base)
    state = (jnp.zeros_like(base[0]), jnp.zeros_like(base[1]))
    for peer in range(peers):
        out_ref[peer, :, 0], out_ref[peer, :, 1] = state
        if peer + 1 < peers:
            moved = times(state, result)
            state = (moved[0] + ends_ref[peer, :, 0], moved[1] + ends_ref[peer, :, 1])


def mix_kernel(
    incoming_hbm, fresh_hbm, dense_hbm, q_hbm, w_hbm, skip_hbm, mixed_hbm,
    incoming_ref, fresh_ref, dense_ref, q_ref, w_ref, skip_ref, mixed_ref, start_ref, coef_ref, tap_ref, out_ref, sems,
):
    copies = Copies(sems)
    loads = [
        copies.start(a, b)
        for a, b in (
            (q_hbm, q_ref), (w_hbm, w_ref), (skip_hbm, skip_ref), (incoming_hbm, incoming_ref), (fresh_hbm, fresh_ref), (dense_hbm, dense_ref),
        )
    ]
    length, channels = mixed_ref.shape
    tiles = channels // LANES
    chunks = length // CHUNK
    step = min(8, tiles)
    for load in loads[:3]:
        load.wait()
    powers_into(
        coef_ref,
        lambda j: times(row_pair(w_ref, j, tiles), row_pair(q_ref, j, tiles)),
        lambda j: row_pair(q_ref, j, tiles),
        CHUNK,
    )
    tap = skip_ref[...]
    for j in range(NDIM):
        tap = tap + row_pair(w_ref, j, tiles)[0]
    tap_ref[0] = tap

    def one_tap(k, _):
        tap = coef_ref[k, 0, 0]
        for j in range(1, NDIM):
            tap = tap + coef_ref[k, j, 0]
        tap_ref[k + 1] = tap
        return _

    lax.fori_loop(0, CHUNK - 1, one_tap, 0)
    for load in loads[3:5]:
        load.wait()

    def one(j, _):
        q = row_pair(q_ref, j, tiles)
        left = CHUNK
        while left > 1:
            q = times(q, q)
            left //= 2
        state = (incoming_ref[j, 0], incoming_ref[j, 1])
        for a in range(chunks):
            start_ref[a, j, 0], start_ref[a, j, 1] = state
            if a + 1 < chunks:
                moved = times(state, q)
                state = (moved[0] + fresh_ref[j, a, 0], moved[1] + fresh_ref[j, a, 1])
        return _

    lax.fori_loop(0, NDIM, one, 0)

    loads[5].wait()
    for low in range(0, tiles, step):
        rows = slice(low, low + step)
        for b in range(0, CHUNK, 2):
            total = [[jnp.zeros((step, LANES), f32) for _ in range(chunks)] for _ in range(2)]

            def carry(j, total, b=b, rows=rows):
                total = [list(t) for t in total]
                coefs = [(coef_ref[b + i, j, 0, rows, :], coef_ref[b + i, j, 1, rows, :]) for i in range(2)]
                for a in range(chunks):
                    re, im = start_ref[a, j, 0, rows, :], start_ref[a, j, 1, rows, :]
                    for i in range(2):
                        total[i][a] = total[i][a] + coefs[i][0] * re - coefs[i][1] * im
                return total

            total = lax.fori_loop(0, NDIM, carry, total, unroll=4)
            for s in range(b + 2):
                for i in range(2):
                    if s > b + i:
                        continue
                    tap = tap_ref[b + i - s, rows, :]
                    for a in range(chunks):
                        at = (a * CHUNK + s) * tiles + low
                        total[i][a] = total[i][a] + tap * dense_ref[at : at + step, :]
            for i in range(2):
                for a in range(chunks):
                    at = (a * CHUNK + b + i) * tiles + low
                    out_ref[at : at + step, :] = total[i][a]
        for tile in range(low, low + step):
            lanes = slice(tile * LANES, (tile + 1) * LANES)
            value = out_ref[pl.ds(tile, length, stride=tiles), :]
            mixed_ref[:, lanes] = (value / (1.0 + jnp.exp(-value))).astype(bf16)
        lanes = slice(low * LANES, (low + step) * LANES)
        loads.append(copies.start(mixed_ref.at[:, lanes], mixed_hbm.at[:, lanes]))
    for store in loads[6:]:
        store.wait()


def along(block, axis, step, group):
    count = lax.axis_size(axis)
    pairs = [(i, i - i % group + (i + step) % group) for i in range(count)]
    return lax.ppermute(block, axis, pairs)


def swap(block, step, group):
    return lax.ppermute(block, "ctx", [(i, i - i % group + (i % group ^ step)) for i in range(lax.axis_size("ctx"))])


def ring_of(layers):
    return [0, *range(1, layers, 2), *reversed(range(2, layers, 2))]


def ring_on(block, members, layers, step):
    ring = ring_of(layers)
    pairs = [
        (ring[k] * members + r, ring[(k + step) % layers] * members + r) for k in range(layers) for r in range(members)
    ]
    return lax.ppermute(block, "ctx", pairs)


def ring_steps(layers):
    return [0, *[(-1) ** (k + 1) * -((k + 1) // 2) for k in range(1, layers)]]


def others(block, axis):
    count = lax.axis_size(axis)
    return [along(block, axis, k, count) for k in range(1, count)]


def part_kernel(members, tp, layers, *refs):
    blocks_hbm, refs = refs[: members * tp], refs[members * tp :]
    weights_hbm, refs = refs[:layers], refs[layers:]
    own_hbm, sent_hbm, refs = refs[0], refs[1:members], refs[members:]
    row_ref, weight_ref, own_ref, sent_ref, sems = refs
    copies = Copies(sems)
    subs, length, depth = blocks_hbm[0].shape
    half, place = lax.axis_index("tp"), lax.axis_index("ctx")
    ring_at = sum(jnp.where(place // members == at, k, 0) for k, at in enumerate(ring_of(layers)))
    loads = []
    for away in range(tp):
        other = lax.rem(half + tp - away, tp)
        for k in range(members):
            for sub in range(subs):
                to = row_ref.at[other * subs + sub, k * length : (k + 1) * length, :]
                loads.append(copies.start(blocks_hbm[away * members + k].at[sub], to))
    later = [copies.start(weight, weight_ref.at[at]) for at, weight in enumerate(weights_hbm)]
    ring = ring_of(layers)
    blocks = []
    for step in ring_steps(layers):
        at = lax.rem(ring_at + layers + step, layers)
        block = jnp.int32(0)
        for place, layer in enumerate(ring):
            block = jnp.where(at == place, layer, block)
        blocks.append(block)
    for load in loads:
        load.wait()
    stores = []
    for k in range(members):
        here = slice(k * length, (k + 1) * length)
        total = None
        for back in range(layers):
            if k == 0:
                later[back].wait()
            product = mm(row_ref[blocks[back], here, :], weight_ref[back])
            total = product if total is None else total + product
        if k == 0:
            own_ref[...] = total
            stores.append(copies.start(own_ref, own_hbm))
        else:
            sent_ref[k - 1] = total.astype(bf16)
            stores.append(copies.start(sent_ref.at[k - 1], sent_hbm[k - 1]))
    for store in stores:
        store.wait()


def values_kernel(*refs):
    *parts_hbm, own_hbm, result_hbm, part_ref, own_ref, value_ref, sems = refs
    copies = Copies(sems)
    loads = [copies.start(own_hbm, own_ref)] + [copies.start(a, part_ref.at[k]) for k, a in enumerate(parts_hbm)]
    for load in loads:
        load.wait()
    total = own_ref[...]
    for k in range(len(parts_hbm)):
        total = total + part_ref[k].astype(f32)
    value_ref[...] = (total / (1.0 + jnp.exp(-total))).astype(bf16)
    copies.start(value_ref, result_hbm).wait()


def attend_kernel(members, tp, *refs):
    weights_hbm, refs = refs[:members], refs[members:]
    mixed_hbm, refs = refs[:tp], refs[tp:]
    values_hbm, gain_hbm, affine_hbm, result_hbm = refs[:4]
    weight_ref, mixed_ref, gain_ref, affine_ref, value_ref, result_ref, sems = refs[4:]
    copies = Copies(sems)
    loads = [copies.start(a, mixed_ref.at[k]) for k, a in enumerate(mixed_hbm)]
    loads += [copies.start(gain_hbm, gain_ref), copies.start(affine_hbm, affine_ref)]
    first = len(loads)
    place, half = lax.axis_index("ctx"), lax.axis_index("tp")
    member, layer = lax.rem(place, members), lax.div(place, members)
    layers, depth, head = weights_hbm[0].shape
    for m in range(members):
        for k in range(layers):
            block = lax.rem(layer + layers - k, layers) * members + partner(member, m)
            rows = pl.ds(pl.multiple_of(block * depth, depth), depth)
            loads.append(copies.start(weights_hbm[m].at[k], weight_ref.at[rows, :]))
    second = len(loads)
    loads.append(copies.start(values_hbm, value_ref))
    _, length, channels = mixed_ref.shape

    for load in loads[:first]:
        load.wait()
    square = jnp.zeros((length, 1), f32)
    for k in range(tp):
        value = mixed_ref[k].astype(f32)
        square = square + jnp.sum(value * value, axis=1, keepdims=True)
    scale = lax.rsqrt(square / (channels * tp) + 1e-06)
    normed = []
    for k in range(tp):
        at = lax.rem(half + tp - k, tp)
        gain = gain_ref[:, pl.ds(pl.multiple_of(at * channels, channels), channels)]
        normed.append((mixed_ref[k].astype(f32) * scale * gain).astype(bf16))
    for load in loads[first:second]:
        load.wait()
    z_total = jnp.zeros((length, head), f32)
    for k in range(tp):
        at = lax.rem(half + tp - k, tp)
        z_total = z_total + mm(normed[k], weight_ref[pl.ds(pl.multiple_of(at * channels, channels), channels), :])
    queries = (z_total * affine_ref[0:1, :] + affine_ref[1:2, :]).astype(bf16)
    key_rows = (z_total * affine_ref[2:3, :] + affine_ref[3:4, :]).astype(bf16)

    for load in loads[second:]:
        load.wait()
    row = lax.broadcasted_iota(jnp.int32, (STRETCH, STRETCH), 0)
    col = lax.broadcasted_iota(jnp.int32, (STRETCH, STRETCH), 1)
    for low in range(0, length, STRETCH):
        here = slice(low, low + STRETCH)
        scores = lax.dot_general(
            queries[here], key_rows[here], (((1,), (1,)), ((), ())), preferred_element_type=f32
        ) * (1.0 / head**0.5)
        scores = jnp.where(row >= col, scores, -1e30)
        weights = jnp.exp(scores - jnp.max(scores, axis=1, keepdims=True))
        probabilities = (weights / jnp.sum(weights, axis=1, keepdims=True)).astype(bf16)
        result_ref[here, :] = mm(probabilities, value_ref[here, :]).astype(bf16)
    copies.start(result_ref, result_hbm).wait()


def body(
    tokens, norm_gain, norm_bias, ema_decay, ema_phase, ema_in, ema_out, ema_skip, rms_gain, z_weight, v_weight, qk_affine
):
    length, channels = tokens.shape
    tiles = channels // LANES
    chunks = length // CHUNK
    width = -(-(channels // GROUP) // LANES) * LANES
    place, peers = lax.axis_index("ctx"), lax.axis_size("ctx")
    half, tp = lax.axis_index("tp"), lax.axis_size("tp")
    depth, columns = v_weight.shape
    head = z_weight.shape[1]
    blocks = channels // depth
    members = 4 if peers % 4 == 0 and blocks % 4 == 0 else 1
    layers = peers // members
    subs = blocks // members
    shape, vmem = jax.ShapeDtypeStruct, pltpu.VMEM

    running, totals = call(
        sums_kernel,
        [shape((2, length, width), f32), shape((peers, 2, width), f32)],
        [tokens],
        plain=1,
        grant=16 * MIB,
    )
    sums = lax.all_to_all(totals, "ctx", 0, 0)
    line_z = [z_weight] + [
        lax.ppermute(z_weight, "ctx", [(i, (i + members * k) % peers) for i in range(peers)])
        for k in range(1, layers)
    ]
    line_z = jnp.stack(line_z)
    sums, v_weight = lax.optimization_barrier((sums, v_weight))
    all_v = [v_weight] + [ring_on(v_weight, members, layers, (-1) ** (k + 1)) for k in range(1, min(layers, 3))]
    all_z = [line_z] + [swap(line_z, k, members) for k in range(1, members)]

    rows = NDIM * 2 * tiles
    *near, dense, fresh, ends, q, w = call(
        functools.partial(feed_kernel, members),
        [shape((subs, length, depth), bf16)] * members
        + [
            shape((length * tiles, LANES), f32),
            shape((NDIM, chunks, 2, tiles, LANES), f32),
            shape((NDIM, 2, tiles, LANES), f32),
            shape((rows, LANES), f32),
            shape((rows, LANES), f32),
        ],
        [tokens, sums, running, norm_gain[None], norm_bias[None], ema_decay, ema_phase, ema_in, ema_out],
        [
            vmem((length, channels), bf16),
            vmem((peers, 2, width), f32),
            vmem((2, length, width), f32),
            vmem((1, channels), f32),
            vmem((1, channels), f32),
            vmem((NDIM, channels), f32),
            vmem((NDIM, channels), f32),
            vmem((NDIM, channels), f32),
            vmem((2, NDIM, channels), f32),
            vmem((blocks, length, depth), bf16),
            vmem((length * tiles, LANES), f32),
            vmem((NDIM, chunks, 2, tiles, LANES), f32),
            vmem((NDIM, 2, tiles, LANES), f32),
            vmem((rows, LANES), f32),
            vmem((rows, LANES), f32),
            vmem((CHUNK + 1, NDIM, 2, tiles, LANES), f32),
        ],
        9 + 3 + blocks + NDIM + 1,
    )
    more = max(1, peers // NDIM)

    def split(a):
        a = a.reshape(NDIM, 2, more, tiles // more, LANES).transpose(0, 2, 1, 3, 4)
        return a.reshape(peers, NDIM * more // peers, 2, tiles // more, LANES)

    def join(a):
        a = a.reshape(NDIM, more, 2, tiles // more, LANES).transpose(0, 2, 1, 3, 4)
        return a.reshape(NDIM, 2, tiles, LANES)

    arrived = lax.all_to_all(split(ends), "ctx", 0, 0)
    near, all_z = lax.optimization_barrier((near, all_z))
    near = near[:1] + [swap(near[k], k, members) for k in range(1, members)]
    my_q = lax.dynamic_index_in_dim(split(q.reshape(NDIM, 2, tiles, LANES)), place, 0, False)
    near, all_v[1], my_q = lax.optimization_barrier((near, all_v[1], my_q))
    for k in range(3, layers):
        all_v.append(ring_on(all_v[k - 2], members, layers, (-1) ** (k + 1)))
    far = [along(block, "tp", k, tp) for k in range(1, tp) for block in near]
    arrived, far, my_q, all_v[2] = lax.optimization_barrier((arrived, far, my_q, all_v[2]))
    (starts,) = call(functools.partial(scan_kernel, length), [shape(arrived.shape, f32)], [arrived, my_q], plain=1, grant=16 * MIB)
    incoming = lax.all_to_all(starts, "ctx", 0, 0)

    own, *sent = call(
        functools.partial(part_kernel, members, tp, layers),
        [shape((length, columns), f32)] + [shape((length, columns), bf16)] * (members - 1),
        [*near, *far, *all_v],
        [
            vmem((layers, members * length, depth), bf16),
            vmem((layers, depth, columns), bf16),
            vmem((length, columns), f32),
            vmem((max(members - 1, 1), length, columns), bf16),
        ],
        layers + tp * members * subs + members,
    )
    returned = [swap(block, k, members) for k, block in enumerate(sent, 1)]
    incoming, own = lax.optimization_barrier((incoming, own))

    (mixed_rows,) = call(
        mix_kernel,
        [shape((length, channels), bf16)],
        [join(incoming), fresh, dense, q, w, ema_skip.reshape(tiles, LANES)],
        [
            vmem((NDIM, 2, tiles, LANES), f32),
            vmem((NDIM, chunks, 2, tiles, LANES), f32),
            vmem((length * tiles, LANES), f32),
            vmem((rows, LANES), f32),
            vmem((rows, LANES), f32),
            vmem((tiles, LANES), f32),
            vmem((length, channels), bf16),
            vmem((chunks, NDIM, 2, tiles, LANES), f32),
            vmem((CHUNK, NDIM, 2, tiles, LANES), f32),
            vmem((CHUNK, tiles, LANES), f32),
            vmem((length * tiles, LANES), f32),
        ],
        6 + max(1, tiles // 8),
    )
    mixed_rows, returned = lax.optimization_barrier((mixed_rows, returned))
    apart = others(mixed_rows, "tp")
    (values,) = call(
        values_kernel,
        [shape((length, columns), bf16)],
        [*returned, own],
        [
            vmem((max(members - 1, 1), length, columns), bf16),
            vmem((length, columns), f32),
            vmem((length, columns), bf16),
        ],
        members + 1,
    )
    (result,) = call(
        functools.partial(attend_kernel, members, tp),
        [shape((length, columns), bf16)],
        [*all_z, mixed_rows, *apart, values, rms_gain[None], qk_affine],
        [
            vmem((tp * channels, head), bf16),
            vmem((tp, length, channels), bf16),
            vmem((1, tp * channels), f32),
            vmem((4, head), f32),
            vmem((length, columns), bf16),
            vmem((length, columns), bf16),
        ],
        tp + 2 + peers + 2,
    )
    return result


def solution(mesh):
    in_specs = (
        P("ctx", "tp"),
        P("tp"),
        P("tp"),
        P(None, "tp"),
        P(None, "tp"),
        P(None, "tp"),
        P(None, None, "tp"),
        P("tp"),
        P(),
        P("ctx", "tp"),
        P("ctx", "tp"),
        P(None, "tp"),
    )
    return jax.shard_map(body, mesh=mesh, in_specs=in_specs, out_specs=P("ctx", "tp"), check_vma=False)
```

```python
import functools

import jax
import jax.numpy as jnp
from jax import lax
from jax.experimental import pallas as pl
from jax.experimental.pallas import tpu as pltpu
from jax.sharding import PartitionSpec as P

NDIM = 16
GROUP = 64
STRETCH = 128
CHUNK = 16
LANES = 128
epsilon = 1e-05
f32 = jnp.float32
bf16 = jnp.bfloat16
MIB = 1024 * 1024
VMEM_LIMIT = 64 * MIB
CHEAP = pl.CostEstimate(flops=1, bytes_accessed=1, transcendentals=0)


def call(kernel, outs, inputs, scratch=(), copies=0, plain=0, grant=VMEM_LIMIT):
    hbm, vmem = pl.BlockSpec(memory_space=pltpu.HBM), pl.BlockSpec(memory_space=pltpu.VMEM)
    here = vmem if plain else hbm
    extra = [pltpu.SemaphoreType.DMA((copies,))] if copies else []
    return pl.pallas_call(
        kernel,
        out_shape=outs,
        in_specs=[here] * len(inputs),
        out_specs=[here] * len(outs),
        scratch_shapes=list(scratch) + extra,
        compiler_params=pltpu.CompilerParams(vmem_limit_bytes=grant),
        cost_estimate=CHEAP,
    )(*inputs)


class Copies:
    def __init__(self, sems):
        self.sems, self.used = sems, 0

    def start(self, source, target):
        copy = pltpu.make_async_copy(source, target, self.sems.at[self.used])
        self.used += 1
        copy.start()
        return copy


def pieces(value):
    first = value.astype(bf16)
    rest = value - first.astype(f32)
    second = rest.astype(bf16)
    third = (rest - second.astype(f32)).astype(bf16)
    return first, second, third


def mm(a, b):
    return jnp.dot(a, b, preferred_element_type=f32)


def membership(channels, width, transposed, first):
    shape = (width, channels) if transposed else (channels, width)
    channel = lax.broadcasted_iota(jnp.int32, shape, 1 if transposed else 0) + first
    group = lax.broadcasted_iota(jnp.int32, shape, 0 if transposed else 1)
    return jnp.where(channel // GROUP == group, 1.0, 0.0).astype(bf16)


def group_sums(x, first, width):
    member = membership(x.shape[1], width, False, first)
    square = x.astype(f32) * x.astype(f32)
    high = square.astype(bf16)
    low = (square - high.astype(f32)).astype(bf16)
    return mm(x, member), mm(high, member) + mm(low, member)


def sums_kernel(x_ref, running_ref, total_ref):
    length, channels = x_ref.shape
    width = running_ref.shape[2]
    rows = lax.broadcasted_iota(jnp.int32, (length, length), 0)
    cols = lax.broadcasted_iota(jnp.int32, (length, length), 1)
    lower = jnp.where(rows >= cols, 1.0, 0.0).astype(bf16)
    for at, value in enumerate(group_sums(x_ref[...], 0, width)):
        one, two, three = pieces(value)
        running = mm(lower, one) + mm(lower, two) + mm(lower, three)
        running_ref[at] = running
        for peer in range(total_ref.shape[0]):
            total_ref[peer, at : at + 1, :] = running[length - 1 : length, :]


def times(a, b):
    return a[0] * b[0] - a[1] * b[1], a[0] * b[1] + a[1] * b[0]


def row_pair(ref, j, tiles):
    start = pl.multiple_of(j * (2 * tiles), 2 * tiles)
    return ref[pl.ds(start, tiles), :], ref[pl.ds(start + tiles, tiles), :]


def powers_into(ref, first, factor, count):
    def one(j, _):
        q, now = factor(j), first(j)
        for k in range(count):
            ref[k, j, 0], ref[k, j, 1] = now
            if k + 1 < count:
                now = times(now, q)
        return _

    lax.fori_loop(0, NDIM, one, 0)


def differ(number, step, count):
    bits = range(count.bit_length() - 1)
    digits = [lax.rem(lax.div(number, 1 << bit), 2) for bit in bits]
    return sum((1 - digit if step >> bit & 1 else digit) * (1 << bit) for bit, digit in zip(bits, digits))


def partner(member, step):
    low, high = lax.rem(member, 2), lax.div(member, 2)
    return (1 - low if step & 1 else low) + 2 * (1 - high if step & 2 else high)


def feed_kernel(members, *refs):
    x_hbm, sums_hbm, running_hbm, gain_hbm, bias_hbm, decay_hbm, phase_hbm, in_hbm, out_hbm = refs[:9]
    near_hbm, (dense_hbm, fresh_hbm, end_hbm, q_hbm, w_hbm) = refs[9 : 9 + members], refs[9 + members : 14 + members]
    (
        x_ref, sums_ref, running_ref, gain_ref, bias_ref, decay_ref, phase_ref, in_ref, out_ref,
        normed_ref, dense_ref, fresh_ref, end_ref, q_ref, w_ref, power_ref, sems,
    ) = refs[14 + members :]
    copies = Copies(sems)
    loads = [
        copies.start(a, b)
        for a, b in (
            (decay_hbm, decay_ref), (phase_hbm, phase_ref), (running_hbm, running_ref), (sums_hbm, sums_ref), (x_hbm, x_ref),
            (gain_hbm, gain_ref), (bias_hbm, bias_ref), (in_hbm, in_ref), (out_hbm, out_ref),
        )
    ]
    length, channels = x_ref.shape
    width = running_ref.shape[2]
    tiles = channels // LANES
    chunks = length // CHUNK
    subs, _, depth = near_hbm[0].shape
    me = lax.axis_index("ctx")
    peers = sums_ref.shape[0]

    loads[0].wait()
    loads[1].wait()
    for tile in range(tiles):
        lanes = slice(tile * LANES, (tile + 1) * LANES)
        phase, decay = phase_ref[:, lanes], decay_ref[:, lanes]
        parts = (decay * jnp.cos(phase), decay * jnp.sin(phase))
        for part in range(2):
            q_ref[pl.ds(part * tiles + tile, NDIM, stride=2 * tiles), :] = parts[part]
    stores = [copies.start(q_ref, q_hbm)]
    one, zero = jnp.ones((tiles, LANES), f32), jnp.zeros((tiles, LANES), f32)
    powers_into(power_ref, lambda j: (one, zero), lambda j: row_pair(q_ref, j, tiles), CHUNK + 1)

    for load in loads[2:7]:
        load.wait()
    before = [jnp.zeros((1, width), f32) for _ in range(2)]
    for peer in range(peers):
        earlier = jnp.where(peer < me, 1.0, 0.0)
        for at in range(2):
            before[at] = before[at] + sums_ref[peer, at : at + 1, :] * earlier
    place = lax.broadcasted_iota(jnp.int32, (length, width), 0) + me * length + 1
    counts = place.astype(f32) * GROUP
    average = (before[0] + running_ref[0]) / counts
    spread = jnp.maximum((before[1] + running_ref[1]) / counts - average * average, 0.0)
    scale = lax.rsqrt(spread + epsilon)
    member = membership(channels, width, True, 0)
    average_pieces, scale_pieces = pieces(average), pieces(scale)
    for tile in range(tiles):
        lanes = slice(tile * LANES, (tile + 1) * LANES)
        mine = member[:, lanes]
        average_wide = sum(mm(p, mine) for p in average_pieces)
        scale_wide = sum(mm(p, mine) for p in scale_pieces)
        scaled = (x_ref[:, lanes].astype(f32) - average_wide) * scale_wide
        normed = (scaled * gain_ref[:, lanes] + bias_ref[:, lanes]).astype(bf16)
        part = min(depth, LANES)
        for low in range(0, LANES, part):
            at = tile * LANES + low
            normed_ref[at // depth, :, at % depth : at % depth + part] = normed[:, low : low + part]
        dense_ref[pl.ds(tile, length, stride=tiles), :] = normed.astype(f32)
    for away, ref in enumerate(near_hbm):
        to = partner(lax.rem(me, members), away)
        for sub in range(subs):
            stores.append(copies.start(normed_ref.at[sub * members + to], ref.at[sub]))
    stores.append(copies.start(dense_ref, dense_hbm))

    loads[7].wait()
    loads[8].wait()
    for tile in range(tiles):
        lanes = slice(tile * LANES, (tile + 1) * LANES)
        for part in range(2):
            w_ref[pl.ds(part * tiles + tile, NDIM, stride=2 * tiles), :] = in_ref[:, lanes] * out_ref[part, :, lanes]
    stores.append(copies.start(w_ref, w_hbm))
    step = min(8, tiles)
    first_sem = copies.used

    def send(j):
        return pltpu.make_async_copy(fresh_ref.at[j], fresh_hbm.at[j], sems.at[first_sem + j])

    def one(j, _):
        for low in range(0, tiles, step):
            rows = slice(low, low + step)
            re = [jnp.zeros((step, LANES), f32) for _ in range(chunks)]
            im = [jnp.zeros((step, LANES), f32) for _ in range(chunks)]
            for b in range(CHUNK):
                p_re = power_ref[CHUNK - 1 - b, j, 0, rows, :]
                p_im = power_ref[CHUNK - 1 - b, j, 1, rows, :]
                for a in range(chunks):
                    at = (a * CHUNK + b) * tiles + low
                    value = dense_ref[at : at + step, :]
                    re[a] = re[a] + p_re * value
                    im[a] = im[a] + p_im * value
            q = (power_ref[CHUNK, j, 0, rows, :], power_ref[CHUNK, j, 1, rows, :])
            state = (re[0], im[0])
            for a in range(chunks):
                fresh_ref[j, a, 0, rows, :] = re[a]
                fresh_ref[j, a, 1, rows, :] = im[a]
                if a:
                    moved = times(state, q)
                    state = (moved[0] + re[a], moved[1] + im[a])
            end_ref[j, 0, rows, :], end_ref[j, 1, rows, :] = state
        send(j).start()
        return _

    lax.fori_loop(0, NDIM, one, 0)
    ends = pltpu.make_async_copy(end_ref, end_hbm, sems.at[first_sem + NDIM])
    ends.start()
    for store in stores:
        store.wait()
    lax.fori_loop(0, NDIM, lambda j, c: (send(j).wait(), c)[1], 0)
    ends.wait()


def scan_kernel(length, ends_ref, q_ref, out_ref):
    peers = ends_ref.shape[0]
    result, base, left = None, (q_ref[:, 0], q_ref[:, 1]), length
    while left:
        if left & 1:
            result = base if result is None else times(result, base)
        left >>= 1
        if left:
            base = times(base, base)
    state = (jnp.zeros_like(base[0]), jnp.zeros_like(base[1]))
    for peer in range(peers):
        out_ref[peer, :, 0], out_ref[peer, :, 1] = state
        if peer + 1 < peers:
            moved = times(state, result)
            state = (moved[0] + ends_ref[peer, :, 0], moved[1] + ends_ref[peer, :, 1])


def mix_kernel(
    incoming_hbm, fresh_hbm, dense_hbm, q_hbm, w_hbm, skip_hbm, mixed_hbm,
    incoming_ref, fresh_ref, dense_ref, q_ref, w_ref, skip_ref, mixed_ref, start_ref, coef_ref, tap_ref, out_ref, sems,
):
    copies = Copies(sems)
    loads = [
        copies.start(a, b)
        for a, b in (
            (q_hbm, q_ref), (w_hbm, w_ref), (skip_hbm, skip_ref), (incoming_hbm, incoming_ref), (fresh_hbm, fresh_ref), (dense_hbm, dense_ref),
        )
    ]
    length, channels = mixed_ref.shape
    tiles = channels // LANES
    chunks = length // CHUNK
    step = min(8, tiles)
    for load in loads[:3]:
        load.wait()
    powers_into(
        coef_ref,
        lambda j: times(row_pair(w_ref, j, tiles), row_pair(q_ref, j, tiles)),
        lambda j: row_pair(q_ref, j, tiles),
        CHUNK,
    )
    tap = skip_ref[...]
    for j in range(NDIM):
        tap = tap + row_pair(w_ref, j, tiles)[0]
    tap_ref[0] = tap

    def one_tap(k, _):
        tap = coef_ref[k, 0, 0]
        for j in range(1, NDIM):
            tap = tap + coef_ref[k, j, 0]
        tap_ref[k + 1] = tap
        return _

    lax.fori_loop(0, CHUNK - 1, one_tap, 0)
    for load in loads[3:5]:
        load.wait()

    def one(j, _):
        q = row_pair(q_ref, j, tiles)
        left = CHUNK
        while left > 1:
            q = times(q, q)
            left //= 2
        state = (incoming_ref[j, 0], incoming_ref[j, 1])
        for a in range(chunks):
            start_ref[a, j, 0], start_ref[a, j, 1] = state
            if a + 1 < chunks:
                moved = times(state, q)
                state = (moved[0] + fresh_ref[j, a, 0], moved[1] + fresh_ref[j, a, 1])
        return _

    lax.fori_loop(0, NDIM, one, 0)

    loads[5].wait()
    for low in range(0, tiles, step):
        rows = slice(low, low + step)
        for b in range(0, CHUNK, 2):
            total = [[jnp.zeros((step, LANES), f32) for _ in range(chunks)] for _ in range(2)]

            def carry(j, total, b=b, rows=rows):
                total = [list(t) for t in total]
                coefs = [(coef_ref[b + i, j, 0, rows, :], coef_ref[b + i, j, 1, rows, :]) for i in range(2)]
                for a in range(chunks):
                    re, im = start_ref[a, j, 0, rows, :], start_ref[a, j, 1, rows, :]
                    for i in range(2):
                        total[i][a] = total[i][a] + coefs[i][0] * re - coefs[i][1] * im
                return total

            total = lax.fori_loop(0, NDIM, carry, total, unroll=4)
            for s in range(b + 2):
                for i in range(2):
                    if s > b + i:
                        continue
                    tap = tap_ref[b + i - s, rows, :]
                    for a in range(chunks):
                        at = (a * CHUNK + s) * tiles + low
                        total[i][a] = total[i][a] + tap * dense_ref[at : at + step, :]
            for i in range(2):
                for a in range(chunks):
                    at = (a * CHUNK + b + i) * tiles + low
                    out_ref[at : at + step, :] = total[i][a]
        for tile in range(low, low + step):
            lanes = slice(tile * LANES, (tile + 1) * LANES)
            value = out_ref[pl.ds(tile, length, stride=tiles), :]
            mixed_ref[:, lanes] = (value / (1.0 + jnp.exp(-value))).astype(bf16)
        lanes = slice(low * LANES, (low + step) * LANES)
        loads.append(copies.start(mixed_ref.at[:, lanes], mixed_hbm.at[:, lanes]))
    for store in loads[6:]:
        store.wait()


def along(block, axis, step, group):
    count = lax.axis_size(axis)
    pairs = [(i, i - i % group + (i + step) % group) for i in range(count)]
    return lax.ppermute(block, axis, pairs)


def line_target(layer, step, layers):
    return (layer + step) % layers if layers & (layers - 1) else layer ^ step


def swap(block, step, group):
    return lax.ppermute(block, "ctx", [(i, i - i % group + (i % group ^ step)) for i in range(lax.axis_size("ctx"))])


def ring_of(layers):
    return [0, *range(1, layers, 2), *reversed(range(2, layers, 2))]


def ring_on(block, members, layers, step):
    ring = ring_of(layers)
    pairs = [
        (ring[k] * members + r, ring[(k + step) % layers] * members + r) for k in range(layers) for r in range(members)
    ]
    return lax.ppermute(block, "ctx", pairs)


def ring_steps(layers):
    return [0, *[(-1) ** (k + 1) * -((k + 1) // 2) for k in range(1, layers)]]


def others(block, axis):
    count = lax.axis_size(axis)
    return [along(block, axis, k, count) for k in range(1, count)]


def part_kernel(members, tp, layers, *refs):
    blocks_hbm, refs = refs[: members * tp], refs[members * tp :]
    weights_hbm, refs = refs[:layers], refs[layers:]
    own_hbm, sent_hbm, refs = refs[0], refs[1:members], refs[members:]
    row_ref, weight_ref, own_ref, sent_ref, sems = refs
    copies = Copies(sems)
    subs, length, depth = blocks_hbm[0].shape
    half, place = lax.axis_index("tp"), lax.axis_index("ctx")
    ring_at = sum(jnp.where(place // members == at, k, 0) for k, at in enumerate(ring_of(layers)))
    loads = []
    for away in range(tp):
        other = lax.rem(half + tp - away, tp)
        for k in range(members):
            for sub in range(subs):
                to = row_ref.at[other * subs + sub, k * length : (k + 1) * length, :]
                loads.append(copies.start(blocks_hbm[away * members + k].at[sub], to))
    later = [copies.start(weight, weight_ref.at[at]) for at, weight in enumerate(weights_hbm)]
    ring = ring_of(layers)
    blocks = []
    for step in ring_steps(layers):
        at = lax.rem(ring_at + layers + step, layers)
        block = jnp.int32(0)
        for place, layer in enumerate(ring):
            block = jnp.where(at == place, layer, block)
        blocks.append(block)
    for load in loads:
        load.wait()
    stores = []
    for k in range(members):
        here = slice(k * length, (k + 1) * length)
        total = None
        for back in range(layers):
            if k == 0:
                later[back].wait()
            product = mm(row_ref[blocks[back], here, :], weight_ref[back])
            total = product if total is None else total + product
        if k == 0:
            own_ref[...] = total
            stores.append(copies.start(own_ref, own_hbm))
        else:
            sent_ref[k - 1] = total.astype(bf16)
            stores.append(copies.start(sent_ref.at[k - 1], sent_hbm[k - 1]))
    for store in stores:
        store.wait()


def values_kernel(*refs):
    *parts_hbm, own_hbm, result_hbm, part_ref, own_ref, value_ref, sems = refs
    copies = Copies(sems)
    loads = [copies.start(own_hbm, own_ref)] + [copies.start(a, part_ref.at[k]) for k, a in enumerate(parts_hbm)]
    for load in loads:
        load.wait()
    total = own_ref[...]
    for k in range(len(parts_hbm)):
        total = total + part_ref[k].astype(f32)
    value_ref[...] = (total / (1.0 + jnp.exp(-total))).astype(bf16)
    copies.start(value_ref, result_hbm).wait()


def attend_kernel(members, tp, *refs):
    weights_hbm, refs = refs[:members], refs[members:]
    mixed_hbm, refs = refs[:tp], refs[tp:]
    values_hbm, gain_hbm, affine_hbm, result_hbm = refs[:4]
    weight_ref, mixed_ref, gain_ref, affine_ref, value_ref, result_ref, sems = refs[4:]
    copies = Copies(sems)
    loads = [copies.start(a, mixed_ref.at[k]) for k, a in enumerate(mixed_hbm)]
    loads += [copies.start(gain_hbm, gain_ref), copies.start(affine_hbm, affine_ref)]
    first = len(loads)
    place, half = lax.axis_index("ctx"), lax.axis_index("tp")
    member, layer = lax.rem(place, members), lax.div(place, members)
    layers, depth, head = weights_hbm[0].shape
    for m in range(members):
        for k in range(layers):
            if layers & (layers - 1):
                source = lax.rem(layer + layers - k, layers)
            else:
                source = differ(layer, k, layers)
            block = source * members + partner(member, m)
            rows = pl.ds(pl.multiple_of(block * depth, depth), depth)
            loads.append(copies.start(weights_hbm[m].at[k], weight_ref.at[rows, :]))
    second = len(loads)
    loads.append(copies.start(values_hbm, value_ref))
    _, length, channels = mixed_ref.shape

    for load in loads[:first]:
        load.wait()
    square = jnp.zeros((length, 1), f32)
    for k in range(tp):
        value = mixed_ref[k].astype(f32)
        square = square + jnp.sum(value * value, axis=1, keepdims=True)
    scale = lax.rsqrt(square / (channels * tp) + 1e-06)
    normed = []
    for k in range(tp):
        at = lax.rem(half + tp - k, tp)
        gain = gain_ref[:, pl.ds(pl.multiple_of(at * channels, channels), channels)]
        normed.append((mixed_ref[k].astype(f32) * scale * gain).astype(bf16))
    for load in loads[first:second]:
        load.wait()
    z_total = jnp.zeros((length, head), f32)
    for k in range(tp):
        at = lax.rem(half + tp - k, tp)
        z_total = z_total + mm(normed[k], weight_ref[pl.ds(pl.multiple_of(at * channels, channels), channels), :])
    queries = (z_total * affine_ref[0:1, :] + affine_ref[1:2, :]).astype(bf16)
    key_rows = (z_total * affine_ref[2:3, :] + affine_ref[3:4, :]).astype(bf16)

    for load in loads[second:]:
        load.wait()
    row = lax.broadcasted_iota(jnp.int32, (STRETCH, STRETCH), 0)
    col = lax.broadcasted_iota(jnp.int32, (STRETCH, STRETCH), 1)
    for low in range(0, length, STRETCH):
        here = slice(low, low + STRETCH)
        scores = lax.dot_general(
            queries[here], key_rows[here], (((1,), (1,)), ((), ())), preferred_element_type=f32
        ) * (1.0 / head**0.5)
        scores = jnp.where(row >= col, scores, -1e30)
        weights = jnp.exp(scores - jnp.max(scores, axis=1, keepdims=True))
        probabilities = (weights / jnp.sum(weights, axis=1, keepdims=True)).astype(bf16)
        result_ref[here, :] = mm(probabilities, value_ref[here, :]).astype(bf16)
    copies.start(result_ref, result_hbm).wait()


def body(
    tokens, norm_gain, norm_bias, ema_decay, ema_phase, ema_in, ema_out, ema_skip, rms_gain, z_weight, v_weight, qk_affine
):
    length, channels = tokens.shape
    tiles = channels // LANES
    chunks = length // CHUNK
    width = -(-(channels // GROUP) // LANES) * LANES
    place, peers = lax.axis_index("ctx"), lax.axis_size("ctx")
    half, tp = lax.axis_index("tp"), lax.axis_size("tp")
    depth, columns = v_weight.shape
    head = z_weight.shape[1]
    blocks = channels // depth
    members = 4 if peers % 4 == 0 and blocks % 4 == 0 else 1
    layers = peers // members
    subs = blocks // members
    shape, vmem = jax.ShapeDtypeStruct, pltpu.VMEM

    running, totals = call(
        sums_kernel,
        [shape((2, length, width), f32), shape((peers, 2, width), f32)],
        [tokens],
        plain=1,
        grant=16 * MIB,
    )
    sums = lax.all_to_all(totals, "ctx", 0, 0)
    line_z = [z_weight] + [
        lax.ppermute(z_weight, "ctx", [(i, line_target(i // members, k, layers) * members + i % members) for i in range(peers)])
        for k in range(1, layers)
    ]
    line_z = jnp.stack(line_z)
    sums, v_weight = lax.optimization_barrier((sums, v_weight))
    all_v = [v_weight] + [ring_on(v_weight, members, layers, (-1) ** (k + 1)) for k in range(1, min(layers, 3))]
    all_z = [line_z] + [swap(line_z, k, members) for k in range(1, members)]

    rows = NDIM * 2 * tiles
    *near, dense, fresh, ends, q, w = call(
        functools.partial(feed_kernel, members),
        [shape((subs, length, depth), bf16)] * members
        + [
            shape((length * tiles, LANES), f32),
            shape((NDIM, chunks, 2, tiles, LANES), f32),
            shape((NDIM, 2, tiles, LANES), f32),
            shape((rows, LANES), f32),
            shape((rows, LANES), f32),
        ],
        [tokens, sums, running, norm_gain[None], norm_bias[None], ema_decay, ema_phase, ema_in, ema_out],
        [
            vmem((length, channels), bf16),
            vmem((peers, 2, width), f32),
            vmem((2, length, width), f32),
            vmem((1, channels), f32),
            vmem((1, channels), f32),
            vmem((NDIM, channels), f32),
            vmem((NDIM, channels), f32),
            vmem((NDIM, channels), f32),
            vmem((2, NDIM, channels), f32),
            vmem((blocks, length, depth), bf16),
            vmem((length * tiles, LANES), f32),
            vmem((NDIM, chunks, 2, tiles, LANES), f32),
            vmem((NDIM, 2, tiles, LANES), f32),
            vmem((rows, LANES), f32),
            vmem((rows, LANES), f32),
            vmem((CHUNK + 1, NDIM, 2, tiles, LANES), f32),
        ],
        9 + 3 + blocks + NDIM + 1,
    )
    more = max(1, peers // NDIM)

    def split(a):
        a = a.reshape(NDIM, 2, more, tiles // more, LANES).transpose(0, 2, 1, 3, 4)
        return a.reshape(peers, NDIM * more // peers, 2, tiles // more, LANES)

    def join(a):
        a = a.reshape(NDIM, more, 2, tiles // more, LANES).transpose(0, 2, 1, 3, 4)
        return a.reshape(NDIM, 2, tiles, LANES)

    arrived = lax.all_to_all(split(ends), "ctx", 0, 0)
    near, all_z = lax.optimization_barrier((near, all_z))
    near = near[:1] + [swap(near[k], k, members) for k in range(1, members)]
    my_q = lax.dynamic_index_in_dim(split(q.reshape(NDIM, 2, tiles, LANES)), place, 0, False)
    near, all_v[1], my_q = lax.optimization_barrier((near, all_v[1], my_q))
    for k in range(3, layers):
        all_v.append(ring_on(all_v[k - 2], members, layers, (-1) ** (k + 1)))
    far = [along(block, "tp", k, tp) for k in range(1, tp) for block in near]
    arrived, far, my_q, all_v[2] = lax.optimization_barrier((arrived, far, my_q, all_v[2]))
    (starts,) = call(functools.partial(scan_kernel, length), [shape(arrived.shape, f32)], [arrived, my_q], plain=1, grant=16 * MIB)
    incoming = lax.all_to_all(starts, "ctx", 0, 0)

    own, *sent = call(
        functools.partial(part_kernel, members, tp, layers),
        [shape((length, columns), f32)] + [shape((length, columns), bf16)] * (members - 1),
        [*near, *far, *all_v],
        [
            vmem((layers, members * length, depth), bf16),
            vmem((layers, depth, columns), bf16),
            vmem((length, columns), f32),
            vmem((max(members - 1, 1), length, columns), bf16),
        ],
        layers + tp * members * subs + members,
    )
    returned = [swap(block, k, members) for k, block in enumerate(sent, 1)]
    incoming, own = lax.optimization_barrier((incoming, own))

    (mixed_rows,) = call(
        mix_kernel,
        [shape((length, channels), bf16)],
        [join(incoming), fresh, dense, q, w, ema_skip.reshape(tiles, LANES)],
        [
            vmem((NDIM, 2, tiles, LANES), f32),
            vmem((NDIM, chunks, 2, tiles, LANES), f32),
            vmem((length * tiles, LANES), f32),
            vmem((rows, LANES), f32),
            vmem((rows, LANES), f32),
            vmem((tiles, LANES), f32),
            vmem((length, channels), bf16),
            vmem((chunks, NDIM, 2, tiles, LANES), f32),
            vmem((CHUNK, NDIM, 2, tiles, LANES), f32),
            vmem((CHUNK, tiles, LANES), f32),
            vmem((length * tiles, LANES), f32),
        ],
        6 + max(1, tiles // 8),
    )
    mixed_rows, returned = lax.optimization_barrier((mixed_rows, returned))
    apart = others(mixed_rows, "tp")
    (values,) = call(
        values_kernel,
        [shape((length, columns), bf16)],
        [*returned, own],
        [
            vmem((max(members - 1, 1), length, columns), bf16),
            vmem((length, columns), f32),
            vmem((length, columns), bf16),
        ],
        members + 1,
    )
    (result,) = call(
        functools.partial(attend_kernel, members, tp),
        [shape((length, columns), bf16)],
        [*all_z, mixed_rows, *apart, values, rms_gain[None], qk_affine],
        [
            vmem((tp * channels, head), bf16),
            vmem((tp, length, channels), bf16),
            vmem((1, tp * channels), f32),
            vmem((4, head), f32),
            vmem((length, columns), bf16),
            vmem((length, columns), bf16),
        ],
        tp + 2 + peers + 2,
    )
    return result


def solution(mesh):
    in_specs = (
        P("ctx", "tp"),
        P("tp"),
        P("tp"),
        P(None, "tp"),
        P(None, "tp"),
        P(None, "tp"),
        P(None, None, "tp"),
        P("tp"),
        P(),
        P("ctx", "tp"),
        P("ctx", "tp"),
        P(None, "tp"),
    )
    return jax.shard_map(body, mesh=mesh, in_specs=in_specs, out_specs=P("ctx", "tp"), check_vma=False)
```
